256 devices in a mesh: context: 32 (over z, x), tensor: 8 (over y, core).
Axes of the slice: x: 4, y: 4, z: 8, core: 2. Of those that a mesh axis runs over, the one named last changes fastest.
Arguments:
- tokens: bfloat16 [4096, 8192], P('context', 'tensor'), may hold values from -40 to 40
- norm_gain: float32 [8192], P('tensor'), may hold values from 0.1 to 1.9
- router: bfloat16 [8192], P('tensor'), may hold values from -0.0625 to 0.0625
- w_gate: bfloat16 [8192, 28672], P('tensor', 'context'), may hold values from -0.0625 to 0.0625
- w_up: bfloat16 [8192, 28672], P('tensor', 'context'), may hold values from -0.0625 to 0.0625
- w_down: bfloat16 [28672, 8192], P('context', 'tensor'), may hold values from -0.03125 to 0.03125
- routes: int32 [32, 24], P('context'), may hold values from 0 to 127, as said below
- counts: int32 [32], P('context'), may hold values from 1 to 24, 512 in all
- cotangent: bfloat16 [4096, 8192], P('context', 'tensor'), may hold values from -6 to 6
Outputs:
- mixed: bfloat16 [4096, 8192], P('context', 'tensor')
- grad_tokens: bfloat16 [4096, 8192], P('context', 'tensor')
- grad_gate: bfloat16 [8192, 28672], P('tensor', 'context')
- grad_up: bfloat16 [8192, 28672], P('tensor', 'context')
- grad_down: bfloat16 [28672, 8192], P('context', 'tensor')
- grad_gain: float32 [8192], P('tensor')
- grad_router: float32 [8192], P('tensor')
The draws below stay inside these ranges and needn't reach their ends.
Inputs may be any that keep to these rules, and one draw needn't show every extreme that they name: `routes`: within a row the 24 entries are distinct local positions; only the first counts entries of a row are used. The counts add up to 512; the largest is 24.
All inputs are finite; a program needn't handle non-finite values. No bound on the sum of `counts` on one device may be relied on, other than what follows from the above.
Results may differ from the reference program's by a relative error of at most 0.015.
Values may be sent and summed in bfloat16 or wider, within the bound.
A program may use at most 64 MiB of HBM per device.

```python
import math
import jax
import jax.numpy as jnp
import numpy as np
from jax import lax

D = 8192
FF = 28672
TOK_DEV = 128
CAP = 24
TOKENS = 4096
PICKED = 512
N_CONTEXT = 32


def draw_tokens(key, part):
    key = jax.random.fold_in(key, 11)
    entry_key, column_key, row_key = jax.random.split(key, 3)
    rising = 3.0 ** (jnp.arange(D, dtype=jnp.float32) / D)
    column = 0.12 * 10.0 ** jax.random.uniform(column_key, (D,), dtype=jnp.float32) * rising
    entries = jnp.clip(jax.random.normal(entry_key, (TOKENS, D), dtype=jnp.float32), -3.0, 3.0)
    row_scale = 10.0 ** jax.random.uniform(row_key, (TOKENS, 1), dtype=jnp.float32, minval=-0.3, maxval=0.3)
    return (entries * column * row_scale).astype(jnp.bfloat16)


def shard_order(shard_key):
    return jax.random.permutation(shard_key, TOK_DEV)


def draw_routes(key, part):
    key = jax.random.fold_in(key, 5)
    shard_keys = jax.random.split(key, N_CONTEXT)
    orders = jax.vmap(shard_order)(shard_keys)
    return orders[:, :CAP].astype(jnp.int32)


def levels(key, extent, cuts, least, high):
    level, own = 1.0, jax.random.fold_in(key, 6)
    for dim, blocks in cuts:
        steps = jnp.exp(jax.random.uniform(jax.random.fold_in(own, dim), (blocks,), jnp.float32, least / len(cuts), high / len(cuts)))
        level = level * jnp.repeat(steps, extent[dim] // blocks).reshape([-1 if axis == dim else 1 for axis in range(len(extent))])
    return level


def split_up(number_of, total, limit, skew):
    loads = [(1 << 20) // math.isqrt(rank ** skew) + 1 for rank in range(2, number_of + 1)]
    rest, given = total - limit - (number_of - 1), [1] * (number_of - 1)
    while rest > 0:
        movable = [i for i in range(number_of - 1) if given[i] < limit]
        whole, budget = sum([loads[i] for i in movable]), rest
        for i in movable:
            more = min(limit - given[i], max(1, budget * loads[i] // whole), rest)
            given[i] = given[i] + more
            rest = rest - more
    return np.array([limit] + given)


def uneven_parts(key, number_of, total, limit, skew):
    if number_of == 2:
        one = jax.random.randint(key, (), max(1, total - limit), min(limit, total - 1) + 1)
        return jnp.stack([one, total - one])
    lengths = jnp.asarray(split_up(number_of, total, limit, skew), jnp.int32)
    couples = (number_of - 1) // 2
    giver, taker = lengths[1:1 + 2 * couples:2], lengths[2:2 + 2 * couples:2]
    room = jnp.minimum(giver - 1, limit - taker)
    moved = jax.random.randint(jax.random.fold_in(key, 1), (couples,), 0, 1 << 20) % (room + 1)
    lengths = lengths.at[1:1 + 2 * couples:2].set(giver - moved).at[2:2 + 2 * couples:2].set(taker + moved)
    return lengths[jax.random.permutation(jax.random.fold_in(key, 2), number_of)]


def bell_draw(own_key, extent, scale, most, pieces=(), held_as=jnp.bfloat16):
    values = jax.random.normal(own_key, extent, jnp.float32) * scale
    if len(pieces) > 0:
        values = levels(own_key, extent, pieces, -0.22, 0.18) * values
    return jnp.clip(values, min=-most, max=most).astype(held_as)


def setup_inputs(seed: int = 0) -> dict:
    streams_of = jax.random.split(jax.random.key(seed), 10)
    return {
        "tokens": draw_tokens(jax.random.fold_in(streams_of[9], 71), 0),
        "norm_gain": jnp.clip(1.0 + 0.18 * jax.random.normal(streams_of[1], (D,), jnp.float32), 0.1, 1.9),
        "router": bell_draw(streams_of[2], (D,), D ** -0.5, 0.0625, ((0, 8),)),
        "w_gate": bell_draw(streams_of[3], (D, FF), D ** -0.5, 0.0625, ((0, 8), (1, 32))),
        "w_up": bell_draw(streams_of[4], (D, FF), D ** -0.5, 0.0625, ((0, 8), (1, 32))),
        "w_down": bell_draw(streams_of[5], (FF, D), FF ** -0.5, 0.03125, ((0, 32), (1, 8))),
        "routes": draw_routes(jax.random.fold_in(streams_of[9], 71), 0),
        "counts": uneven_parts(streams_of[7], N_CONTEXT, PICKED, CAP, 2).astype(jnp.int32),
        "cotangent": bell_draw(streams_of[8], (TOKENS, D), 1.0, 6.0, ((0, 32), (1, 8))),
    }


EPS = 1e-05

def contract_rows(left, right):
    return lax.dot_general(left, right, (((0,), (0,)), ((), ())), preferred_element_type=jnp.float32)

def contract_cols(left, right):
    return lax.dot_general(left, right, (((1,), (1,)), ((), ())), preferred_element_type=jnp.float32)

def reference(tokens, norm_gain, router, w_gate, w_up, w_down, routes, counts, cotangent):
    slot_ids = jnp.arange(CAP, dtype=jnp.int32)
    usable = (slot_ids[None, :] < counts[:, None]).reshape(-1)
    bases = jnp.arange(N_CONTEXT, dtype=jnp.int32) * TOK_DEV
    places = (routes + bases[:, None]).reshape(-1).astype(jnp.int32)
    chosen = jnp.nonzero(usable, size=PICKED)[0].astype(jnp.int32)
    row_ids = places[chosen].astype(jnp.int32)
    picked_low = tokens[row_ids]
    picked = picked_low.astype(jnp.float32)
    inv_rms = lax.rsqrt(lax.optimization_barrier(jnp.mean(picked * picked, axis=1, keepdims=True)) + EPS)
    scaled = picked * inv_rms
    normed = (scaled * norm_gain).astype(jnp.bfloat16)
    logit = jnp.dot(picked_low, router, preferred_element_type=jnp.float32)
    weight = jax.nn.sigmoid(logit)[:, None]
    gate = jnp.dot(normed, w_gate, preferred_element_type=jnp.float32)
    upward = jnp.dot(normed, w_up, preferred_element_type=jnp.float32)
    hidden = (jax.nn.silu(gate) * upward).astype(jnp.bfloat16)
    branch = jnp.dot(hidden, w_down, preferred_element_type=jnp.float32)
    mixed = tokens.at[row_ids].set((picked + weight * branch).astype(jnp.bfloat16))
    slope = cotangent[row_ids].astype(jnp.float32)
    d_branch = (weight * slope).astype(jnp.bfloat16)
    d_logit = lax.optimization_barrier(jnp.sum(slope * branch, axis=1, keepdims=True)) * weight * (1.0 - weight)
    d_hidden = contract_cols(d_branch, w_down)
    sigma = jax.nn.sigmoid(gate)
    d_gate = (d_hidden * upward * sigma * (1.0 + gate * (1.0 - sigma))).astype(jnp.bfloat16)
    d_upward = (d_hidden * gate * sigma).astype(jnp.bfloat16)
    grad_down = contract_rows(hidden, d_branch).astype(jnp.bfloat16)
    grad_gate = contract_rows(normed, d_gate).astype(jnp.bfloat16)
    grad_up = contract_rows(normed, d_upward).astype(jnp.bfloat16)
    d_normed = contract_cols(d_gate, w_gate) + contract_cols(d_upward, w_up)
    grad_gain = lax.optimization_barrier(jnp.sum(d_normed * scaled, axis=0))
    d_scaled = d_normed * norm_gain
    mean_term = lax.optimization_barrier(jnp.mean(d_scaled * picked, axis=1, keepdims=True))
    d_picked = inv_rms * (d_scaled - picked * inv_rms * inv_rms * mean_term) + d_logit * router.astype(jnp.float32)
    grad_tokens = cotangent.astype(jnp.float32).at[row_ids].add(d_picked).astype(jnp.bfloat16)
    grad_router = lax.optimization_barrier(jnp.sum(d_logit * picked, axis=0))
    return (mixed, grad_tokens, grad_gate, grad_up, grad_down, grad_gain, grad_router)
```

```python
import jax
import jax.numpy as jnp
from jax import lax
from jax.experimental import pallas as pl
from jax.experimental.pallas import tpu as pltpu
from jax.sharding import PartitionSpec as P

D = 8192
EPS = 1e-05
NX, NZ, NY = 4, 8, 4
SHARDS = NX * NZ
CAP = 24
ROWS = 512
CHUNK = 64
FFL = 896
COLS = 1024
MARK = 1024.0
MESH = pl.DeviceIdType.MESH
VMEM = pltpu.VMEM
F32 = jnp.float32
BF16 = jnp.bfloat16


def contract_rows(left, right):
    return lax.dot_general(left, right, (((0,), (0,)), ((), ())), preferred_element_type=F32)


def contract_cols(left, right):
    return lax.dot_general(left, right, (((1,), (1,)), ((), ())), preferred_element_type=F32)


def dot(left, right):
    return jnp.dot(left, right, preferred_element_type=F32)


class Net:
    def __init__(self, send_sems, recv_sems):
        self.send_sems, self.recv_sems = send_sems, recv_sems
        self.index, self.sent = {}, []

    def make(self, key, src, dst, device):
        k = self.index.setdefault(key, len(self.index))
        return pltpu.make_async_remote_copy(
            src_ref=src,
            dst_ref=dst,
            send_sem=self.send_sems.at[k],
            recv_sem=self.recv_sems.at[k],
            device_id=device,
            device_id_type=MESH,
        )

    def send(self, key, src, dst, device):
        copy = self.make(key, src, dst, device)
        copy.start()
        self.sent.append(copy)

    def arrive(self, key, dst, device):
        self.make(key, dst, dst, device).wait_recv()

    def finish(self):
        for copy in self.sent:
            copy.wait_send()


def enter(partners):
    barrier = pltpu.get_barrier_semaphore()
    for device in partners:
        pl.semaphore_signal(barrier, inc=1, device_id=device, device_id_type=MESH)
    pl.semaphore_wait(barrier, len(partners))


def place():
    c, t = lax.axis_index("context"), lax.axis_index("tensor")
    z, x = lax.div(c, NX), lax.rem(c, NX)

    def at(dz, dx):
        return lax.rem(z + dz + NZ, NZ) * NX + lax.rem(x + dx + NX, NX)

    return t, at


HALF = COLS // 2
QUART = COLS // 4
ORDER = (0, -1, 1, -2, 2, -3, 3, 4)


def gather_kernel(b_ref, g_ref, send_sems, recv_sems):
    t, at = place()
    net = Net(send_sems, recv_sems)

    def dev(dz, dx):
        return (at(dz, dx), t)

    def part(dz, dx, lo, n):
        return g_ref.at[at(dz, dx), :, pl.ds(lo, n)]

    g_ref[at(0, 0)] = b_ref[...]
    enter([dev(0, 1), dev(0, 2), dev(0, 3), dev(1, 0), dev(-1, 0)])

    def a_pass(s, j):
        if s < 4:
            r = part(1 - s, j, 0, HALF)
            net.send(("ar", s, j), r, r, dev(1, 0))
            r = part(s - 1, j, 0, HALF)
            net.send(("al", s, j), r, r, dev(-1, 0))
        else:
            r = part(1 - s, j, 0, QUART)
            net.send(("ar", s, j), r, r, dev(1, 0))
            r = part(s - 1, j, QUART, QUART)
            net.send(("al", s, j), r, r, dev(-1, 0))

    def a_take(s, j):
        if s < 4:
            net.arrive(("ar", s, j), part(-s, j, 0, HALF), dev(-1, 0))
            net.arrive(("al", s, j), part(s, j, 0, HALF), dev(1, 0))
        else:
            net.arrive(("ar", s, j), part(-s, j, 0, QUART), dev(-1, 0))
            net.arrive(("al", s, j), part(s, j, QUART, QUART), dev(1, 0))

    def b_pass(s):
        n = HALF if s < 4 else QUART
        r = part(1 - s, 0, HALF, n)
        net.send(("br", s), r, r, dev(1, 0))
        r = part(s - 1, 0, HALF + HALF - n, n)
        net.send(("bl", s), r, r, dev(-1, 0))

    def b_take(s):
        n = HALF if s < 4 else QUART
        net.arrive(("br", s), part(-s, 0, HALF, n), dev(-1, 0))
        net.arrive(("bl", s), part(s, 0, HALF + HALF - n, n), dev(1, 0))

    def b_side(o):
        r = part(o, 0, HALF, HALF)
        net.send(("xr", o), r, r, dev(0, 1))
        net.send(("xl", o), r, r, dev(0, -1))

    def b_cross(o):
        net.arrive(("xr", o), part(o, -1, HALF, HALF), dev(0, -1))
        r = part(o, -1, HALF, QUART)
        net.send(("dr", o), r, r, dev(0, 1))
        net.arrive(("xl", o), part(o, 1, HALF, HALF), dev(0, 1))
        r = part(o, 1, HALF + QUART, QUART)
        net.send(("dl", o), r, r, dev(0, -1))

    own = part(0, 0, 0, HALF)
    b_pass(1)
    for j in (1, 2, 3):
        net.send(("ax", j), own, own, dev(0, j))
    a_pass(1, 0)
    b_side(0)
    for j in (1, 3, 2):
        net.arrive(("ax", 4 - j), part(0, j, 0, HALF), dev(0, j))
        a_pass(1, j)
    for s in (1, 2, 3, 4):
        b_take(s)
        if s < 4:
            b_pass(s + 1)
            b_side(-s)
            b_side(s)
        else:
            b_side(4)
        for j in (0, 1, 3, 2):
            a_take(s, j)
            if s < 4:
                a_pass(s + 1, j)
        if s == 1:
            b_cross(0)
        else:
            b_cross(1 - s)
            b_cross(s - 1)
    b_cross(4)
    for o in ORDER:
        net.arrive(("dr", o), part(o, 2, HALF, QUART), dev(0, -1))
        net.arrive(("dl", o), part(o, 2, HALF + QUART, QUART), dev(0, 1))
    net.finish()


def gather_shards(block):
    return pl.pallas_call(
        gather_kernel,
        out_shape=jax.ShapeDtypeStruct((SHARDS, 2 * CAP, COLS), BF16),
        in_specs=[pl.BlockSpec(memory_space=VMEM)],
        out_specs=pl.BlockSpec(memory_space=VMEM),
        scratch_shapes=[
            pltpu.SemaphoreType.DMA((80,)),
            pltpu.SemaphoreType.DMA((80,)),
        ],
        compiler_params=pltpu.CompilerParams(
            collective_id=0, has_side_effects=True, vmem_limit_bytes=24 << 20
        ),
        name="gather_shards",
    )(block)


def middle_kernel(
    y_ref, st_ref, h_ref, stat_ref, p_ref,
    r1, acc, rd, rf, st_slots, p_slots, send_sems, recv_sems,
):
    c, t = lax.axis_index("context"), lax.axis_index("tensor")
    y, core = lax.div(t, 2), lax.rem(t, 2)
    net = Net(send_sems, recv_sems)

    def dev(dy, flip=0):
        k = 1 - core if flip else core
        return (c, lax.rem(y + dy + NY, NY) * 2 + k)

    def chunk(dy, flip=0):
        return dev(dy, flip)[1]

    peers = [(dy, f) for dy in range(NY) for f in (0, 1) if (dy, f) != (0, 0)]
    st_slots[t] = st_ref[...]
    enter([dev(dy, f) for dy, f in peers])

    for dy in (2, 1, 3, 0):
        net.send(("c", dy), y_ref.at[chunk(dy, 1)], r1.at[dy], dev(0, 1))
    for dy, f in peers:
        s = st_slots.at[t]
        net.send(("st", dy, f), s, s, dev(dy, f))

    def pair(dy, rows):
        return y_ref[chunk(dy), rows].astype(F32) + r1[dy, rows].astype(F32)

    top, low = pl.ds(0, 32), pl.ds(32, 32)
    net.arrive(("c", 2), r1.at[2], dev(0, 1))
    for i in range(4):
        rows = pl.ds(16 * i, 16)
        acc[2, rows] = pair(2, rows).astype(BF16)
    net.send(("dr",), acc.at[2, top], rd.at[0], dev(1))
    net.send(("dl",), acc.at[2, low], rd.at[1], dev(-1))
    for dy, k, key, plus in ((1, 0, ("dr",), (0, 1)), (3, 1, ("dl",), (2, 3))):
        net.arrive(("c", dy), r1.at[dy], dev(0, 1))
        net.arrive(key, rd.at[k], dev(-1 if dy == 1 else 1))
        for i in range(4):
            rows = pl.ds(16 * i, 16)
            v = pair(dy, rows)
            if i in plus:
                v = v + rd[k, pl.ds(16 * i - 32 * k, 16)].astype(F32)
            acc[dy, rows] = v.astype(BF16)
        net.send(("f", k), acc.at[dy], rf.at[k], dev(1 if dy == 1 else -1))

    for dy, f in peers:
        back = (NY - dy) % NY
        net.arrive(("st", dy, f), st_slots.at[chunk(back, f)], dev(back, f))
    stat = st_slots[0]
    for k in range(1, 8):
        stat = stat + st_slots[k]
    stat_ref[...] = stat
    sub = lax.broadcasted_iota(jnp.int32, (8, 128), 0)
    lane = lax.broadcasted_iota(jnp.int32, (CHUNK, 128), 1)
    row = lax.broadcasted_iota(jnp.int32, (CHUNK, 128), 0)
    mine = lane == row + core * CHUNK

    def column(which):
        line = jnp.sum(jnp.where(sub == which, stat, 0.0), axis=0, keepdims=True)
        return jnp.sum(jnp.where(mine, line, 0.0), axis=1, keepdims=True)

    inv_rms = lax.rsqrt(column(y) / D + EPS)
    weight = jax.nn.sigmoid(column(4 + y))

    net.arrive(("c", 0), r1.at[0], dev(0, 1))
    net.arrive(("f", 0), rf.at[0], dev(-1))
    net.arrive(("f", 1), rf.at[1], dev(1))
    firsts, seconds = [], []
    for i in range(4):
        rows = pl.ds(16 * i, 16)
        inv = inv_rms[16 * i:16 * i + 16]
        w = weight[16 * i:16 * i + 16]

        def total(k):
            cols = pl.ds(k * FFL, FFL)
            return (
                y_ref[t, rows, cols].astype(F32)
                + r1[0, rows, cols].astype(F32)
                + rf[0, rows, cols].astype(F32)
                + rf[1, rows, cols].astype(F32)
            )

        g_raw, u_raw, d_raw = total(0), total(1), total(2)
        gate, upward = g_raw * inv, u_raw * inv
        sigma = jax.nn.sigmoid(gate)
        act = gate * sigma
        hidden = (act * upward * w).astype(BF16)
        d_hidden = d_raw * (w * inv)
        d_gate = (d_hidden * upward * sigma * (1.0 + gate * (1.0 - sigma))).astype(BF16)
        d_up = (d_hidden * act).astype(BF16)
        h_ref[t, rows, pl.ds(0, FFL)] = hidden
        h_ref[t, rows, pl.ds(FFL, FFL)] = d_gate
        h_ref[t, rows, pl.ds(2 * FFL, FFL)] = d_up
        firsts.append(jnp.sum(d_raw * hidden.astype(F32), axis=1, keepdims=True))
        seconds.append(
            jnp.sum(d_gate.astype(F32) * g_raw + d_up.astype(F32) * u_raw, axis=1, keepdims=True)
        )

    own = h_ref.at[t]
    net.send(("gr",), own, own, dev(1))
    net.send(("gl",), own, own, dev(-1))
    net.send(("g", 0), own, own, dev(0, 1))

    def line_of(parts):
        return jnp.sum(jnp.where(mine, jnp.concatenate(parts, axis=0), 0.0), axis=0, keepdims=True)

    p_slots[t] = jnp.where(sub == y, line_of(firsts), 0.0) + jnp.where(
        sub == 4 + y, line_of(seconds), 0.0
    )
    for dy, f in peers:
        s = p_slots.at[t]
        net.send(("p", dy, f), s, s, dev(dy, f))

    net.arrive(("gr",), h_ref.at[chunk(-1)], dev(-1))
    r = h_ref.at[chunk(-1), top]
    net.send(("er",), r, r, dev(1))
    net.arrive(("gl",), h_ref.at[chunk(1)], dev(1))
    r = h_ref.at[chunk(1), low]
    net.send(("el",), r, r, dev(-1))
    for dy in (3, 1):
        r = h_ref.at[chunk(dy)]
        net.send(("g", dy), r, r, dev(0, 1))
    net.arrive(("er",), h_ref.at[chunk(2), top], dev(-1))
    net.arrive(("el",), h_ref.at[chunk(2), low], dev(1))
    r = h_ref.at[chunk(2)]
    net.send(("g", 2), r, r, dev(0, 1))
    for dy, f in peers:
        back = (NY - dy) % NY
        net.arrive(("p", dy, f), p_slots.at[chunk(back, f)], dev(back, f))
    p = p_slots[0]
    for k in range(1, 8):
        p = p + p_slots[k]
    p_ref[...] = p
    for dy in (0, 3, 1, 2):
        net.arrive(("g", dy), h_ref.at[chunk(dy, 1)], dev(0, 1))
    net.finish()


def middle(parts, stats):
    return pl.pallas_call(
        middle_kernel,
        out_shape=(
            jax.ShapeDtypeStruct((8, CHUNK, 3 * FFL), BF16),
            jax.ShapeDtypeStruct((8, 128), F32),
            jax.ShapeDtypeStruct((8, 128), F32),
        ),
        in_specs=[pl.BlockSpec(memory_space=VMEM)] * 2,
        out_specs=(pl.BlockSpec(memory_space=VMEM),) * 3,
        scratch_shapes=[
            VMEM((4, CHUNK, 3 * FFL), BF16),
            VMEM((4, CHUNK, 3 * FFL), BF16),
            VMEM((2, CHUNK // 2, 3 * FFL), BF16),
            VMEM((2, CHUNK, 3 * FFL), BF16),
            VMEM((8, 8, 128), F32),
            VMEM((8, 8, 128), F32),
            pltpu.SemaphoreType.DMA((40,)),
            pltpu.SemaphoreType.DMA((40,)),
        ],
        compiler_params=pltpu.CompilerParams(
            collective_id=1, has_side_effects=True, vmem_limit_bytes=32 << 20
        ),
        name="middle",
    )(parts, stats)


def scatter_kernel(
    v_ref, small_ref, out_ref, tot_ref,
    za, zb, xa, xb, w, sx, sz, send_sems, recv_sems,
):
    t, at = place()
    net = Net(send_sems, recv_sems)

    def dev(dz, dx):
        return (at(dz, dx), t)

    own_x = at(0, 0)
    sx[0] = small_ref[...]
    enter([dev(0, dx) for dx in (1, 2, 3)] + [dev(dz, 0) for dz in range(1, NZ)])

    def mine(dz, dx, lo, n):
        return v_ref[at(dz, dx), :, pl.ds(lo, n)].astype(F32)

    def b_start(i, o):
        far = v_ref.at[at(o, 2), :, pl.ds(HALF, QUART)]
        net.send(("xr1", i), far, xb.at[i, 0, :, pl.ds(0, QUART)], dev(0, 1))
        far = v_ref.at[at(o, 2), :, pl.ds(HALF + QUART, QUART)]
        net.send(("xl1", i), far, xb.at[i, 1, :, pl.ds(QUART, QUART)], dev(0, -1))

    first, second = pl.ds(0, QUART), pl.ds(QUART, QUART)

    def b_next(i, o):
        net.arrive(("xr1", i), xb.at[i, 0, :, first], dev(0, -1))
        xb[i, 0, :, first] = (xb[i, 0, :, first].astype(F32) + mine(o, 1, HALF, QUART)).astype(BF16)
        xb[i, 0, :, second] = v_ref[at(o, 1), :, pl.ds(HALF + QUART, QUART)]
        net.send(("xr2", i), xb.at[i, 0], xb.at[i, 2], dev(0, 1))
        net.arrive(("xl1", i), xb.at[i, 1, :, second], dev(0, 1))
        xb[i, 1, :, second] = (
            xb[i, 1, :, second].astype(F32) + mine(o, -1, HALF + QUART, QUART)
        ).astype(BF16)
        xb[i, 1, :, first] = v_ref[at(o, -1), :, pl.ds(HALF, QUART)]
        net.send(("xl2", i), xb.at[i, 1], xb.at[i, 3], dev(0, -1))

    def b_sum(i, o):
        net.arrive(("xr2", i), xb.at[i, 2], dev(0, -1))
        net.arrive(("xl2", i), xb.at[i, 3], dev(0, 1))
        return mine(o, 0, HALF, HALF) + xb[i, 2].astype(F32) + xb[i, 3].astype(F32)

    def ring_first(tag, k, right, left, buf):
        net.send((tag, "r", 1, k), right, buf.at[0, 0, :, first], dev(1, 0))
        net.send((tag, "l", 1, k), left, buf.at[1, 0, :, second], dev(-1, 0))

    def ring_next(tag, k, s, right, left, buf):
        for d, (name, term, back) in enumerate((("r", right, -1), ("l", left, 1))):
            if s == 2:
                cols, rest = (first, second) if d == 0 else (second, first)
                net.arrive((tag, name, 1, k), buf.at[d, 0, :, cols], dev(back, 0))
                lo = 0 if d == 0 else QUART
                hi = QUART - lo
                buf[d, 0, :, cols] = (
                    buf[d, 0, :, cols].astype(F32) + term[:, lo:lo + QUART]
                ).astype(BF16)
                buf[d, 0, :, rest] = term[:, hi:hi + QUART].astype(BF16)
            else:
                net.arrive((tag, name, s - 1, k), buf.at[d, s - 2], dev(back, 0))
                buf[d, s - 2] = (buf[d, s - 2].astype(F32) + term).astype(BF16)
            net.send((tag, name, s, k), buf.at[d, s - 2], buf.at[d, s - 1], dev(-back, 0))

    def ring_last(tag, k, term, buf):
        net.arrive((tag, "r", 4, k), buf.at[0, 3], dev(-1, 0))
        net.arrive((tag, "l", 4, k), buf.at[1, 3], dev(1, 0))
        return term + buf[0, 3].astype(F32) + buf[1, 3].astype(F32)

    order = (4, 3, -3, 2, -2, 1, -1, 0)
    lanes = (2, 1, 3, 0)
    for i in (0, 1, 2):
        b_start(i, order[i])
    for j in lanes:
        ring_first(
            "a", j,
            v_ref.at[at(4, j), :, pl.ds(0, QUART)],
            v_ref.at[at(4, j), :, pl.ds(QUART, QUART)],
            za.at[j],
        )
    for i in (3, 4, 5, 6, 7):
        b_start(i, order[i])
    for dx in (1, 2, 3):
        net.send(("sx", dx), sx.at[0], sx.at[dx], dev(0, dx))

    for i in (0, 1, 2):
        b_next(i, order[i])
    for j in lanes:
        ring_next("a", j, 2, mine(3, j, 0, HALF), mine(-3, j, 0, HALF), za.at[j])
    for i in (3, 4, 5, 6, 7):
        b_next(i, order[i])

    for dx in (1, 2, 3):
        net.arrive(("sx", dx), sx.at[dx], dev(0, -dx))
    sz[0] = sx[0] + sx[1] + sx[2] + sx[3]
    for dz in range(1, NZ):
        net.send(("sz", dz), sz.at[0], sz.at[dz], dev(dz, 0))

    w[...] = b_sum(0, 4).astype(BF16)
    ring_first("b", 0, w.at[:, first], w.at[:, second], zb)
    for j in lanes:
        ring_next("a", j, 3, mine(2, j, 0, HALF), mine(-2, j, 0, HALF), za.at[j])
    ring_next("b", 0, 2, b_sum(1, 3), b_sum(2, -3), zb)
    for j in lanes:
        ring_next("a", j, 4, mine(1, j, 0, HALF), mine(-1, j, 0, HALF), za.at[j])
    ring_next("b", 0, 3, b_sum(3, 2), b_sum(4, -2), zb)
    for j in (2, 1, 3):
        v = ring_last("a", j, mine(0, j, 0, HALF), za.at[j])
        xa[j, 0] = v.astype(BF16)
        net.send(("xa", j), xa.at[j, 0], xa.at[j, 1], dev(0, j))
    ring_next("b", 0, 4, b_sum(5, 1), b_sum(6, -1), zb)
    v = ring_last("a", 0, mine(0, 0, 0, HALF), za.at[0])
    for j in (1, 3, 2):
        net.arrive(("xa", j), xa.at[j, 1], dev(0, -j))
        v = v + xa[j, 1].astype(F32)
    out_ref[:, pl.ds(0, HALF)] = v
    out_ref[:, pl.ds(HALF, HALF)] = ring_last("b", 0, b_sum(7, 0), zb)
    for dz in range(1, NZ):
        net.arrive(("sz", dz), sz.at[dz], dev(-dz, 0))
    tot = sz[0]
    for dz in range(1, NZ):
        tot = tot + sz[dz]
    tot_ref[...] = tot
    net.finish()


def scatter_sums(values, small):
    n = 2 * CAP
    return pl.pallas_call(
        scatter_kernel,
        out_shape=(
            jax.ShapeDtypeStruct((n, COLS), F32),
            jax.ShapeDtypeStruct((16, 128), F32),
        ),
        in_specs=[pl.BlockSpec(memory_space=VMEM)] * 2,
        out_specs=(pl.BlockSpec(memory_space=VMEM),) * 2,
        scratch_shapes=[
            VMEM((4, 2, 4, n, HALF), BF16),
            VMEM((2, 4, n, HALF), BF16),
            VMEM((4, 2, n, HALF), BF16),
            VMEM((8, 4, n, HALF), BF16),
            VMEM((n, HALF), BF16),
            VMEM((4, 16, 128), F32),
            VMEM((8, 16, 128), F32),
            pltpu.SemaphoreType.DMA((96,)),
            pltpu.SemaphoreType.DMA((96,)),
        ],
        compiler_params=pltpu.CompilerParams(
            collective_id=2, has_side_effects=True, vmem_limit_bytes=32 << 20
        ),
        name="scatter_sums",
    )(values, small)


def body(tokens, norm_gain, router, w_gate, w_up, w_down, routes, counts, cotangent):
    live_count = counts[0]
    usable = (jnp.arange(CAP, dtype=jnp.int32) < live_count)[:, None]
    local_ids = routes[0]
    picked_low = jnp.take(tokens, local_ids, axis=0)
    slope_low = jnp.take(cotangent, local_ids, axis=0)
    block = jnp.concatenate(
        [jnp.where(usable, picked_low, jnp.asarray(MARK, BF16)), slope_low], axis=0
    )
    blocks = gather_shards(block)
    x_pad = blocks[:, :CAP].reshape(SHARDS * CAP, COLS)
    s_pad = blocks[:, CAP:].reshape(SHARDS * CAP, COLS)
    live = x_pad[:, 0].astype(F32) < 0.5 * MARK
    spot = jnp.cumsum(live.astype(jnp.int32)) - 1
    spot = jnp.where(live, spot, -1)
    select = (spot[None, :] == jnp.arange(ROWS, dtype=jnp.int32)[:, None]).astype(BF16)
    x_all = dot(select, x_pad).astype(BF16)
    s_all = dot(select, s_pad).astype(BF16)
    x_f32 = x_all.astype(F32)
    normed = (x_f32 * norm_gain).astype(BF16)
    sums = jnp.concatenate(
        [
            dot(normed, w_gate).astype(BF16),
            dot(normed, w_up).astype(BF16),
            contract_cols(s_all, w_down).astype(BF16),
        ],
        axis=1,
    )
    stats = jnp.concatenate(
        [
            jnp.sum(x_f32 * x_f32, axis=1),
            jnp.sum(x_f32 * router.astype(F32), axis=1),
        ]
    ).reshape(8, 128)
    acts, stats, inner = middle(sums.reshape(8, CHUNK, 3 * FFL), stats)
    acts = acts.reshape(ROWS, 3 * FFL)
    hidden, d_gate, d_up = acts[:, :FFL], acts[:, FFL:2 * FFL], acts[:, 2 * FFL:]
    branch = dot(hidden, w_down)
    d_normed = contract_cols(d_gate, w_gate) + contract_cols(d_up, w_up)
    gain_part = jnp.sum(d_normed * x_f32, axis=0)
    values = jnp.concatenate(
        [
            contract_rows(select, branch.astype(BF16)).astype(BF16).reshape(SHARDS, CAP, COLS),
            contract_rows(select, d_normed.astype(BF16)).astype(BF16).reshape(SHARDS, CAP, COLS),
        ],
        axis=1,
    )
    small = jnp.concatenate([inner, gain_part.reshape(8, 128)], axis=0)
    ends, small = scatter_sums(values, small)
    grad_down = contract_rows(hidden, s_all).astype(BF16)
    grad_gate = contract_rows(normed, d_gate).astype(BF16)
    grad_up = contract_rows(normed, d_up).astype(BF16)

    inv_sq = 1.0 / (stats[:4].reshape(ROWS) / D + EPS)
    weight = jax.nn.sigmoid(stats[4:].reshape(ROWS))
    d_logit = small[:4].reshape(ROWS) * (1.0 - weight)
    mean_term = small[4:8].reshape(ROWS) / D * inv_sq
    grad_gain = small[8:].reshape(COLS)
    grad_router = jnp.sum(d_logit[:, None] * x_f32, axis=0)
    own = lax.dynamic_slice(spot, (lax.axis_index("context") * CAP,), (CAP,))
    own = jnp.maximum(own, 0)
    d_logit = jnp.take(d_logit, own)[:, None]
    mean_term = jnp.take(mean_term, own)[:, None]
    picked = picked_low.astype(F32)
    mixed_rows = (picked + ends[:CAP]).astype(BF16)
    mixed = tokens.at[local_ids].set(jnp.where(usable, mixed_rows, picked_low))
    d_picked = ends[CAP:] * norm_gain - picked * mean_term + d_logit * router.astype(F32)
    grad_rows = (slope_low.astype(F32) + d_picked).astype(BF16)
    grad_tokens = cotangent.at[local_ids].set(jnp.where(usable, grad_rows, slope_low))
    return (mixed, grad_tokens, grad_gate, grad_up, grad_down, grad_gain, grad_router)


def solution(mesh):
    return jax.shard_map(
        body,
        mesh=mesh,
        in_specs=(
            P("context", "tensor"),
            P("tensor"),
            P("tensor"),
            P("tensor", "context"),
            P("tensor", "context"),
            P("context", "tensor"),
            P("context", None),
            P("context"),
            P("context", "tensor"),
        ),
        out_specs=(
            P("context", "tensor"),
            P("context", "tensor"),
            P("tensor", "context"),
            P("tensor", "context"),
            P("context", "tensor"),
            P("tensor"),
            P("tensor"),
        ),
        check_vma=False,
    )
```

```python
import jax
import jax.numpy as jnp
from jax import lax
from jax.experimental import pallas as pl
from jax.experimental.pallas import tpu as pltpu
from jax.sharding import PartitionSpec as P

D = 8192
EPS = 1e-05
NX, NZ, NY = 4, 8, 4
SHARDS = NX * NZ
CAP = 24
SLOTS = SHARDS * CAP
ROWS = 512
CHUNK = 64
FFL = 896
COLS = 1024
TALL, WIDE = 2 * CAP, COLS // 2
HALF, QUART = WIDE // 2, WIDE // 4
MARK = 1024.0
SEMS = 320
MESH = pl.DeviceIdType.MESH
VMEM = pltpu.VMEM
F32 = jnp.float32
BF16 = jnp.bfloat16
FF_TILES = ((0, 256), (256, 256), (512, 256), (768, 128))
COL_TILES = ((0, 256), (256, 256), (512, 256), (768, 256))


def contract_rows(left, right):
    return lax.dot_general(left, right, (((0,), (0,)), ((), ())), preferred_element_type=F32)


def contract_cols(left, right):
    return lax.dot_general(left, right, (((1,), (1,)), ((), ())), preferred_element_type=F32)


def dot(left, right):
    return jnp.dot(left, right, preferred_element_type=F32)


class Net:
    def __init__(self, send_sems, recv_sems):
        self.send_sems, self.recv_sems = send_sems, recv_sems
        self.index, self.sent = {}, []

    def make(self, key, src, dst, device):
        k = self.index.setdefault(key, len(self.index))
        assert k < SEMS
        return pltpu.make_async_remote_copy(
            src_ref=src,
            dst_ref=dst,
            send_sem=self.send_sems.at[k],
            recv_sem=self.recv_sems.at[k],
            device_id=device,
            device_id_type=MESH,
        )

    def send(self, key, src, dst, device):
        copy = self.make(key, src, dst, device)
        copy.start()
        self.sent.append(copy)

    def arrive(self, key, dst, device):
        self.make(key, dst, dst, device).wait_recv()

    def finish(self):
        for copy in self.sent:
            copy.wait_send()


class Place:
    def __init__(self):
        self.c, self.t = lax.axis_index("context"), lax.axis_index("tensor")
        self.z, self.x = lax.div(self.c, NX), lax.rem(self.c, NX)
        self.y, self.core = lax.div(self.t, 2), lax.rem(self.t, 2)
        self.odd = lax.rem(self.x, 2)
        self.pair = lax.div(self.x, 2)

    def at_z(self, dz):
        return lax.rem(self.z + dz + NZ, NZ)

    def at(self, dz, dx):
        return self.at_z(dz) * NX + lax.rem(self.x + dx + NX, NX)

    def dev(self, dz, dx):
        return (self.at(dz, dx), self.t)

    def mate(self, q):
        if q == 1:
            return self.x + 1 - 2 * self.odd
        return lax.rem(self.x + 2, NX) if q == 2 else 3 - self.x

    def mate_at(self, q):
        return self.z * NX + self.mate(q)

    def mate_dev(self, q):
        return (self.mate_at(q), self.t)

    def pair_at(self, dz, other):
        p = 1 - self.pair if other else self.pair
        return pl.ds(self.at_z(dz) * NX + 2 * p, 2)

    def chunk(self, dy, flip=0):
        k = 1 - self.core if flip else self.core
        return lax.rem(self.y + dy + NY, NY) * 2 + k

    def peer(self, dy, flip=0):
        return (self.c, self.chunk(dy, flip))


PEERS = [(dy, f) for dy in range(NY) for f in (0, 1) if (dy, f) != (0, 0)]


class Gather:
    def __init__(self, tag, net, me, g):
        self.tag, self.net, self.me, self.g = tag, net, me, g

    def part(self, dz, dx, lo, n):
        return self.g.at[self.me.at(dz, dx), :, pl.ds(lo, n)]

    def duo(self, dz, other, lo, n):
        return self.g.at[self.me.pair_at(dz, other), :, pl.ds(lo, n)]

    def send(self, key, ref, device):
        self.net.send((self.tag,) + key, ref, ref, device)

    def arrive(self, key, ref, device):
        self.net.arrive((self.tag,) + key, ref, device)

    def spans(self, s):
        return ((0, HALF), (0, HALF)) if s < 4 else ((0, QUART), (QUART, QUART))

    def a_pass(self, s, other):
        right, left = self.spans(s)
        self.send(("ar", s, other), self.duo(1 - s, other, *right), self.me.dev(1, 0))
        self.send(("al", s, other), self.duo(s - 1, other, *left), self.me.dev(-1, 0))

    def a_take(self, s, other):
        right, left = self.spans(s)
        self.arrive(("ar", s, other), self.duo(-s, other, *right), self.me.dev(-1, 0))
        self.arrive(("al", s, other), self.duo(s, other, *left), self.me.dev(1, 0))

    def b_pass(self, s):
        (r, n), (l, _) = self.spans(s)
        self.send(("br", s), self.part(1 - s, 0, HALF + r, n), self.me.dev(1, 0))
        self.send(("bl", s), self.part(s - 1, 0, HALF + l, n), self.me.dev(-1, 0))

    def b_take(self, s):
        (r, n), (l, _) = self.spans(s)
        self.arrive(("br", s), self.part(-s, 0, HALF + r, n), self.me.dev(-1, 0))
        self.arrive(("bl", s), self.part(s, 0, HALF + l, n), self.me.dev(1, 0))

    def b_side(self, o):
        r = self.part(o, 0, HALF, HALF)
        self.send(("xr", o), r, self.me.dev(0, 1))
        self.send(("xl", o), r, self.me.dev(0, -1))

    def b_cross(self, o):
        self.arrive(("xr", o), self.part(o, -1, HALF, HALF), self.me.dev(0, -1))
        self.send(("dr", o), self.part(o, -1, HALF, QUART), self.me.dev(0, 1))
        self.arrive(("xl", o), self.part(o, 1, HALF, HALF), self.me.dev(0, 1))
        self.send(("dl", o), self.part(o, 1, HALF + QUART, QUART), self.me.dev(0, -1))

    def start(self):
        own = self.part(0, 0, 0, HALF)
        for q in (1, 2, 3):
            self.send(("ax", q), own, self.me.mate_dev(q))
        self.b_pass(1)
        self.b_side(0)

    def begin_ring(self):
        for q in (1, 2, 3):
            ref = self.g.at[self.me.mate_at(q), :, pl.ds(0, HALF)]
            self.arrive(("ax", q), ref, self.me.mate_dev(q))
            if q != 2:
                self.a_pass(1, int(q == 3))

    def step(self, s):
        self.b_take(s)
        if s < 4:
            self.b_pass(s + 1)
            self.b_side(-s)
            self.b_side(s)
        else:
            self.b_side(4)
        for other in (0, 1):
            self.a_take(s, other)
            if s < 4:
                self.a_pass(s + 1, other)
        for o in ((0,) if s == 1 else (1 - s, s - 1)):
            self.b_cross(o)

    def drain(self):
        self.b_cross(4)
        for o in (0, -1, 1, -2, 2, -3, 3, 4):
            self.arrive(("dr", o), self.part(o, 2, HALF, QUART), self.me.dev(0, -1))
            self.arrive(("dl", o), self.part(o, 2, HALF + QUART, QUART), self.me.dev(0, 1))


class Scatter:
    ORDER = (4, 3, -3, 2, -2, 1, -1, 0)

    def __init__(self, tag, net, me, v, za, zb, xa, xb, fin, w):
        self.tag, self.net, self.me, self.v = tag, net, me, v
        self.za, self.zb, self.xa, self.xb, self.fin, self.w = za, zb, xa, xb, fin, w

    def send(self, key, src, dst, device):
        self.net.send((self.tag,) + key, src, dst, device)

    def arrive(self, key, ref, device):
        self.net.arrive((self.tag,) + key, ref, device)

    def mine(self, dz, dx, lo, n):
        return self.v[self.me.at(dz, dx), :, pl.ds(lo, n)].astype(F32)

    def duo(self, dz, other):
        return self.v[self.me.pair_at(dz, other), :, pl.ds(0, HALF)].astype(F32)

    def b_start(self, i):
        o = self.ORDER[i]
        k = self.me.at(o, 2)
        self.send(("xr1", i), self.v.at[k, :, pl.ds(HALF, QUART)],
                  self.xb.at[i, 0, :, pl.ds(0, QUART)], self.me.dev(0, 1))
        self.send(("xl1", i), self.v.at[k, :, pl.ds(HALF + QUART, QUART)],
                  self.xb.at[i, 1, :, pl.ds(QUART, QUART)], self.me.dev(0, -1))

    def b_next(self, i):
        o, xb = self.ORDER[i], self.xb
        first, second = pl.ds(0, QUART), pl.ds(QUART, QUART)
        self.arrive(("xr1", i), xb.at[i, 0, :, first], self.me.dev(0, -1))
        term = self.mine(o, 1, HALF, HALF)
        xb[i, 0, :, first] = (xb[i, 0, :, first].astype(F32) + term[:, :QUART]).astype(BF16)
        xb[i, 0, :, second] = term[:, QUART:].astype(BF16)
        self.send(("xr2", i), xb.at[i, 0], xb.at[i, 2], self.me.dev(0, 1))
        self.arrive(("xl1", i), xb.at[i, 1, :, second], self.me.dev(0, 1))
        term = self.mine(o, -1, HALF, HALF)
        xb[i, 1, :, second] = (xb[i, 1, :, second].astype(F32) + term[:, QUART:]).astype(BF16)
        xb[i, 1, :, first] = term[:, :QUART].astype(BF16)
        self.send(("xl2", i), xb.at[i, 1], xb.at[i, 3], self.me.dev(0, -1))

    def b_sum(self, i):
        self.arrive(("xr2", i), self.xb.at[i, 2], self.me.dev(0, -1))
        self.arrive(("xl2", i), self.xb.at[i, 3], self.me.dev(0, 1))
        return (self.mine(self.ORDER[i], 0, HALF, HALF)
                + self.xb[i, 2].astype(F32) + self.xb[i, 3].astype(F32))

    def ring_first(self, k, right, left, buf):
        self.send(("r", 1, k), right, buf.at[0, 0, ..., pl.ds(0, QUART)], self.me.dev(1, 0))
        self.send(("l", 1, k), left, buf.at[1, 0, ..., pl.ds(QUART, QUART)], self.me.dev(-1, 0))

    def ring_next(self, k, s, right, left, buf):
        for d, (name, term, back) in enumerate((("r", right, -1), ("l", left, 1))):
            if s == 2:
                lo = d * QUART
                hi = QUART - lo
                cols = pl.ds(lo, QUART)
                self.arrive((name, 1, k), buf.at[d, 0, ..., cols], self.me.dev(back, 0))
                buf[d, 0, ..., cols] = (
                    buf[d, 0, ..., cols].astype(F32) + term[..., lo:lo + QUART]
                ).astype(BF16)
                buf[d, 0, ..., pl.ds(hi, QUART)] = term[..., hi:hi + QUART].astype(BF16)
            else:
                self.arrive((name, s - 1, k), buf.at[d, s - 2], self.me.dev(back, 0))
                buf[d, s - 2] = (buf[d, s - 2].astype(F32) + term).astype(BF16)
            self.send((name, s, k), buf.at[d, s - 2], buf.at[d, s - 1], self.me.dev(-back, 0))

    def ring_last(self, k, term, buf):
        self.arrive(("r", 4, k), buf.at[0, 3], self.me.dev(-1, 0))
        self.arrive(("l", 4, k), buf.at[1, 3], self.me.dev(1, 0))
        return term + buf[0, 3].astype(F32) + buf[1, 3].astype(F32)

    def a_ring(self, s):
        for other in (1, 0):
            self.ring_next(other, s, self.duo(5 - s, other), self.duo(s - 5, other),
                           self.za.at[other])

    def start(self):
        for i in range(4):
            self.b_start(i)
        for other in (1, 0):
            k = self.me.pair_at(4, other)
            self.ring_first(other, self.v.at[k, :, pl.ds(0, QUART)],
                            self.v.at[k, :, pl.ds(QUART, QUART)], self.za.at[other])
        for i in range(4, 8):
            self.b_start(i)

    def turn(self):
        for i in range(3):
            self.b_next(i)
        self.a_ring(2)
        for i in range(3, 8):
            self.b_next(i)

    def second(self):
        self.w[...] = self.b_sum(0).astype(BF16)
        self.ring_first("b", self.w.at[:, pl.ds(0, QUART)], self.w.at[:, pl.ds(QUART, QUART)], self.zb)
        self.a_ring(3)
        self.ring_next("b", 2, self.b_sum(1), self.b_sum(2), self.zb)

    def third(self):
        self.a_ring(4)
        self.ring_next("b", 3, self.b_sum(3), self.b_sum(4), self.zb)

    def fourth(self):
        me, odd = self.me, self.me.odd
        for other in (1, 0):
            total = self.ring_last(other, self.duo(0, other), self.za.at[other])
            self.fin[other] = total.astype(BF16)
        for q, other, k in ((3, 1, 1 - odd), (2, 1, odd), (1, 0, 1 - odd)):
            self.send(("xa", q), self.fin.at[other, k], self.xa.at[q], me.mate_dev(q))
        self.ring_next("b", 4, self.b_sum(5), self.b_sum(6), self.zb)

    def last(self):
        total = self.fin[0, self.me.odd].astype(F32)
        for q in (1, 3, 2):
            self.arrive(("xa", q), self.xa.at[q], self.me.mate_dev(q))
            total = total + self.xa[q].astype(F32)
        return total, self.ring_last("b", self.b_sum(7), self.zb)


class Unit:
    def __init__(self, net, me, y, h, r1, acc, rd, rf):
        self.net, self.me, self.y, self.h = net, me, y, h
        self.r1, self.acc, self.rd, self.rf = r1, acc, rd, rf

    def pair(self, k, dy):
        return self.y[k, self.me.chunk(dy)].astype(F32) + self.r1[k, dy].astype(F32)

    def share(self, k):
        for dy in (2, 1, 3, 0):
            self.net.send(("c", k, dy), self.y.at[k, self.me.chunk(dy, 1)], self.r1.at[k, dy],
                          self.me.peer(0, 1))

    def far(self, k):
        self.net.arrive(("c", k, 2), self.r1.at[k, 2], self.me.peer(0, 1))
        self.acc[k, 2] = self.pair(k, 2).astype(BF16)
        self.net.send(("dr", k), self.acc.at[k, 2, pl.ds(0, 32)], self.rd.at[k, 0], self.me.peer(1))
        self.net.send(("dl", k), self.acc.at[k, 2, pl.ds(32, 32)], self.rd.at[k, 1], self.me.peer(-1))

    def near(self, k):
        for dy, i, key, back in ((1, 0, "dr", -1), (3, 1, "dl", 1)):
            self.net.arrive(("c", k, dy), self.r1.at[k, dy], self.me.peer(0, 1))
            v = self.pair(k, dy)
            self.net.arrive((key, k), self.rd.at[k, i], self.me.peer(back))
            lo = 32 * i
            hi = 32 - lo
            self.acc[k, dy, pl.ds(lo, 32)] = (
                v[lo:lo + 32] + self.rd[k, i].astype(F32)
            ).astype(BF16)
            self.acc[k, dy, pl.ds(hi, 32)] = v[hi:hi + 32].astype(BF16)
            self.net.send(("f", k, i), self.acc.at[k, dy], self.rf.at[k, i], self.me.peer(-back))

    def settle(self, k):
        self.net.arrive(("c", k, 0), self.r1.at[k, 0], self.me.peer(0, 1))
        self.net.arrive(("f", k, 0), self.rf.at[k, 0], self.me.peer(-1))
        self.net.arrive(("f", k, 1), self.rf.at[k, 1], self.me.peer(1))

    def total(self, k, rows):
        return (
            self.y[k, self.me.t, rows].astype(F32)
            + self.r1[k, 0, rows].astype(F32)
            + self.rf[k, 0, rows].astype(F32)
            + self.rf[k, 1, rows].astype(F32)
        )

    def spread(self, k):
        own = self.h.at[k, self.me.t]
        self.net.send(("gr", k), own, own, self.me.peer(1))
        self.net.send(("gl", k), own, own, self.me.peer(-1))
        self.net.send(("g", k, 0), own, own, self.me.peer(0, 1))

    def relay(self, k):
        me = self.me
        for key, onward, dy, lo in (("gr", "er", -1, 0), ("gl", "el", 1, 32)):
            ref = self.h.at[k, me.chunk(dy)]
            self.net.arrive((key, k), ref, me.peer(dy))
            half = self.h.at[k, me.chunk(dy), pl.ds(lo, 32)]
            self.net.send((onward, k), half, half, me.peer(-dy))
            self.net.send(("g", k, dy), ref, ref, me.peer(0, 1))

    def close(self, k):
        me = self.me
        self.net.arrive(("er", k), self.h.at[k, me.chunk(2), pl.ds(0, 32)], me.peer(-1))
        self.net.arrive(("el", k), self.h.at[k, me.chunk(2), pl.ds(32, 32)], me.peer(1))
        ref = self.h.at[k, me.chunk(2)]
        self.net.send(("g", k, 2), ref, ref, me.peer(0, 1))
        for dy in (0, -1, 1, 2):
            self.net.arrive(("g", k, dy), self.h.at[k, me.chunk(dy, 1)], me.peer(0, 1))


def block_kernel(
    xb_ref, sb_ref, gain_ref, router_ref, wg_hbm, wu_hbm, wd_hbm,
    mix_ref, gt_ref, tot_ref, gr_ref, gg_hbm, gu_hbm, gd_hbm,
    wg, wu, wd, gx, gs, pad, low, up, spot, sel, sel_t, x_all, x_gain, s_all,
    y, h, r1, acc, rd, rf, st_slots, p_slots, prod, vb, vn,
    za_b, zb_b, xa_b, xb_b, fin_b, w_b, za_n, zb_n, xa_n, xb_n, fin_n, w_n,
    sx, sz, go, local_sems, send_sems, recv_sems,
):
    me = Place()
    net = Net(send_sems, recv_sems)
    loads = [
        pltpu.make_async_copy(src, dst, local_sems.at[i])
        for i, (src, dst) in enumerate(((wg_hbm, wg), (wu_hbm, wu), (wd_hbm, wd)))
    ]
    for load in loads:
        load.start()
    gx[me.c] = xb_ref[...]
    gs[me.c] = sb_ref[...]
    barrier = pltpu.get_barrier_semaphore()
    friends = (
        [me.dev(dz, 0) for dz in range(1, NZ)]
        + [me.dev(0, dx) for dx in range(1, NX)]
        + [me.peer(dy, f) for dy, f in PEERS]
    )
    for device in friends:
        pl.semaphore_signal(barrier, inc=1, device_id=device, device_id_type=MESH)
    pl.semaphore_wait(barrier, len(friends))

    gather_x = Gather("X", net, me, gx)
    gather_s = Gather("S", net, me, gs)
    unit = Unit(net, me, y, h, r1, acc, rd, rf)

    gather_x.start()
    for i in range(6):
        rows = pl.ds(128 * i, 128)
        r = lax.broadcasted_iota(jnp.int32, (128, SLOTS), 0) + 128 * i
        k = lax.broadcasted_iota(jnp.int32, (128, SLOTS), 1)
        same = jnp.where(r == k, MARK, 0.0)
        low[rows] = jnp.where(k < r, 1.0, same).astype(BF16)
        up[rows] = jnp.where(r < k, 1.0, same).astype(BF16)
    gather_x.begin_ring()
    for s in (1, 2, 3):
        gather_x.step(s)
    gather_s.start()
    gather_x.step(4)
    gather_x.drain()
    gather_s.begin_ring()

    def flatten(g):
        @pl.loop(0, NZ)
        def _(i):
            v = g[pl.ds(NX * i, NX)].astype(F32)
            rows = pl.ds(pl.multiple_of(i * (NX * CAP), 32), NX * CAP)
            pad[rows, pl.ds(0, WIDE)] = v[:, :CAP].reshape(NX * CAP, WIDE).astype(BF16)
            pad[rows, pl.ds(WIDE, WIDE)] = v[:, CAP:].reshape(NX * CAP, WIDE).astype(BF16)

    flatten(gx)
    live = jnp.where(pad[:, pl.ds(0, 128)].astype(F32)[:, 0:1] < 0.5 * MARK, 1.0, 0.0)
    live = jnp.broadcast_to(live, (SLOTS, 128)).astype(BF16)
    spot[...] = dot(low[...], live) - MARK
    line = contract_rows(live, up[...])[0:1] - MARK
    sel[...] = jnp.where(
        line == lax.broadcasted_iota(jnp.int32, (ROWS, SLOTS), 0).astype(F32), 1.0, 0.0
    ).astype(BF16)
    sq = jnp.zeros((ROWS, 128), F32)
    lg = jnp.zeros((ROWS, 128), F32)
    for lo, n in COL_TILES:
        cols = pl.ds(lo, n)
        v = dot(sel[...], pad[:, cols])
        x_all[:, cols] = v.astype(BF16)
        x_gain[:, cols] = (v * gain_ref[:, cols]).astype(BF16)
        s2, rl = v * v, v * router_ref[:, cols]
        for a in range(0, n, 128):
            sq = sq + s2[:, a:a + 128]
            lg = lg + rl[:, a:a + 128]
    sq = jnp.sum(sq, axis=1, keepdims=True)
    lg = jnp.sum(lg, axis=1, keepdims=True)
    eye = lax.broadcasted_iota(jnp.int32, (128, 128), 0) == lax.broadcasted_iota(
        jnp.int32, (128, 128), 1
    )
    for i in range(8):
        v = (sq, lg)[i // 4][128 * (i % 4):128 * (i % 4) + 128]
        st_slots[me.t, pl.ds(i, 1)] = jnp.sum(jnp.where(eye, v, 0.0), axis=0, keepdims=True)
    for dy, f in PEERS:
        s = st_slots.at[me.t]
        net.send(("st", dy, f), s, s, me.peer(dy, f))

    gather_s.step(1)
    loads[0].wait()
    for lo, n in FF_TILES:
        v = dot(x_gain[...], wg[:, pl.ds(lo, n)])
        y[0, :, :, pl.ds(lo, n)] = v.astype(BF16).reshape(8, CHUNK, n)
    unit.share(0)
    gather_s.step(2)
    loads[1].wait()
    for lo, n in FF_TILES:
        v = dot(x_gain[...], wu[:, pl.ds(lo, n)])
        y[1, :, :, pl.ds(lo, n)] = v.astype(BF16).reshape(8, CHUNK, n)
    unit.share(1)
    unit.far(0)
    gather_s.step(3)
    unit.far(1)
    sel_t[...] = jnp.where(
        jnp.concatenate([spot[...]] * 4, axis=1)
        == lax.broadcasted_iota(jnp.int32, (SLOTS, ROWS), 1).astype(F32), 1.0, 0.0
    ).astype(BF16)
    gather_s.step(4)
    unit.near(0)
    gather_s.drain()
    flatten(gs)
    for lo, n in COL_TILES:
        cols = pl.ds(lo, n)
        s_all[:, cols] = dot(sel[...], pad[:, cols]).astype(BF16)
    unit.near(1)
    loads[2].wait()
    for lo, n in FF_TILES:
        v = contract_cols(s_all[...], wd[pl.ds(lo, n), :])
        y[2, :, :, pl.ds(lo, n)] = v.astype(BF16).reshape(8, CHUNK, n)
    unit.share(2)
    unit.far(2)

    for dy, f in PEERS:
        back = (NY - dy) % NY
        net.arrive(("st", dy, f), st_slots.at[me.chunk(back, f)], me.peer(back, f))
    stat = st_slots[0]
    for k in range(1, 8):
        stat = stat + st_slots[k]
    sub = lax.broadcasted_iota(jnp.int32, (8, 128), 0)
    lane = lax.broadcasted_iota(jnp.int32, (CHUNK, 128), 1)
    row = lax.broadcasted_iota(jnp.int32, (CHUNK, 128), 0)
    at_own = lane == row + me.core * CHUNK

    def column(which):
        line = jnp.sum(jnp.where(sub == which, stat, 0.0), axis=0, keepdims=True)
        return jnp.sum(jnp.where(at_own, line, 0.0), axis=1, keepdims=True)

    inv_rms = lax.rsqrt(column(me.y) / D + EPS)
    weight = jax.nn.sigmoid(column(4 + me.y))
    unit.near(2)
    for k in range(3):
        unit.settle(k)
    firsts, seconds = [], []
    for i in range(4):
        rows = pl.ds(16 * i, 16)
        inv = inv_rms[16 * i:16 * i + 16]
        w = weight[16 * i:16 * i + 16]
        g_raw, u_raw, d_raw = unit.total(0, rows), unit.total(1, rows), unit.total(2, rows)
        gate, upward = g_raw * inv, u_raw * inv
        sigma = jax.nn.sigmoid(gate)
        act = gate * sigma
        hidden = (act * upward * w).astype(BF16)
        d_hidden = d_raw * (w * inv)
        d_gate = (d_hidden * upward * sigma * (1.0 + gate * (1.0 - sigma))).astype(BF16)
        d_up = (d_hidden * act).astype(BF16)
        h[0, me.t, rows] = hidden
        h[1, me.t, rows] = d_gate
        h[2, me.t, rows] = d_up
        firsts.append(jnp.sum(d_raw * hidden.astype(F32), axis=1, keepdims=True))
        seconds.append(
            jnp.sum(d_gate.astype(F32) * g_raw + d_up.astype(F32) * u_raw, axis=1, keepdims=True)
        )
    for k in range(3):
        unit.spread(k)

    def line_of(parts):
        return jnp.sum(jnp.where(at_own, jnp.concatenate(parts, axis=0), 0.0), axis=0, keepdims=True)

    p_slots[me.t] = jnp.where(sub == me.y, line_of(firsts), 0.0) + jnp.where(
        sub == 4 + me.y, line_of(seconds), 0.0
    )
    for dy, f in PEERS:
        s = p_slots.at[me.t]
        net.send(("p", dy, f), s, s, me.peer(dy, f))

    scatter_b = Scatter("B", net, me, vb, za_b, zb_b, xa_b, xb_b, fin_b, w_b)
    scatter_n = Scatter("N", net, me, vn, za_n, zb_n, xa_n, xb_n, fin_n, w_n)

    def all_rows(k):
        return h[k].reshape(ROWS, FFL)

    def expand(v):
        for g in range(2):
            s = sel_t[pl.ds(384 * g, 384), :]
            parts = [
                dot(s, prod[:, pl.ds(WIDE * i, WIDE)]).reshape(16, CAP, WIDE) for i in range(2)
            ]
            v[pl.ds(16 * g, 16)] = jnp.concatenate(parts, axis=1).astype(BF16)

    unit.relay(0)
    unit.close(0)
    for lo, n in COL_TILES:
        cols = pl.ds(lo, n)
        prod[:, cols] = dot(all_rows(0), wd[:, cols]).astype(BF16)
    unit.relay(1)
    expand(vb)
    scatter_b.start()
    unit.relay(2)
    unit.close(1)
    scatter_b.turn()
    unit.close(2)
    for i, (lo, n) in enumerate(COL_TILES):
        cols = pl.ds(lo, n)
        v = contract_cols(all_rows(1), wg[cols, :]) + contract_cols(all_rows(2), wu[cols, :])
        prod[:, cols] = v.astype(BF16)
        line = jnp.sum(v * x_all[:, cols].astype(F32), axis=0, keepdims=True)
        sx[0, pl.ds(8 + 2 * i, 1)] = line[:, :128]
        sx[0, pl.ds(9 + 2 * i, 1)] = line[:, 128:]
    for dy, f in PEERS:
        back = (NY - dy) % NY
        net.arrive(("p", dy, f), p_slots.at[me.chunk(back, f)], me.peer(back, f))
    p = p_slots[0]
    for k in range(1, 8):
        p = p + p_slots[k]
    sx[0, pl.ds(0, 8)] = p
    for dx in (1, 2, 3):
        net.send(("sx", dx), sx.at[0], sx.at[dx], me.dev(0, dx))
    scatter_b.second()
    expand(vn)
    scatter_n.start()
    scatter_b.third()
    for dx in (1, 2, 3):
        net.arrive(("sx", dx), sx.at[dx], me.dev(0, -dx))
    sz[0] = sx[0] + sx[1] + sx[2] + sx[3]
    for dz in range(1, NZ):
        net.send(("sz", dz), sz.at[0], sz.at[dz], me.dev(dz, 0))

    scatter_n.turn()
    scatter_b.fourth()
    stores = []

    def write(i, src, out):
        store = pltpu.make_async_copy(src, out, local_sems.at[3 + i])
        store.start()
        stores.append(store)

    for lo in range(0, FFL, 128):
        left = h[0, :, :, pl.ds(lo, 128)].reshape(ROWS, 128)
        go[0, pl.ds(lo, 128), :] = contract_rows(left, s_all[...]).astype(BF16)
    write(0, go.at[0, pl.ds(0, FFL)], gd_hbm)
    scatter_n.second()
    for lo in range(0, COLS, 256):
        left = x_gain[:, pl.ds(lo, 256)]
        go[1, pl.ds(lo, 256), pl.ds(0, FFL)] = contract_rows(left, all_rows(1)).astype(BF16)
    write(1, go.at[1, :, pl.ds(0, FFL)], gg_hbm)
    scatter_n.third()
    for lo in range(0, COLS, 256):
        left = x_gain[:, pl.ds(lo, 256)]
        go[2, pl.ds(lo, 256), pl.ds(0, FFL)] = contract_rows(left, all_rows(2)).astype(BF16)
    write(2, go.at[2, :, pl.ds(0, FFL)], gu_hbm)
    branch_a, branch_b = scatter_b.last()
    scatter_n.fourth()

    for dz in range(1, NZ):
        net.arrive(("sz", dz), sz.at[dz], me.dev(-dz, 0))
    tot = sz[0]
    for dz in range(1, NZ):
        tot = tot + sz[dz]
    tot_ref[...] = tot
    d_logit = tot[0:4] * (1.0 - jax.nn.sigmoid(stat[4:8]))
    mean_term = tot[4:8] / D / (stat[0:4] / D + EPS)

    def flat(v):
        return jnp.concatenate([v[i:i + 1] for i in range(4)], axis=1)

    d_logit, mean_term = flat(d_logit), flat(mean_term)
    first = d_logit.astype(BF16)
    rest = d_logit - first.astype(F32)
    second = rest.astype(BF16)
    third = (rest - second.astype(F32)).astype(BF16)
    for lo, n in COL_TILES:
        cols = pl.ds(lo, n)
        x = x_all[:, cols]
        gr_ref[:, cols] = dot(first, x) + dot(second, x) + dot(third, x)
    own = spot[pl.ds(pl.multiple_of(me.c * CAP, 8), CAP), :]
    own = jnp.concatenate([own] * 4, axis=1)
    hit = own == lax.broadcasted_iota(jnp.int32, (CAP, ROWS), 1).astype(F32)
    d_logit = jnp.sum(jnp.where(hit, d_logit, 0.0), axis=1, keepdims=True)
    mean_term = jnp.sum(jnp.where(hit, mean_term, 0.0), axis=1, keepdims=True)

    normed_a, normed_b = scatter_n.last()
    for at, branch, d_normed in ((0, branch_a, normed_a), (HALF, branch_b, normed_b)):
        cols = pl.ds(at, HALF)
        picked = xb_ref[:, cols].astype(F32)
        slope = sb_ref[:, cols].astype(F32)
        mix_ref[:, cols] = picked + branch
        for i in range(2):
            r = slice(CAP * i, CAP * i + CAP)
            feats = pl.ds(WIDE * i + at, HALF)
            gt_ref[pl.ds(CAP * i, CAP), cols] = slope[r] + (
                d_normed[r] * gain_ref[:, feats] - picked[r] * mean_term
                + d_logit * router_ref[:, feats]
            )
    for store in stores:
        store.wait()
    net.finish()


def block(x_block, s_block, gain, router, w_gate, w_up, w_down):
    vm = pl.BlockSpec(memory_space=VMEM)
    hbm = pl.BlockSpec(memory_space=pl.ANY)
    ring = [
        VMEM((2, 2, 4, 2, TALL, HALF), BF16),
        VMEM((2, 4, TALL, HALF), BF16),
        VMEM((4, TALL, HALF), BF16),
        VMEM((8, 4, TALL, HALF), BF16),
        VMEM((2, 2, TALL, HALF), BF16),
        VMEM((TALL, HALF), BF16),
    ]
    return pl.pallas_call(
        block_kernel,
        out_shape=(
            jax.ShapeDtypeStruct((TALL, WIDE), F32),
            jax.ShapeDtypeStruct((TALL, WIDE), F32),
            jax.ShapeDtypeStruct((16, 128), F32),
            jax.ShapeDtypeStruct((1, COLS), F32),
            jax.ShapeDtypeStruct((COLS, FFL), BF16),
            jax.ShapeDtypeStruct((COLS, FFL), BF16),
            jax.ShapeDtypeStruct((FFL, COLS), BF16),
        ),
        in_specs=[vm] * 4 + [hbm] * 3,
        out_specs=(vm,) * 4 + (hbm,) * 3,
        scratch_shapes=[
            VMEM((COLS, FFL), BF16),
            VMEM((COLS, FFL), BF16),
            VMEM((FFL, COLS), BF16),
            VMEM((SHARDS, TALL, WIDE), BF16),
            VMEM((SHARDS, TALL, WIDE), BF16),
            VMEM((SLOTS, COLS), BF16),
            VMEM((SLOTS, SLOTS), BF16),
            VMEM((SLOTS, SLOTS), BF16),
            VMEM((SLOTS, 128), F32),
            VMEM((ROWS, SLOTS), BF16),
            VMEM((SLOTS, ROWS), BF16),
            VMEM((ROWS, COLS), BF16),
            VMEM((ROWS, COLS), BF16),
            VMEM((ROWS, COLS), BF16),
            VMEM((3, 8, CHUNK, FFL), BF16),
            VMEM((3, 8, CHUNK, FFL), BF16),
            VMEM((3, 4, CHUNK, FFL), BF16),
            VMEM((3, 4, CHUNK, FFL), BF16),
            VMEM((3, 2, CHUNK // 2, FFL), BF16),
            VMEM((3, 2, CHUNK, FFL), BF16),
            VMEM((8, 8, 128), F32),
            VMEM((8, 8, 128), F32),
            VMEM((ROWS, COLS), BF16),
            VMEM((SHARDS, TALL, WIDE), BF16),
            VMEM((SHARDS, TALL, WIDE), BF16),
            *ring,
            *ring,
            VMEM((4, 16, 128), F32),
            VMEM((8, 16, 128), F32),
            VMEM((3, COLS, COLS), BF16),
            pltpu.SemaphoreType.DMA((6,)),
            pltpu.SemaphoreType.DMA((SEMS,)),
            pltpu.SemaphoreType.DMA((SEMS,)),
        ],
        compiler_params=pltpu.CompilerParams(
            collective_id=0, has_side_effects=True, vmem_limit_bytes=56 << 20
        ),
        name="block",
    )(x_block, s_block, gain, router, w_gate, w_up, w_down)


def fold(rows):
    return jnp.concatenate([rows[:, :WIDE], rows[:, WIDE:]], axis=0)


def unfold(rows):
    return jnp.concatenate([rows[:CAP], rows[CAP:]], axis=1)


def body(tokens, norm_gain, router, w_gate, w_up, w_down, routes, counts, cotangent):
    usable = (jnp.arange(CAP, dtype=jnp.int32) < counts[0])[:, None]
    local_ids = routes[0]
    picked = jnp.take(tokens, local_ids, axis=0)
    slope = jnp.take(cotangent, local_ids, axis=0)
    mixed_rows, grad_rows, sums, grad_router, grad_gate, grad_up, grad_down = block(
        fold(jnp.where(usable, picked, jnp.asarray(MARK, BF16))),
        fold(slope),
        norm_gain[None, :],
        router.astype(F32)[None, :],
        w_gate,
        w_up,
        w_down,
    )
    mixed_rows = jnp.where(usable, unfold(mixed_rows).astype(BF16), picked)
    grad_rows = jnp.where(usable, unfold(grad_rows).astype(BF16), slope)
    mixed = tokens.at[local_ids].set(mixed_rows)
    grad_tokens = cotangent.at[local_ids].set(grad_rows)
    return (
        mixed, grad_tokens, grad_gate, grad_up, grad_down,
        sums[8:].reshape(COLS), grad_router.reshape(COLS),
    )


def solution(mesh):
    return jax.shard_map(
        body,
        mesh=mesh,
        in_specs=(
            P("context", "tensor"),
            P("tensor"),
            P("tensor"),
            P("tensor", "context"),
            P("tensor", "context"),
            P("context", "tensor"),
            P("context", None),
            P("context"),
            P("context", "tensor"),
        ),
        out_specs=(
            P("context", "tensor"),
            P("context", "tensor"),
            P("tensor", "context"),
            P("tensor", "context"),
            P("context", "tensor"),
            P("tensor"),
            P("tensor"),
        ),
        check_vma=False,
    )
```

```python
import jax
import jax.numpy as jnp
from jax import lax
from jax.experimental import pallas as pl
from jax.experimental.pallas import tpu as pltpu
from jax.sharding import PartitionSpec as P

D = 8192
EPS = 1e-05
NX, NZ, NY = 4, 8, 4
SHARDS = NX * NZ
CAP = 24
SLOTS = SHARDS * CAP
ROWS = 512
CHUNK = 64
FFL = 896
COLS = 1024
TALL, WIDE = 2 * CAP, COLS // 2
SEND_SEMS, RECV_SEMS = 16, 232
MESH = pl.DeviceIdType.MESH
VMEM = pltpu.VMEM
F32 = jnp.float32
BF16 = jnp.bfloat16
FF_TILES = ((0, 256), (256, 256), (512, 256), (768, 128))
COL_TILES = ((0, 256), (256, 256), (512, 256), (768, 256))


def contract_rows(left, right):
    return lax.dot_general(left, right, (((0,), (0,)), ((), ())), preferred_element_type=F32)


def contract_cols(left, right):
    return lax.dot_general(left, right, (((1,), (1,)), ((), ())), preferred_element_type=F32)


def dot(left, right):
    return jnp.dot(left, right, preferred_element_type=F32)


class Net:
    def __init__(self, send_sems, recv_sems, other):
        self.send_sems, self.recv_sems, self.other = send_sems, recv_sems, other
        self.keys, self.groups = {}, {}

    def make(self, key, group, src, dst, device):
        k = self.keys.setdefault(key, len(self.keys))
        g = self.groups.setdefault(group, len(self.groups))
        assert k < RECV_SEMS and g < SEND_SEMS
        return pltpu.make_async_remote_copy(
            src_ref=src,
            dst_ref=dst,
            send_sem=self.send_sems.at[g],
            recv_sem=self.recv_sems.at[k],
            device_id=device,
            device_id_type=MESH,
        )

    def send(self, key, group, src, dst, device):
        self.make(key, group, src, dst, device).start()

    def arrive(self, key, group, ref):
        self.make(key, group, ref, ref, self.other).wait_recv()

    def left(self, key, group, ref):
        self.make(key, group, ref, ref, self.other).wait_send()


def slot_ids(routes_ref, counts_ref):
    row = lax.broadcasted_iota(jnp.int32, (32, 128), 0)
    ids = jnp.full((32, 128), -1, jnp.int32)
    for k in range(CAP):
        ids = jnp.where(row == k, routes_ref[0, k], ids)
    return jnp.where(row < counts_ref[0], ids, -1)


def one_hot(ids):
    lane = lax.broadcasted_iota(jnp.int32, (32, 128), 1)
    return jnp.where(ids == lane, 1.0, 0.0).astype(BF16)


class Place:
    def __init__(self):
        self.c, self.t = lax.axis_index("context"), lax.axis_index("tensor")
        self.z, self.x = lax.div(self.c, NX), lax.rem(self.c, NX)
        self.y, self.core = lax.div(self.t, 2), lax.rem(self.t, 2)
        self.odd = lax.rem(self.x, 2)
        self.pair = lax.div(self.x, 2)

    def at_z(self, dz):
        return lax.rem(self.z + dz + NZ, NZ)

    def at(self, dz, dx):
        return self.at_z(dz) * NX + lax.rem(self.x + dx + NX, NX)

    def dev(self, dz, dx):
        return (self.at(dz, dx), self.t)

    def mate(self, q):
        if q == 1:
            return self.x + 1 - 2 * self.odd
        return lax.rem(self.x + 2, NX) if q == 2 else 3 - self.x

    def mate_at(self, q):
        return self.z * NX + self.mate(q)

    def mate_dev(self, q):
        return (self.mate_at(q), self.t)

    def pair_at(self, dz, other):
        p = 1 - self.pair if other else self.pair
        return pl.ds(self.at_z(dz) * NX + 2 * p, 2)

    def chunk(self, dy, flip=0):
        k = 1 - self.core if flip else self.core
        return lax.rem(self.y + dy + NY, NY) * 2 + k

    def peer(self, dy, flip=0):
        return (self.c, self.chunk(dy, flip))


def flat(v):
    return jnp.concatenate([v[i:i + 1] for i in range(v.shape[0])], axis=1)


PEERS = [(dy, f) for dy in range(NY) for f in (0, 1) if (dy, f) != (0, 0)]


class Paths:
    def __init__(self, tag, net, me, wa):
        self.tag, self.net, self.me = tag, net, me
        self.wa, self.wb = wa, WIDE - wa

    def halves(self, odd):
        cut = 128 if odd else self.wb - 128
        return (0, cut), (cut, self.wb - cut)

    def send(self, key, src, dst, device):
        self.net.send((self.tag,) + key, (self.tag, key[0][0]), src, dst, device)

    def arrive(self, key, ref):
        self.net.arrive((self.tag,) + key, (self.tag, key[0][0]), ref)

    def left(self, ref):
        for part, key, lo, n in (("a", ("a", 2, 0), 0, self.wa), ("b", ("br", 2), self.wa, self.wb)):
            self.net.left((self.tag,) + key, (self.tag, part),
                          ref.at[pl.ds(0, SHARDS - 1), :, pl.ds(lo, n)])

    def longer(self, right, other):
        return right != bool(other)


class Gather(Paths):
    def __init__(self, tag, net, me, wa, g):
        super().__init__(tag, net, me, wa)
        self.g = g

    def part(self, dz, dx, span=None):
        lo, n = span or (0, self.wb)
        return self.g.at[self.me.at(dz, dx), :, pl.ds(self.wa + lo, n)]

    def duo(self, dz, other):
        return self.g.at[self.me.pair_at(dz, other), :, pl.ds(0, self.wa)]

    def pass_on(self, key, ref, device):
        self.send(key, ref, ref, device)

    def a_pass(self, s, other):
        for right, back in ((True, -1), (False, 1)):
            if s < 4 or self.longer(right, other):
                self.pass_on(("a", s, other, right), self.duo(back * (s - 1), other),
                             self.me.dev(-back, 0))

    def a_take(self, s, other):
        for right, back in ((True, -1), (False, 1)):
            if s < 4 or self.longer(right, other):
                self.arrive(("a", s, other, right), self.duo(back * s, other))

    def b_pass(self, s):
        r, l = self.halves(0) if s == 4 else (None, None)
        self.pass_on(("br", s), self.part(1 - s, 0, r), self.me.dev(1, 0))
        self.pass_on(("bl", s), self.part(s - 1, 0, l), self.me.dev(-1, 0))

    def b_take(self, s):
        r, l = self.halves(0) if s == 4 else (None, None)
        self.arrive(("br", s), self.part(-s, 0, r))
        self.arrive(("bl", s), self.part(s, 0, l))

    def b_side(self, o):
        r = self.part(o, 0)
        self.pass_on(("bxr", o), r, self.me.dev(0, 1))
        self.pass_on(("bxl", o), r, self.me.dev(0, -1))

    def b_cross(self, o):
        r, l = self.halves(o % 2)
        self.arrive(("bxr", o), self.part(o, -1))
        self.pass_on(("bd",), self.part(o, -1, r), self.me.dev(0, 1))
        self.arrive(("bxl", o), self.part(o, 1))
        self.pass_on(("bd",), self.part(o, 1, l), self.me.dev(0, -1))

    def start(self):
        own = self.g.at[self.me.c, :, pl.ds(0, self.wa)]
        self.b_pass(1)
        for q in (1, 2, 3):
            self.pass_on(("ax", q), own, self.me.mate_dev(q))
        self.b_side(0)

    def begin_ring(self):
        for q in (1, 2, 3):
            self.arrive(("ax", q), self.g.at[self.me.mate_at(q), :, pl.ds(0, self.wa)])
            if q != 2:
                self.a_pass(1, int(q == 3))

    def step(self, s):
        self.b_take(s)
        if s < 4:
            self.b_pass(s + 1)
            self.b_side(-s)
            self.b_side(s)
        else:
            self.b_side(4)
        for other in (0, 1):
            self.a_take(s, other)
            if s < 4:
                self.a_pass(s + 1, other)
        for o in ((0,) if s == 1 else (1 - s, s - 1)):
            self.b_cross(o)

    def drain(self):
        self.b_cross(4)
        self.arrive(("bd",), self.g.at[pl.ds(0, NZ), :, pl.ds(self.wa, self.wb)])


class Scatter(Paths):
    ORDER = (4, 3, -3, 2, -2, 1, -1, 0)

    def __init__(self, tag, net, me, wa, v, za, zb, xa, xb, fin, w):
        super().__init__(tag, net, me, wa)
        self.v = v
        self.za, self.zb, self.xa, self.xb, self.fin, self.w = za, zb, xa, xb, fin, w

    def mine(self, dz, dx):
        return self.v[self.me.at(dz, dx), :, pl.ds(self.wa, self.wb)].astype(F32)

    def duo(self, dz, other):
        return self.v.at[self.me.pair_at(dz, other), :, pl.ds(0, self.wa)]

    def b_start(self, i):
        o = self.ORDER[i]
        k = self.me.at(o, 2)
        for d, (lo, n) in enumerate(self.halves(o % 2)):
            self.send(("bx1", i, d), self.v.at[k, :, pl.ds(self.wa + lo, n)],
                      self.xb.at[i, d, :, pl.ds(lo, n)], self.me.dev(0, 1 - 2 * d))

    def join(self, ref, term, came, rest):
        (lo, n), (at, m) = came, rest
        cols = pl.ds(lo, n)
        ref[:, cols] = (ref[:, cols].astype(F32) + term[:, lo:lo + n]).astype(BF16)
        ref[:, pl.ds(at, m)] = term[:, at:at + m].astype(BF16)

    def b_next(self, i):
        o = self.ORDER[i]
        spans = self.halves(o % 2)
        for d in range(2):
            lo, n = spans[d]
            self.arrive(("bx1", i, d), self.xb.at[i, d, :, pl.ds(lo, n)])
            self.join(self.xb.at[i, d], self.mine(o, 1 - 2 * d), spans[d], spans[1 - d])
            self.send(("bx2", i, d), self.xb.at[i, d], self.xb.at[i, 2 + d], self.me.dev(0, 1 - 2 * d))

    def b_sum(self, i):
        for d in range(2):
            self.arrive(("bx2", i, d), self.xb.at[i, 2 + d])
        return (self.mine(self.ORDER[i], 0)
                + self.xb[i, 2].astype(F32) + self.xb[i, 3].astype(F32))

    def a_ring(self, s):
        for other in (1, 0):
            for d, right in ((0, True), (1, False)):
                ahead = (1 - 2 * d) * (5 - s)
                first = 1 if self.longer(right, other) else 2
                if s < first:
                    continue
                term = self.duo(ahead, other)
                src = term
                if s > first:
                    src = self.za.at[other, d, s - 2]
                    self.arrive(("a", s - 1, other, d), src)
                    src[...] = (src[...].astype(F32) + term[...].astype(F32)).astype(BF16)
                self.send(("a", s, other, d), src, self.za.at[other, d, s - 1],
                          self.me.dev(1 - 2 * d, 0))

    def a_sum(self, other):
        for d in range(2):
            self.arrive(("a", 4, other, d), self.za.at[other, d, 3])
        return (self.duo(0, other)[...].astype(F32)
                + self.za[other, 0, 3].astype(F32) + self.za[other, 1, 3].astype(F32))

    def b_ring(self, s, right=None, left=None):
        spans = self.halves(0)
        for d, (name, term) in enumerate((("br", right), ("bl", left))):
            lo, n = spans[d]
            if s == 1:
                src, dst = self.w.at[:, pl.ds(lo, n)], self.zb.at[d, 0, :, pl.ds(lo, n)]
            else:
                src, dst = self.zb.at[d, s - 2], self.zb.at[d, s - 1]
                if s == 2:
                    self.arrive((name, 1), self.zb.at[d, 0, :, pl.ds(lo, n)])
                    self.join(src, term, spans[d], spans[1 - d])
                else:
                    self.arrive((name, s - 1), src)
                    src[...] = (src[...].astype(F32) + term).astype(BF16)
            self.send((name, s), src, dst, self.me.dev(1 - 2 * d, 0))

    def start(self):
        for i in range(4):
            self.b_start(i)
        self.a_ring(1)
        for i in range(4, 8):
            self.b_start(i)

    def turn(self):
        for i in range(3):
            self.b_next(i)
        self.a_ring(2)
        for i in range(3, 8):
            self.b_next(i)

    def second(self):
        self.w[...] = self.b_sum(0).astype(BF16)
        self.b_ring(1)
        self.a_ring(3)
        self.b_ring(2, self.b_sum(1), self.b_sum(2))

    def third(self):
        self.a_ring(4)
        self.b_ring(3, self.b_sum(3), self.b_sum(4))

    def fourth(self):
        me, odd = self.me, self.me.odd
        for other in (1, 0):
            self.fin[other] = self.a_sum(other).astype(BF16)
        for q, other, k in ((3, 1, 1 - odd), (2, 1, odd), (1, 0, 1 - odd)):
            self.send(("ax",), self.fin.at[other, k], self.xa.at[q], me.mate_dev(q))
        self.b_ring(4, self.b_sum(5), self.b_sum(6))

    def last(self):
        self.arrive(("ax",), self.xa.at[pl.ds(1, 3)])
        a = self.fin[0, self.me.odd].astype(F32)
        for q in (1, 3, 2):
            a = a + self.xa[q].astype(F32)
        for d, name in enumerate(("br", "bl")):
            self.arrive((name, 4), self.zb.at[d, 3])
        b = self.b_sum(7) + self.zb[0, 3].astype(F32) + self.zb[1, 3].astype(F32)
        return jnp.concatenate([a, b], axis=1)


class Unit:
    def __init__(self, net, me, y, h, r1, acc, rd, rf):
        self.net, self.me, self.y, self.h = net, me, y, h
        self.r1, self.acc, self.rd, self.rf = r1, acc, rd, rf

    def pair(self, k, dy):
        return self.y[k, self.me.chunk(dy)].astype(F32) + self.r1[k, dy].astype(F32)

    def share(self, k):
        for dy in (2, 1, 3, 0):
            key = ("c", k, dy) if dy else ("end",)
            self.net.send(key, "u1", self.y.at[k, self.me.chunk(dy, 1)], self.r1.at[k, dy],
                          self.me.peer(0, 1))

    def far(self, k):
        self.net.arrive(("c", k, 2), "u1", self.r1.at[k, 2])
        self.acc[k, 2] = self.pair(k, 2).astype(BF16)
        for i in range(2):
            self.net.send(("d", k, i), "u1", self.acc.at[k, 2, pl.ds(32 * i, 32)],
                          self.rd.at[k, i], self.me.peer(1 - 2 * i))

    def near(self, k):
        for dy, i in ((1, 0), (3, 1)):
            self.net.arrive(("c", k, dy), "u1", self.r1.at[k, dy])
            v = self.pair(k, dy)
            self.net.arrive(("d", k, i), "u1", self.rd.at[k, i])
            lo = 32 * i
            hi = 32 - lo
            self.acc[k, dy, pl.ds(lo, 32)] = (
                v[lo:lo + 32] + self.rd[k, i].astype(F32)
            ).astype(BF16)
            self.acc[k, dy, pl.ds(hi, 32)] = v[hi:hi + 32].astype(BF16)
            self.net.send(("end",), "u1", self.acc.at[k, dy], self.rf.at[k, i],
                          self.me.peer(1 - 2 * i))

    def settle(self):
        self.net.arrive(("end",), "u1", self.y.at[:, pl.ds(0, 3)])
        self.net.left(("end",), "u1", self.y.at[:, pl.ds(0, 7)])

    def total(self, k, rows):
        return (
            self.y[k, self.me.t, rows].astype(F32)
            + self.r1[k, 0, rows].astype(F32)
            + self.rf[k, 0, rows].astype(F32)
            + self.rf[k, 1, rows].astype(F32)
        )

    def spread(self, k):
        own = self.h.at[k, self.me.t]
        self.net.send(("gr", k), "u2", own, own, self.me.peer(1))
        self.net.send(("gl", k), "u2", own, own, self.me.peer(-1))
        self.net.send(("g", k), "u2", own, own, self.me.peer(0, 1))

    def relay(self, k):
        me = self.me
        for key, dy, lo in (("gr", -1, 0), ("gl", 1, 32)):
            ref = self.h.at[k, me.chunk(dy)]
            self.net.arrive((key, k), "u2", ref)
            half = self.h.at[k, me.chunk(dy), pl.ds(lo, 32)]
            self.net.send(("e", k), "u2", half, half, me.peer(-dy))
            self.net.send(("g", k), "u2", ref, ref, me.peer(0, 1))

    def close(self, k):
        me = self.me
        ref = self.h.at[k, me.chunk(2)]
        self.net.arrive(("e", k), "u2", ref)
        self.net.send(("g", k), "u2", ref, ref, me.peer(0, 1))
        self.net.arrive(("g", k), "u2", self.h.at[k, pl.ds(0, 4)])


def block_kernel(
    routes_ref, counts_ref, tok_ref, cot_ref, gain_ref, router_ref, wg_hbm, wu_hbm, wd_hbm,
    mix_ref, gt_ref, gain_out, router_out, gg_hbm, gu_hbm, gd_hbm,
    wg, wu, wd, gx, gs, pad, spot, sel, sel_t, x_all, x_gain, s_all,
    y, h, r1, acc, rd, rf, st_slots, p_slots, prod, vb, vn,
    za_b, zb_b, xa_b, xb_b, fin_b, w_b, za_n, zb_n, xa_n, xb_n, fin_n, w_n,
    cx, cz, sx, sz, go, local_sems, send_sems, recv_sems,
):
    me = Place()
    net = Net(send_sems, recv_sems, me.peer(0, 1))
    barrier = pltpu.get_barrier_semaphore()
    friends = (
        [me.dev(dz, 0) for dz in range(1, NZ)]
        + [me.dev(0, dx) for dx in range(1, NX)]
        + [me.peer(dy, f) for dy, f in PEERS]
    )
    for device in friends:
        pl.semaphore_signal(barrier, inc=1, device_id=device, device_id_type=MESH)
    loads = [
        pltpu.make_async_copy(src, dst, local_sems.at[i])
        for i, (src, dst) in enumerate(((wg_hbm, wg), (wu_hbm, wu), (wd_hbm, wd)))
    ]
    for load in loads:
        load.start()
    hot = one_hot(slot_ids(routes_ref, counts_ref))
    for src, dst in ((tok_ref, gx), (cot_ref, gs)):
        rows = dot(hot, src[...])[:CAP]
        dst[me.c] = jnp.concatenate([rows[:, :WIDE], rows[:, WIDE:]], axis=0).astype(BF16)
    lane8 = lax.broadcasted_iota(jnp.int32, (8, 128), 1)
    cx[0] = jnp.where(lane8 == me.c, counts_ref[0].astype(F32), 0.0)
    pl.semaphore_wait(barrier, len(friends))

    gather_x = Gather("X", net, me, 128, gx)
    gather_s = Gather("S", net, me, 256, gs)
    unit = Unit(net, me, y, h, r1, acc, rd, rf)

    gather_x.start()
    for dx in (1, 2, 3):
        net.send(("cx",), "cx", cx.at[0], cx.at[dx], me.dev(0, dx))
    gather_x.begin_ring()
    net.arrive(("cx",), "cx", cx.at[pl.ds(1, 3)])
    cz[0] = cx[0] + cx[1] + cx[2] + cx[3]
    for dz in range(1, NZ):
        net.send(("cz",), "cz", cz.at[0], cz.at[dz], me.dev(dz, 0))
    gather_x.step(1)
    gather_s.start()
    gather_x.step(2)
    gather_s.begin_ring()
    net.arrive(("cz",), "cz", cz.at[pl.ds(1, NZ - 1)])
    held = cz[0]
    for dz in range(1, NZ):
        held = held + cz[dz]

    def place_of(shard, slot, combine):
        ahead = jnp.where(slot >= CAP * shard + CAP, 1.0, 0.0)
        inside = jnp.where(slot >= CAP * shard, 1.0 - ahead, 0.0)
        ahead, inside = ahead.astype(BF16), inside.astype(BF16)
        count, offset, shards = combine(inside, ahead)
        k = (slot[:1] if slot.shape[1] == SLOTS else slot).astype(F32) - CAP * shards
        return jnp.where(k < count, offset + k, -1.0)

    def as_row(inside, ahead):
        c = held.astype(BF16)
        one = jnp.ones((8, 128), BF16)
        return dot(c, inside)[0:1], dot(c, ahead)[0:1], dot(one, ahead)[0:1]

    line = place_of(
        lax.broadcasted_iota(jnp.int32, (128, SLOTS), 0),
        lax.broadcasted_iota(jnp.int32, (128, SLOTS), 1),
        as_row,
    )
    sel[...] = jnp.where(
        line == lax.broadcasted_iota(jnp.int32, (ROWS, SLOTS), 0).astype(F32), 1.0, 0.0
    ).astype(BF16)
    gather_x.step(3)
    eye = lax.broadcasted_iota(jnp.int32, (128, 128), 0) == lax.broadcasted_iota(
        jnp.int32, (128, 128), 1
    )

    def as_column(inside, ahead):
        c = jnp.sum(jnp.where(eye, held[0:1], 0.0), axis=1, keepdims=True)
        c = jnp.broadcast_to(c, (128, 128)).astype(BF16)
        one = jnp.ones((128, 128), BF16)
        return dot(inside, c), dot(ahead, c), dot(ahead, one)

    spot[...] = place_of(
        lax.broadcasted_iota(jnp.int32, (SLOTS, 128), 1),
        lax.broadcasted_iota(jnp.int32, (SLOTS, 128), 0),
        as_column,
    )
    sel_t[...] = jnp.where(
        jnp.concatenate([spot[...]] * 4, axis=1)
        == lax.broadcasted_iota(jnp.int32, (SLOTS, ROWS), 1).astype(F32), 1.0, 0.0
    ).astype(BF16)
    gather_x.step(4)
    gather_s.step(1)
    gather_x.drain()

    def flatten(g):
        @pl.loop(0, NZ)
        def _(i):
            v = g[pl.ds(NX * i, NX)].astype(F32)
            rows = pl.ds(pl.multiple_of(i * (NX * CAP), 32), NX * CAP)
            pad[rows, pl.ds(0, WIDE)] = v[:, :CAP].reshape(NX * CAP, WIDE).astype(BF16)
            pad[rows, pl.ds(WIDE, WIDE)] = v[:, CAP:].reshape(NX * CAP, WIDE).astype(BF16)

    flatten(gx)
    for lo, n in COL_TILES:
        cols = pl.ds(lo, n)
        v = dot(sel[...], pad[:, cols])
        x_all[:, cols] = v.astype(BF16)
        x_gain[:, cols] = (v * gain_ref[:, cols]).astype(BF16)
    loads[0].wait()
    for lo, n in FF_TILES:
        v = dot(x_gain[...], wg[:, pl.ds(lo, n)])
        y[0, :, :, pl.ds(lo, n)] = v.astype(BF16).reshape(8, CHUNK, n)
    unit.share(0)
    gather_s.step(2)
    loads[1].wait()
    for lo, n in FF_TILES:
        v = dot(x_gain[...], wu[:, pl.ds(lo, n)])
        y[1, :, :, pl.ds(lo, n)] = v.astype(BF16).reshape(8, CHUNK, n)
    unit.share(1)
    unit.far(0)
    gather_s.step(3)
    unit.far(1)
    unit.near(0)
    router = flat(router_ref[...].astype(F32))
    sq = jnp.zeros((ROWS, 128), F32)
    lg = jnp.zeros((ROWS, 128), F32)
    for lo in range(0, COLS, 128):
        v = x_all[:, pl.ds(lo, 128)].astype(F32)
        sq = sq + v * v
        lg = lg + v * router[:, lo:lo + 128]
    sq = jnp.sum(sq, axis=1, keepdims=True)
    lg = jnp.sum(lg, axis=1, keepdims=True)
    for i in range(8):
        v = (sq, lg)[i // 4][128 * (i % 4):128 * (i % 4) + 128]
        st_slots[me.t, pl.ds(i, 1)] = jnp.sum(jnp.where(eye, v, 0.0), axis=0, keepdims=True)
    for dy, f in PEERS:
        ref = st_slots.at[me.t]
        net.send(("st",), "st", ref, ref, me.peer(dy, f))
    gather_s.step(4)
    unit.near(1)
    gather_s.drain()
    flatten(gs)
    for lo, n in COL_TILES:
        cols = pl.ds(lo, n)
        s_all[:, cols] = dot(sel[...], pad[:, cols]).astype(BF16)
    loads[2].wait()
    for lo, n in FF_TILES:
        v = contract_cols(s_all[...], wd[pl.ds(lo, n), :])
        y[2, :, :, pl.ds(lo, n)] = v.astype(BF16).reshape(8, CHUNK, n)
    unit.share(2)
    unit.far(2)

    net.arrive(("st",), "st", st_slots.at[pl.ds(0, 7)])
    stat = st_slots[0]
    for k in range(1, 8):
        stat = stat + st_slots[k]
    sub = lax.broadcasted_iota(jnp.int32, (8, 128), 0)
    lane = lax.broadcasted_iota(jnp.int32, (CHUNK, 128), 1)
    row = lax.broadcasted_iota(jnp.int32, (CHUNK, 128), 0)
    at_own = lane == row + me.core * CHUNK

    def column(which):
        line = jnp.sum(jnp.where(sub == which, stat, 0.0), axis=0, keepdims=True)
        return jnp.sum(jnp.where(at_own, line, 0.0), axis=1, keepdims=True)

    inv_rms = lax.rsqrt(column(me.y) / D + EPS)
    weight = jax.nn.sigmoid(column(4 + me.y))
    unit.near(2)
    unit.settle()
    firsts, seconds = [], []
    for i in range(4):
        rows = pl.ds(16 * i, 16)
        inv = inv_rms[16 * i:16 * i + 16]
        w = weight[16 * i:16 * i + 16]
        g_raw, u_raw, d_raw = unit.total(0, rows), unit.total(1, rows), unit.total(2, rows)
        gate, upward = g_raw * inv, u_raw * inv
        sigma = jax.nn.sigmoid(gate)
        act = gate * sigma
        hidden = (act * upward * w).astype(BF16)
        d_hidden = d_raw * (w * inv)
        d_gate = (d_hidden * upward * sigma * (1.0 + gate * (1.0 - sigma))).astype(BF16)
        d_up = (d_hidden * act).astype(BF16)
        h[0, me.t, rows] = hidden
        h[1, me.t, rows] = d_gate
        h[2, me.t, rows] = d_up
        firsts.append(jnp.sum(d_raw * hidden.astype(F32), axis=1, keepdims=True))
        seconds.append(
            jnp.sum(d_gate.astype(F32) * g_raw + d_up.astype(F32) * u_raw, axis=1, keepdims=True)
        )
    for k in range(3):
        unit.spread(k)

    def line_of(parts):
        return jnp.sum(jnp.where(at_own, jnp.concatenate(parts, axis=0), 0.0), axis=0, keepdims=True)

    p_slots[me.t] = jnp.where(sub == me.y, line_of(firsts), 0.0) + jnp.where(
        sub == 4 + me.y, line_of(seconds), 0.0
    )
    for dy, f in PEERS:
        ref = p_slots.at[me.t]
        net.send(("p",), "p", ref, ref, me.peer(dy, f))

    scatter_b = Scatter("B", net, me, 256, vb, za_b, zb_b, xa_b, xb_b, fin_b, w_b)
    scatter_n = Scatter("N", net, me, 128, vn, za_n, zb_n, xa_n, xb_n, fin_n, w_n)

    def all_rows(k):
        return h[k].reshape(ROWS, FFL)

    def expand(v):
        for g in range(2):
            s = sel_t[pl.ds(384 * g, 384), :]
            parts = [
                dot(s, prod[:, pl.ds(WIDE * i, WIDE)]).reshape(16, CAP, WIDE) for i in range(2)
            ]
            v[pl.ds(16 * g, 16)] = jnp.concatenate(parts, axis=1).astype(BF16)

    unit.relay(0)
    unit.close(0)
    for lo, n in COL_TILES:
        cols = pl.ds(lo, n)
        prod[:, cols] = dot(all_rows(0), wd[:, cols]).astype(BF16)
    unit.relay(1)
    expand(vb)
    scatter_b.start()
    unit.relay(2)
    unit.close(1)
    scatter_b.turn()
    unit.close(2)
    for i, (lo, n) in enumerate(COL_TILES):
        cols = pl.ds(lo, n)
        v = contract_cols(all_rows(1), wg[cols, :]) + contract_cols(all_rows(2), wu[cols, :])
        prod[:, cols] = v.astype(BF16)
        line = jnp.sum(v * x_all[:, cols].astype(F32), axis=0, keepdims=True)
        sx[0, pl.ds(8 + 2 * i, 1)] = line[:, :128]
        sx[0, pl.ds(9 + 2 * i, 1)] = line[:, 128:]
    net.arrive(("p",), "p", p_slots.at[pl.ds(0, 7)])
    p = p_slots[0]
    for k in range(1, 8):
        p = p + p_slots[k]
    sx[0, pl.ds(0, 8)] = p
    for dx in (1, 2, 3):
        net.send(("sx",), "sx", sx.at[0], sx.at[dx], me.dev(0, dx))
    scatter_b.second()
    expand(vn)
    scatter_n.start()
    scatter_b.third()
    net.arrive(("sx",), "sx", sx.at[pl.ds(1, 3)])
    sz[0] = sx[0] + sx[1] + sx[2] + sx[3]
    for dz in range(1, NZ):
        net.send(("sz",), "sz", sz.at[0], sz.at[dz], me.dev(dz, 0))

    scatter_n.turn()
    scatter_b.fourth()
    stores = []

    def write(i, src, out):
        store = pltpu.make_async_copy(src, out, local_sems.at[3 + i])
        store.start()
        stores.append(store)

    for lo in range(0, FFL, 128):
        left = h[0, :, :, pl.ds(lo, 128)].reshape(ROWS, 128)
        go[0, pl.ds(lo, 128), :] = contract_rows(left, s_all[...]).astype(BF16)
    write(0, go.at[0, pl.ds(0, FFL)], gd_hbm)
    scatter_n.second()
    for lo in range(0, COLS, 256):
        left = x_gain[:, pl.ds(lo, 256)]
        go[1, pl.ds(lo, 256), pl.ds(0, FFL)] = contract_rows(left, all_rows(1)).astype(BF16)
    write(1, go.at[1, :, pl.ds(0, FFL)], gg_hbm)
    scatter_n.third()
    for lo in range(0, COLS, 256):
        left = x_gain[:, pl.ds(lo, 256)]
        go[2, pl.ds(lo, 256), pl.ds(0, FFL)] = contract_rows(left, all_rows(2)).astype(BF16)
    write(2, go.at[2, :, pl.ds(0, FFL)], gu_hbm)
    branch = scatter_b.last()
    scatter_n.fourth()

    net.arrive(("sz",), "sz", sz.at[pl.ds(1, NZ - 1)])
    tot = sz[0]
    for dz in range(1, NZ):
        tot = tot + sz[dz]
    d_logit = tot[0:4] * (1.0 - jax.nn.sigmoid(stat[4:8]))
    mean_term = tot[4:8] / D / (stat[0:4] / D + EPS)

    d_logit, mean_term = flat(d_logit), flat(mean_term)
    first = d_logit.astype(BF16)
    rest = d_logit - first.astype(F32)
    second = rest.astype(BF16)
    third = (rest - second.astype(F32)).astype(BF16)
    for lo, n in COL_TILES:
        cols = pl.ds(lo, n)
        x = x_all[:, cols]
        line = dot(first, x) + dot(second, x) + dot(third, x)
        for k in range(0, n, 128):
            router_out[pl.ds((lo + k) // 128, 1)] = line[:, k:k + 128]
    gain_out[...] = tot[8:16]
    own = spot[pl.ds(pl.multiple_of(me.c * CAP, 8), CAP), :]
    own = jnp.concatenate([own] * 4, axis=1)
    hit = own == lax.broadcasted_iota(jnp.int32, (CAP, ROWS), 1).astype(F32)
    d_logit = jnp.sum(jnp.where(hit, d_logit, 0.0), axis=1, keepdims=True)
    mean_term = jnp.sum(jnp.where(hit, mean_term, 0.0), axis=1, keepdims=True)

    d_normed = scatter_n.last()
    picked, slope = gx[me.c].astype(F32), gs[me.c].astype(F32)
    mix_ref[...] = picked + branch
    for i in range(2):
        r = slice(CAP * i, CAP * i + CAP)
        feats = slice(WIDE * i, WIDE * i + WIDE)
        gt_ref[pl.ds(CAP * i, CAP), :] = slope[r] + (
            d_normed[r] * gain_ref[:, pl.ds(WIDE * i, WIDE)] - picked[r] * mean_term
            + d_logit * router[:, feats]
        )
    for store in stores:
        store.wait()
    for paths, ref in ((gather_x, gx), (gather_s, gs), (scatter_b, vb), (scatter_n, vn)):
        paths.left(ref)
    net.left(("g", 0), "u2", h.at[:, pl.ds(0, 7)])
    for name, ref, n in (
        ("cx", cx, 3), ("cz", cz, 7), ("sx", sx, 3), ("sz", sz, 7), ("st", st_slots, 7), ("p", p_slots, 7)
    ):
        net.left((name,), name, ref.at[pl.ds(0, n)])


def block(routes, counts, tokens, cotangent, gain, router, w_gate, w_up, w_down):
    vm = pl.BlockSpec(memory_space=VMEM)
    sm = pl.BlockSpec(memory_space=pltpu.SMEM)
    hbm = pl.BlockSpec(memory_space=pl.ANY)
    ring_b, ring_n = (
        [
            VMEM((2, 2, 4, 2, TALL, wa), BF16),
            VMEM((2, 4, TALL, WIDE - wa), BF16),
            VMEM((4, TALL, wa), BF16),
            VMEM((8, 4, TALL, WIDE - wa), BF16),
            VMEM((2, 2, TALL, wa), BF16),
            VMEM((TALL, WIDE - wa), BF16),
        ]
        for wa in (256, 128)
    )
    return pl.pallas_call(
        block_kernel,
        out_shape=(
            jax.ShapeDtypeStruct((TALL, WIDE), F32),
            jax.ShapeDtypeStruct((TALL, WIDE), F32),
            jax.ShapeDtypeStruct((8, 128), F32),
            jax.ShapeDtypeStruct((8, 128), F32),
            jax.ShapeDtypeStruct((COLS, FFL), BF16),
            jax.ShapeDtypeStruct((COLS, FFL), BF16),
            jax.ShapeDtypeStruct((FFL, COLS), BF16),
        ),
        in_specs=[sm] * 2 + [vm] * 4 + [hbm] * 3,
        out_specs=(vm,) * 4 + (hbm,) * 3,
        scratch_shapes=[
            VMEM((COLS, FFL), BF16),
            VMEM((COLS, FFL), BF16),
            VMEM((FFL, COLS), BF16),
            VMEM((SHARDS, TALL, WIDE), BF16),
            VMEM((SHARDS, TALL, WIDE), BF16),
            VMEM((SLOTS, COLS), BF16),
            VMEM((SLOTS, 128), F32),
            VMEM((ROWS, SLOTS), BF16),
            VMEM((SLOTS, ROWS), BF16),
            VMEM((ROWS, COLS), BF16),
            VMEM((ROWS, COLS), BF16),
            VMEM((ROWS, COLS), BF16),
            VMEM((3, 8, CHUNK, FFL), BF16),
            VMEM((3, 8, CHUNK, FFL), BF16),
            VMEM((3, 4, CHUNK, FFL), BF16),
            VMEM((3, 4, CHUNK, FFL), BF16),
            VMEM((3, 2, CHUNK // 2, FFL), BF16),
            VMEM((3, 2, CHUNK, FFL), BF16),
            VMEM((8, 8, 128), F32),
            VMEM((8, 8, 128), F32),
            VMEM((ROWS, COLS), BF16),
            VMEM((SHARDS, TALL, WIDE), BF16),
            VMEM((SHARDS, TALL, WIDE), BF16),
            *ring_b,
            *ring_n,
            VMEM((4, 8, 128), F32),
            VMEM((8, 8, 128), F32),
            VMEM((4, 16, 128), F32),
            VMEM((8, 16, 128), F32),
            VMEM((3, COLS, COLS), BF16),
            pltpu.SemaphoreType.DMA((6,)),
            pltpu.SemaphoreType.DMA((SEND_SEMS,)),
            pltpu.SemaphoreType.DMA((RECV_SEMS,)),
        ],
        compiler_params=pltpu.CompilerParams(
            collective_id=0, has_side_effects=True, vmem_limit_bytes=56 << 20
        ),
        name="block",
    )(routes, counts, tokens, cotangent, gain, router, w_gate, w_up, w_down)


def merge_kernel(
    routes_ref, counts_ref, tok_ref, cot_ref, mix_ref, gt_ref, gain_ref, router_ref, a_hbm, b_hbm, c_hbm,
    mixed_ref, grad_ref, gain_out, router_out, a_out, b_out, c_out,
    a, b, c, sems,
):
    n = 2
    ways = []
    for i, (src, held, dst) in enumerate(((a_hbm, a, a_out), (b_hbm, b, b_out), (c_hbm, c, c_out))):
        rows = src.shape[0] // n
        for j in range(n):
            part = pl.ds(rows * j, rows)
            k = i * n + j
            ways.append((
                pltpu.make_async_copy(src.at[part], held.at[part], sems.at[0, k]),
                pltpu.make_async_copy(held.at[part], dst.at[part], sems.at[1, k]),
            ))
    for come, _ in ways:
        come.start()
    gain_out[...] = gain_ref[...]
    router_out[...] = router_ref[...]
    hot = one_hot(slot_ids(routes_ref, counts_ref))
    picked = contract_rows(hot, jnp.ones((32, 128), BF16))[:, 0:1] > 0.5
    blank = jnp.zeros((32 - CAP, COLS), F32)
    for come, go in ways[:2]:
        come.wait()
        go.start()
    for old, new, out in ((tok_ref, mix_ref, mixed_ref), (cot_ref, gt_ref, grad_ref)):
        rows = jnp.concatenate([new[pl.ds(0, CAP), :], new[pl.ds(CAP, CAP), :]], axis=1)
        rows = jnp.concatenate([rows, blank], axis=0).astype(BF16)
        out[...] = jnp.where(picked, contract_rows(hot, rows), old[...].astype(F32)).astype(BF16)
    for come, go in ways[2:]:
        come.wait()
        go.start()
    for _, go in ways:
        go.wait()


def merge(routes, counts, tokens, cotangent, mixed_rows, grad_rows, gain, router, *grads):
    vm = pl.BlockSpec(memory_space=VMEM)
    sm = pl.BlockSpec(memory_space=pltpu.SMEM)
    hbm = pl.BlockSpec(memory_space=pl.ANY)
    same = [
        jax.ShapeDtypeStruct(v.shape, v.dtype) for v in (tokens, cotangent, gain, router) + grads
    ]
    return pl.pallas_call(
        merge_kernel,
        out_shape=same,
        in_specs=[sm] * 2 + [vm] * 6 + [hbm] * 3,
        out_specs=[vm] * 4 + [hbm] * 3,
        scratch_shapes=[VMEM(v.shape, v.dtype) for v in grads] + [pltpu.SemaphoreType.DMA((2, 6))],
        compiler_params=pltpu.CompilerParams(vmem_limit_bytes=60 << 20),
        name="merge",
    )(routes, counts, tokens, cotangent, mixed_rows, grad_rows, gain, router, *grads)


def body(tokens, norm_gain, router, w_gate, w_up, w_down, routes, counts, cotangent):
    new = block(
        routes, counts, tokens, cotangent, norm_gain[None, :], router.reshape(8, 128),
        w_gate, w_up, w_down,
    )
    mixed, grad_tokens, gain, router, *grads = merge(routes, counts, tokens, cotangent, *new)
    return (mixed, grad_tokens, *grads, gain.reshape(COLS), router.reshape(COLS))


def solution(mesh):
    return jax.shard_map(
        body,
        mesh=mesh,
        in_specs=(
            P("context", "tensor"),
            P("tensor"),
            P("tensor"),
            P("tensor", "context"),
            P("tensor", "context"),
            P("context", "tensor"),
            P("context", None),
            P("context"),
            P("context", "tensor"),
        ),
        out_specs=(
            P("context", "tensor"),
            P("context", "tensor"),
            P("tensor", "context"),
            P("tensor", "context"),
            P("context", "tensor"),
            P("tensor"),
            P("tensor"),
        ),
        check_vma=False,
    )
```

```python
import jax
import jax.numpy as jnp
from jax import lax
from jax.experimental import pallas as pl
from jax.experimental.pallas import tpu as pltpu
from jax.sharding import PartitionSpec as P

D = 8192
EPS = 1e-05
NX, NZ, NY = 4, 8, 4
SHARDS = NX * NZ
CAP = 24
SLOTS = SHARDS * CAP
ROWS = 512
CHUNK = 64
FFL = 896
COLS = 1024
TALL, WIDE = 2 * CAP, COLS // 2
SEND_SEMS, RECV_SEMS = 16, 236
MESH = pl.DeviceIdType.MESH
VMEM = pltpu.VMEM
F32 = jnp.float32
BF16 = jnp.bfloat16
FF_TILES = ((0, 256), (256, 256), (512, 256), (768, 128))
COL_TILES = ((0, 256), (256, 256), (512, 256), (768, 256))


def contract_rows(left, right):
    return lax.dot_general(left, right, (((0,), (0,)), ((), ())), preferred_element_type=F32)


def contract_cols(left, right):
    return lax.dot_general(left, right, (((1,), (1,)), ((), ())), preferred_element_type=F32)


def dot(left, right):
    return jnp.dot(left, right, preferred_element_type=F32)


class Net:
    def __init__(self, send_sems, recv_sems, other):
        self.send_sems, self.recv_sems, self.other = send_sems, recv_sems, other
        self.keys, self.groups = {}, {}

    def make(self, key, group, src, dst, device):
        k = self.keys.setdefault(key, len(self.keys))
        g = self.groups.setdefault(group, len(self.groups))
        assert k < RECV_SEMS and g < SEND_SEMS
        return pltpu.make_async_remote_copy(
            src_ref=src,
            dst_ref=dst,
            send_sem=self.send_sems.at[g],
            recv_sem=self.recv_sems.at[k],
            device_id=device,
            device_id_type=MESH,
        )

    def send(self, key, group, src, dst, device):
        self.make(key, group, src, dst, device).start()

    def arrive(self, key, group, ref):
        self.make(key, group, ref, ref, self.other).wait_recv()

    def left(self, key, group, ref):
        self.make(key, group, ref, ref, self.other).wait_send()


def slot_ids(routes_ref, counts_ref):
    row = lax.broadcasted_iota(jnp.int32, (32, 128), 0)
    ids = jnp.full((32, 128), -1, jnp.int32)
    for k in range(CAP):
        ids = jnp.where(row == k, routes_ref[0, k], ids)
    return jnp.where(row < counts_ref[0], ids, -1)


def one_hot(ids):
    lane = lax.broadcasted_iota(jnp.int32, (32, 128), 1)
    return jnp.where(ids == lane, 1.0, 0.0).astype(BF16)


class Place:
    def __init__(self):
        self.c, self.t = lax.axis_index("context"), lax.axis_index("tensor")
        self.z, self.x = lax.div(self.c, NX), lax.rem(self.c, NX)
        self.y, self.core = lax.div(self.t, 2), lax.rem(self.t, 2)
        self.odd = lax.rem(self.x, 2)
        self.pair = lax.div(self.x, 2)

    def at_z(self, dz):
        return lax.rem(self.z + dz + NZ, NZ)

    def at(self, dz, dx):
        return self.at_z(dz) * NX + lax.rem(self.x + dx + NX, NX)

    def dev(self, dz, dx):
        return (self.at(dz, dx), self.t)

    def mate(self, q):
        if q == 1:
            return self.x + 1 - 2 * self.odd
        return lax.rem(self.x + 2, NX) if q == 2 else 3 - self.x

    def mate_at(self, q):
        return self.z * NX + self.mate(q)

    def mate_dev(self, q):
        return (self.mate_at(q), self.t)

    def pair_at(self, dz, other):
        p = 1 - self.pair if other else self.pair
        return pl.ds(self.at_z(dz) * NX + 2 * p, 2)

    def chunk(self, dy, flip=0):
        k = 1 - self.core if flip else self.core
        return lax.rem(self.y + dy + NY, NY) * 2 + k

    def peer(self, dy, flip=0):
        return (self.c, self.chunk(dy, flip))


def flat(v):
    return jnp.concatenate([v[i:i + 1] for i in range(v.shape[0])], axis=1)


PEERS = [(dy, f) for dy in range(NY) for f in (0, 1) if (dy, f) != (0, 0)]


class Paths:
    def __init__(self, tag, net, me, wa):
        self.tag, self.net, self.me = tag, net, me
        self.wa, self.wb = wa, WIDE - wa

    def halves(self, odd):
        cut = 128 if odd else self.wb - 128
        return (0, cut), (cut, self.wb - cut)

    def send(self, key, src, dst, device):
        self.net.send((self.tag,) + key, (self.tag, key[0][0]), src, dst, device)

    def arrive(self, key, ref):
        self.net.arrive((self.tag,) + key, (self.tag, key[0][0]), ref)

    def left(self, ref):
        for part, key, lo, n in (("a", ("a", 2, 0), 0, self.wa), ("b", ("br", 2), self.wa, self.wb)):
            self.net.left((self.tag,) + key, (self.tag, part),
                          ref.at[pl.ds(0, SHARDS - 1), :, pl.ds(lo, n)])

    def longer(self, right, other):
        return right != bool(other)


class Gather(Paths):
    def __init__(self, tag, net, me, wa, g):
        super().__init__(tag, net, me, wa)
        self.g = g

    def part(self, dz, dx, span=None):
        lo, n = span or (0, self.wb)
        return self.g.at[self.me.at(dz, dx), :, pl.ds(self.wa + lo, n)]

    def duo(self, dz, other):
        return self.g.at[self.me.pair_at(dz, other), :, pl.ds(0, self.wa)]

    def pass_on(self, key, ref, device):
        self.send(key, ref, ref, device)

    def a_pass(self, s, other):
        for right, back in ((True, -1), (False, 1)):
            if s < 4 or self.longer(right, other):
                self.pass_on(("a", s, other, right), self.duo(back * (s - 1), other),
                             self.me.dev(-back, 0))

    def a_take(self, s, other):
        for right, back in ((True, -1), (False, 1)):
            if s < 4 or self.longer(right, other):
                self.arrive(("a", s, other, right), self.duo(back * s, other))

    def b_pass(self, s):
        r, l = self.halves(0) if s == 4 else (None, None)
        self.pass_on(("br", s), self.part(1 - s, 0, r), self.me.dev(1, 0))
        self.pass_on(("bl", s), self.part(s - 1, 0, l), self.me.dev(-1, 0))

    def b_take(self, s):
        r, l = self.halves(0) if s == 4 else (None, None)
        self.arrive(("br", s), self.part(-s, 0, r))
        self.arrive(("bl", s), self.part(s, 0, l))

    def b_side(self, o):
        r = self.part(o, 0)
        self.pass_on(("bxr", o), r, self.me.dev(0, 1))
        self.pass_on(("bxl", o), r, self.me.dev(0, -1))

    def b_cross(self, o):
        r, l = self.halves(o % 2)
        self.arrive(("bxr", o), self.part(o, -1))
        self.pass_on(("bd",), self.part(o, -1, r), self.me.dev(0, 1))
        self.arrive(("bxl", o), self.part(o, 1))
        self.pass_on(("bd",), self.part(o, 1, l), self.me.dev(0, -1))

    def start(self):
        own = self.g.at[self.me.c, :, pl.ds(0, self.wa)]
        self.b_pass(1)
        for q in (1, 2, 3):
            self.pass_on(("ax", q), own, self.me.mate_dev(q))
        self.b_side(0)

    def begin_ring(self):
        for q in (1, 2, 3):
            self.arrive(("ax", q), self.g.at[self.me.mate_at(q), :, pl.ds(0, self.wa)])
            if q != 2:
                self.a_pass(1, int(q == 3))

    def step(self, s):
        self.b_take(s)
        if s < 4:
            self.b_pass(s + 1)
            self.b_side(-s)
            self.b_side(s)
        else:
            self.b_side(4)
        for other in (0, 1):
            self.a_take(s, other)
            if s < 4:
                self.a_pass(s + 1, other)
        for o in ((0,) if s == 1 else (1 - s, s - 1)):
            self.b_cross(o)

    def drain(self):
        self.b_cross(4)
        self.arrive(("bd",), self.g.at[pl.ds(0, NZ), :, pl.ds(self.wa, self.wb)])


class Scatter(Paths):
    ORDER = (4, 3, -3, 2, -2, 1, -1, 0)

    def __init__(self, tag, net, me, wa, v, za, zb, xa, xb, fin, w):
        super().__init__(tag, net, me, wa)
        self.v = v
        self.za, self.zb, self.xa, self.xb, self.fin, self.w = za, zb, xa, xb, fin, w

    def mine(self, dz, dx):
        return self.v[self.me.at(dz, dx), :, pl.ds(self.wa, self.wb)].astype(F32)

    def duo(self, dz, other):
        return self.v.at[self.me.pair_at(dz, other), :, pl.ds(0, self.wa)]

    def b_start(self, i):
        o = self.ORDER[i]
        k = self.me.at(o, 2)
        for d, (lo, n) in enumerate(self.halves(o % 2)):
            self.send(("bx1", i, d), self.v.at[k, :, pl.ds(self.wa + lo, n)],
                      self.xb.at[i, d, :, pl.ds(lo, n)], self.me.dev(0, 1 - 2 * d))

    def join(self, ref, term, came, rest):
        (lo, n), (at, m) = came, rest
        cols = pl.ds(lo, n)
        ref[:, cols] = (ref[:, cols].astype(F32) + term[:, lo:lo + n]).astype(BF16)
        ref[:, pl.ds(at, m)] = term[:, at:at + m].astype(BF16)

    def b_next(self, i):
        o = self.ORDER[i]
        spans = self.halves(o % 2)
        for d in range(2):
            lo, n = spans[d]
            self.arrive(("bx1", i, d), self.xb.at[i, d, :, pl.ds(lo, n)])
            self.join(self.xb.at[i, d], self.mine(o, 1 - 2 * d), spans[d], spans[1 - d])
            self.send(("bx2", i, d), self.xb.at[i, d], self.xb.at[i, 2 + d], self.me.dev(0, 1 - 2 * d))

    def b_sum(self, i):
        for d in range(2):
            self.arrive(("bx2", i, d), self.xb.at[i, 2 + d])
        return (self.mine(self.ORDER[i], 0)
                + self.xb[i, 2].astype(F32) + self.xb[i, 3].astype(F32))

    def a_ring(self, s):
        for other in (1, 0):
            for d, right in ((0, True), (1, False)):
                ahead = (1 - 2 * d) * (5 - s)
                first = 1 if self.longer(right, other) else 2
                if s < first:
                    continue
                term = self.duo(ahead, other)
                src = term
                if s > first:
                    src = self.za.at[other, d, s - 2]
                    self.arrive(("a", s - 1, other, d), src)
                    src[...] = (src[...].astype(F32) + term[...].astype(F32)).astype(BF16)
                self.send(("a", s, other, d), src, self.za.at[other, d, s - 1],
                          self.me.dev(1 - 2 * d, 0))

    def a_sum(self, other):
        for d in range(2):
            self.arrive(("a", 4, other, d), self.za.at[other, d, 3])
        return (self.duo(0, other)[...].astype(F32)
                + self.za[other, 0, 3].astype(F32) + self.za[other, 1, 3].astype(F32))

    def b_ring(self, s, right=None, left=None):
        spans = self.halves(0)
        for d, (name, term) in enumerate((("br", right), ("bl", left))):
            lo, n = spans[d]
            if s == 1:
                src, dst = self.w.at[:, pl.ds(lo, n)], self.zb.at[d, 0, :, pl.ds(lo, n)]
            else:
                src, dst = self.zb.at[d, s - 2], self.zb.at[d, s - 1]
                if s == 2:
                    self.arrive((name, 1), self.zb.at[d, 0, :, pl.ds(lo, n)])
                    self.join(src, term, spans[d], spans[1 - d])
                else:
                    self.arrive((name, s - 1), src)
                    src[...] = (src[...].astype(F32) + term).astype(BF16)
            self.send((name, s), src, dst, self.me.dev(1 - 2 * d, 0))

    def start(self):
        for i in range(4):
            self.b_start(i)
        self.a_ring(1)
        for i in range(4, 8):
            self.b_start(i)

    def turn(self):
        for i in range(3):
            self.b_next(i)
        self.a_ring(2)
        for i in range(3, 8):
            self.b_next(i)

    def second(self):
        self.w[...] = self.b_sum(0).astype(BF16)
        self.b_ring(1)
        self.a_ring(3)
        self.b_ring(2, self.b_sum(1), self.b_sum(2))

    def third(self):
        self.a_ring(4)
        self.b_ring(3, self.b_sum(3), self.b_sum(4))

    def fourth(self):
        me, odd = self.me, self.me.odd
        for other in (1, 0):
            self.fin[other] = self.a_sum(other).astype(BF16)
        for q, other, k in ((3, 1, 1 - odd), (2, 1, odd), (1, 0, 1 - odd)):
            self.send(("ax",), self.fin.at[other, k], self.xa.at[q], me.mate_dev(q))
        self.b_ring(4, self.b_sum(5), self.b_sum(6))

    def last(self):
        self.arrive(("ax",), self.xa.at[pl.ds(1, 3)])
        a = self.fin[0, self.me.odd].astype(F32)
        for q in (1, 3, 2):
            a = a + self.xa[q].astype(F32)
        for d, name in enumerate(("br", "bl")):
            self.arrive((name, 4), self.zb.at[d, 3])
        b = self.b_sum(7) + self.zb[0, 3].astype(F32) + self.zb[1, 3].astype(F32)
        return jnp.concatenate([a, b], axis=1)


class Unit:
    def __init__(self, net, me, y, h, r1, acc, rd, rf):
        self.net, self.me, self.y, self.h = net, me, y, h
        self.r1, self.acc, self.rd, self.rf = r1, acc, rd, rf

    def pair(self, k, dy):
        return self.y[k, self.me.chunk(dy)].astype(F32) + self.r1[k, dy].astype(F32)

    def share(self, k):
        for dy in (2, 1, 3, 0):
            key = ("c", k, dy) if dy else ("end", k)
            self.net.send(key, "u1", self.y.at[k, self.me.chunk(dy, 1)], self.r1.at[k, dy],
                          self.me.peer(0, 1))

    def far(self, k):
        self.net.arrive(("c", k, 2), "u1", self.r1.at[k, 2])
        self.acc[k, 2] = self.pair(k, 2).astype(BF16)
        for i in range(2):
            self.net.send(("d", k, i), "u1", self.acc.at[k, 2, pl.ds(32 * i, 32)],
                          self.rd.at[k, i], self.me.peer(1 - 2 * i))

    def near(self, k):
        for dy, i in ((1, 0), (3, 1)):
            self.net.arrive(("c", k, dy), "u1", self.r1.at[k, dy])
            v = self.pair(k, dy)
            self.net.arrive(("d", k, i), "u1", self.rd.at[k, i])
            lo = 32 * i
            hi = 32 - lo
            self.acc[k, dy, pl.ds(lo, 32)] = (
                v[lo:lo + 32] + self.rd[k, i].astype(F32)
            ).astype(BF16)
            self.acc[k, dy, pl.ds(hi, 32)] = v[hi:hi + 32].astype(BF16)
            self.net.send(("end", k), "u1", self.acc.at[k, dy], self.rf.at[k, i],
                          self.me.peer(1 - 2 * i))

    def settle(self, k):
        self.net.arrive(("end", k), "u1", self.y.at[k, pl.ds(0, 3)])

    def total(self, k, rows):
        return (
            self.y[k, self.me.t, rows].astype(F32)
            + self.r1[k, 0, rows].astype(F32)
            + self.rf[k, 0, rows].astype(F32)
            + self.rf[k, 1, rows].astype(F32)
        )

    def spread(self, k):
        own = self.h.at[k, self.me.t]
        self.net.send(("gr", k), "u2", own, own, self.me.peer(1))
        self.net.send(("gl", k), "u2", own, own, self.me.peer(-1))
        self.net.send(("g", k), "u2", own, own, self.me.peer(0, 1))

    def relay(self, k):
        me = self.me
        for key, dy, lo in (("gr", -1, 0), ("gl", 1, 32)):
            ref = self.h.at[k, me.chunk(dy)]
            self.net.arrive((key, k), "u2", ref)
            half = self.h.at[k, me.chunk(dy), pl.ds(lo, 32)]
            self.net.send(("e", k), "u2", half, half, me.peer(-dy))
            self.net.send(("g", k), "u2", ref, ref, me.peer(0, 1))

    def close(self, k):
        me = self.me
        ref = self.h.at[k, me.chunk(2)]
        self.net.arrive(("e", k), "u2", ref)
        self.net.send(("g", k), "u2", ref, ref, me.peer(0, 1))
        self.net.arrive(("g", k), "u2", self.h.at[k, pl.ds(0, 4)])


def block_kernel(
    routes_ref, counts_ref, tok_ref, cot_ref, gain_ref, router_ref, wg_hbm, wu_hbm, wd_hbm,
    mix_ref, gt_ref, gain_out, router_out, gg_hbm, gu_hbm, gd_hbm,
    wg, wu, wd, gx, gs, pad, spot, sel, sel_t, x_all, x_gain, s_all,
    y, h, r1, acc, rd, rf, st_slots, p_slots, prod, part, vb, vn,
    za_b, zb_b, xa_b, xb_b, fin_b, w_b, za_n, zb_n, xa_n, xb_n, fin_n, w_n,
    cx, cz, sx, sz, go, local_sems, send_sems, recv_sems,
):
    me = Place()
    net = Net(send_sems, recv_sems, me.peer(0, 1))
    barrier = pltpu.get_barrier_semaphore()
    friends = (
        [me.dev(dz, 0) for dz in range(1, NZ)]
        + [me.dev(0, dx) for dx in range(1, NX)]
        + [me.peer(dy, f) for dy, f in PEERS]
    )
    for device in friends:
        pl.semaphore_signal(barrier, inc=1, device_id=device, device_id_type=MESH)
    loads = [
        pltpu.make_async_copy(src, dst, local_sems.at[i])
        for i, (src, dst) in enumerate(((wg_hbm, wg), (wu_hbm, wu), (wd_hbm, wd)))
    ]
    for load in loads:
        load.start()
    hot = one_hot(slot_ids(routes_ref, counts_ref))
    for src, dst in ((tok_ref, gx), (cot_ref, gs)):
        rows = dot(hot, src[...])[:CAP]
        dst[me.c] = jnp.concatenate([rows[:, :WIDE], rows[:, WIDE:]], axis=0).astype(BF16)
    lane8 = lax.broadcasted_iota(jnp.int32, (8, 128), 1)
    cx[0] = jnp.where(lane8 == me.c, counts_ref[0].astype(F32), 0.0)
    pl.semaphore_wait(barrier, len(friends))

    gather_x = Gather("X", net, me, 128, gx)
    gather_s = Gather("S", net, me, 256, gs)
    unit = Unit(net, me, y, h, r1, acc, rd, rf)

    gather_x.start()
    for dx in (1, 2, 3):
        net.send(("cx",), "cx", cx.at[0], cx.at[dx], me.dev(0, dx))
    gather_s.start()
    gather_x.begin_ring()
    net.arrive(("cx",), "cx", cx.at[pl.ds(1, 3)])
    cz[0] = cx[0] + cx[1] + cx[2] + cx[3]
    for dz in range(1, NZ):
        net.send(("cz",), "cz", cz.at[0], cz.at[dz], me.dev(dz, 0))
    gather_s.begin_ring()
    gather_x.step(1)
    gather_s.step(1)
    gather_x.step(2)
    net.arrive(("cz",), "cz", cz.at[pl.ds(1, NZ - 1)])
    held = cz[0]
    for dz in range(1, NZ):
        held = held + cz[dz]

    def place_of(shard, slot, combine):
        ahead = jnp.where(slot >= CAP * shard + CAP, 1.0, 0.0)
        inside = jnp.where(slot >= CAP * shard, 1.0 - ahead, 0.0)
        ahead, inside = ahead.astype(BF16), inside.astype(BF16)
        count, offset, shards = combine(inside, ahead)
        k = (slot[:1] if slot.shape[1] == SLOTS else slot).astype(F32) - CAP * shards
        return jnp.where(k < count, offset + k, -1.0)

    def as_row(inside, ahead):
        c = held.astype(BF16)
        one = jnp.ones((8, 128), BF16)
        return dot(c, inside)[0:1], dot(c, ahead)[0:1], dot(one, ahead)[0:1]

    line = place_of(
        lax.broadcasted_iota(jnp.int32, (128, SLOTS), 0),
        lax.broadcasted_iota(jnp.int32, (128, SLOTS), 1),
        as_row,
    )
    sel[...] = jnp.where(
        line == lax.broadcasted_iota(jnp.int32, (ROWS, SLOTS), 0).astype(F32), 1.0, 0.0
    ).astype(BF16)
    gather_s.step(2)
    gather_x.step(3)
    eye = lax.broadcasted_iota(jnp.int32, (128, 128), 0) == lax.broadcasted_iota(
        jnp.int32, (128, 128), 1
    )

    def as_column(inside, ahead):
        c = jnp.sum(jnp.where(eye, held[0:1], 0.0), axis=1, keepdims=True)
        c = jnp.broadcast_to(c, (128, 128)).astype(BF16)
        one = jnp.ones((128, 128), BF16)
        return dot(inside, c), dot(ahead, c), dot(ahead, one)

    spot[...] = place_of(
        lax.broadcasted_iota(jnp.int32, (SLOTS, 128), 1),
        lax.broadcasted_iota(jnp.int32, (SLOTS, 128), 0),
        as_column,
    )
    sel_t[...] = jnp.where(
        jnp.concatenate([spot[...]] * 4, axis=1)
        == lax.broadcasted_iota(jnp.int32, (SLOTS, ROWS), 1).astype(F32), 1.0, 0.0
    ).astype(BF16)
    gather_s.step(3)
    gather_x.step(4)
    gather_x.drain()

    def flatten(g):
        @pl.loop(0, NZ)
        def _(i):
            v = g[pl.ds(NX * i, NX)].astype(F32)
            rows = pl.ds(pl.multiple_of(i * (NX * CAP), 32), NX * CAP)
            pad[rows, pl.ds(0, WIDE)] = v[:, :CAP].reshape(NX * CAP, WIDE).astype(BF16)
            pad[rows, pl.ds(WIDE, WIDE)] = v[:, CAP:].reshape(NX * CAP, WIDE).astype(BF16)

    flatten(gx)
    for lo, n in COL_TILES:
        cols = pl.ds(lo, n)
        v = dot(sel[...], pad[:, cols])
        x_all[:, cols] = v.astype(BF16)
        x_gain[:, cols] = (v * gain_ref[:, cols]).astype(BF16)
    loads[0].wait()
    for lo, n in FF_TILES:
        v = dot(x_gain[...], wg[:, pl.ds(lo, n)])
        y[0, :, :, pl.ds(lo, n)] = v.astype(BF16).reshape(8, CHUNK, n)
    unit.share(0)
    gather_s.step(4)
    loads[1].wait()
    for lo, n in FF_TILES:
        v = dot(x_gain[...], wu[:, pl.ds(lo, n)])
        y[1, :, :, pl.ds(lo, n)] = v.astype(BF16).reshape(8, CHUNK, n)
    unit.share(1)
    unit.far(0)
    gather_s.drain()
    flatten(gs)
    for lo, n in COL_TILES:
        cols = pl.ds(lo, n)
        s_all[:, cols] = dot(sel[...], pad[:, cols]).astype(BF16)
    loads[2].wait()
    unit.far(1)
    for lo, n in FF_TILES:
        v = contract_cols(s_all[...], wd[pl.ds(lo, n), :])
        y[2, :, :, pl.ds(lo, n)] = v.astype(BF16).reshape(8, CHUNK, n)
    unit.share(2)
    unit.near(0)

    router = flat(router_ref[...].astype(F32))
    sq = jnp.zeros((ROWS, 128), F32)
    lg = jnp.zeros((ROWS, 128), F32)
    for lo in range(0, COLS, 128):
        v = x_all[:, pl.ds(lo, 128)].astype(F32)
        sq = sq + v * v
        lg = lg + v * router[:, lo:lo + 128]
    sq = jnp.sum(sq, axis=1, keepdims=True)
    lg = jnp.sum(lg, axis=1, keepdims=True)
    for i in range(8):
        v = (sq, lg)[i // 4][128 * (i % 4):128 * (i % 4) + 128]
        st_slots[me.t, pl.ds(i, 1)] = jnp.sum(jnp.where(eye, v, 0.0), axis=0, keepdims=True)
    for dy, f in PEERS:
        ref = st_slots.at[me.t]
        net.send(("st",), "st", ref, ref, me.peer(dy, f))
    unit.near(1)
    unit.far(2)

    net.arrive(("st",), "st", st_slots.at[pl.ds(0, 7)])
    stat = st_slots[0]
    for k in range(1, 8):
        stat = stat + st_slots[k]
    sub = lax.broadcasted_iota(jnp.int32, (8, 128), 0)
    lane = lax.broadcasted_iota(jnp.int32, (CHUNK, 128), 1)
    row = lax.broadcasted_iota(jnp.int32, (CHUNK, 128), 0)
    at_own = lane == row + me.core * CHUNK

    def column(which):
        line = jnp.sum(jnp.where(sub == which, stat, 0.0), axis=0, keepdims=True)
        return jnp.sum(jnp.where(at_own, line, 0.0), axis=1, keepdims=True)

    inv_rms = lax.rsqrt(column(me.y) / D + EPS)
    weight = jax.nn.sigmoid(column(4 + me.y))
    unit.settle(0)
    unit.settle(1)
    for i in range(4):
        rows = pl.ds(16 * i, 16)
        inv = inv_rms[16 * i:16 * i + 16]
        gate, upward = unit.total(0, rows) * inv, unit.total(1, rows) * inv
        h[0, me.t, rows] = (
            gate * jax.nn.sigmoid(gate) * upward * weight[16 * i:16 * i + 16]
        ).astype(BF16)
    unit.spread(0)
    unit.near(2)
    unit.relay(0)
    unit.settle(2)
    firsts, seconds = [], []
    for i in range(4):
        rows = pl.ds(16 * i, 16)
        inv = inv_rms[16 * i:16 * i + 16]
        w = weight[16 * i:16 * i + 16]
        g_raw, u_raw, d_raw = unit.total(0, rows), unit.total(1, rows), unit.total(2, rows)
        gate, upward = g_raw * inv, u_raw * inv
        sigma = jax.nn.sigmoid(gate)
        d_hidden = d_raw * (w * inv)
        d_gate = (d_hidden * upward * sigma * (1.0 + gate * (1.0 - sigma))).astype(BF16)
        d_up = (d_hidden * (gate * sigma)).astype(BF16)
        h[1, me.t, rows] = d_gate
        h[2, me.t, rows] = d_up
        firsts.append(jnp.sum(d_raw * h[0, me.t, rows].astype(F32), axis=1, keepdims=True))
        seconds.append(
            jnp.sum(d_gate.astype(F32) * g_raw + d_up.astype(F32) * u_raw, axis=1, keepdims=True)
        )
    unit.spread(1)
    unit.spread(2)

    def line_of(parts):
        return jnp.sum(jnp.where(at_own, jnp.concatenate(parts, axis=0), 0.0), axis=0, keepdims=True)

    p_slots[me.t] = jnp.where(sub == me.y, line_of(firsts), 0.0) + jnp.where(
        sub == 4 + me.y, line_of(seconds), 0.0
    )
    for dy, f in PEERS:
        ref = p_slots.at[me.t]
        net.send(("p",), "p", ref, ref, me.peer(dy, f))

    scatter_b = Scatter("B", net, me, 256, vb, za_b, zb_b, xa_b, xb_b, fin_b, w_b)
    scatter_n = Scatter("N", net, me, 128, vn, za_n, zb_n, xa_n, xb_n, fin_n, w_n)

    def all_rows(k):
        return h[k].reshape(ROWS, FFL)

    def expand(v):
        for g in range(2):
            s = sel_t[pl.ds(384 * g, 384), :]
            parts = [
                dot(s, prod[:, pl.ds(WIDE * i, WIDE)]).reshape(16, CAP, WIDE) for i in range(2)
            ]
            v[pl.ds(16 * g, 16)] = jnp.concatenate(parts, axis=1).astype(BF16)

    unit.close(0)
    for lo, n in COL_TILES:
        cols = pl.ds(lo, n)
        prod[:, cols] = dot(all_rows(0), wd[:, cols]).astype(BF16)
    expand(vb)
    scatter_b.start()
    unit.relay(1)
    scatter_b.turn()
    unit.relay(2)
    stores = []

    def write(i, src, out):
        store = pltpu.make_async_copy(src, out, local_sems.at[3 + i])
        store.start()
        stores.append(store)

    for lo in range(0, FFL, 128):
        left = h[0, :, :, pl.ds(lo, 128)].reshape(ROWS, 128)
        go[0, pl.ds(lo, 128), :] = contract_rows(left, s_all[...]).astype(BF16)
    write(0, go.at[0, pl.ds(0, FFL)], gd_hbm)
    unit.close(1)
    scatter_b.second()
    for lo, n in COL_TILES:
        cols = pl.ds(lo, n)
        part[:, cols] = contract_cols(all_rows(1), wg[cols, :])
    unit.close(2)
    for i, (lo, n) in enumerate(COL_TILES):
        cols = pl.ds(lo, n)
        v = part[:, cols] + contract_cols(all_rows(2), wu[cols, :])
        prod[:, cols] = v.astype(BF16)
        line = jnp.sum(v * x_all[:, cols].astype(F32), axis=0, keepdims=True)
        sx[0, pl.ds(8 + 2 * i, 1)] = line[:, :128]
        sx[0, pl.ds(9 + 2 * i, 1)] = line[:, 128:]
    net.arrive(("p",), "p", p_slots.at[pl.ds(0, 7)])
    p = p_slots[0]
    for k in range(1, 8):
        p = p + p_slots[k]
    sx[0, pl.ds(0, 8)] = p
    for dx in (1, 2, 3):
        net.send(("sx",), "sx", sx.at[0], sx.at[dx], me.dev(0, dx))
    expand(vn)
    scatter_n.start()
    scatter_b.third()
    net.arrive(("sx",), "sx", sx.at[pl.ds(1, 3)])
    sz[0] = sx[0] + sx[1] + sx[2] + sx[3]
    for dz in range(1, NZ):
        net.send(("sz",), "sz", sz.at[0], sz.at[dz], me.dev(dz, 0))
    scatter_n.turn()
    scatter_b.fourth()
    for lo in range(0, COLS, 256):
        left = x_gain[:, pl.ds(lo, 256)]
        go[1, pl.ds(lo, 256), pl.ds(0, FFL)] = contract_rows(left, all_rows(1)).astype(BF16)
    write(1, go.at[1, :, pl.ds(0, FFL)], gg_hbm)
    scatter_n.second()
    for lo in range(0, COLS, 256):
        left = x_gain[:, pl.ds(lo, 256)]
        go[2, pl.ds(lo, 256), pl.ds(0, FFL)] = contract_rows(left, all_rows(2)).astype(BF16)
    write(2, go.at[2, :, pl.ds(0, FFL)], gu_hbm)
    scatter_n.third()
    branch = scatter_b.last()
    scatter_n.fourth()

    net.arrive(("sz",), "sz", sz.at[pl.ds(1, NZ - 1)])
    tot = sz[0]
    for dz in range(1, NZ):
        tot = tot + sz[dz]
    d_logit = tot[0:4] * (1.0 - jax.nn.sigmoid(stat[4:8]))
    mean_term = tot[4:8] / D / (stat[0:4] / D + EPS)

    d_logit, mean_term = flat(d_logit), flat(mean_term)
    first = d_logit.astype(BF16)
    rest = d_logit - first.astype(F32)
    second = rest.astype(BF16)
    third = (rest - second.astype(F32)).astype(BF16)
    for lo, n in COL_TILES:
        cols = pl.ds(lo, n)
        x = x_all[:, cols]
        line = dot(first, x) + dot(second, x) + dot(third, x)
        for k in range(0, n, 128):
            router_out[pl.ds((lo + k) // 128, 1)] = line[:, k:k + 128]
    gain_out[...] = tot[8:16]
    own = spot[pl.ds(pl.multiple_of(me.c * CAP, 8), CAP), :]
    own = jnp.concatenate([own] * 4, axis=1)
    hit = own == lax.broadcasted_iota(jnp.int32, (CAP, ROWS), 1).astype(F32)
    d_logit = jnp.sum(jnp.where(hit, d_logit, 0.0), axis=1, keepdims=True)
    mean_term = jnp.sum(jnp.where(hit, mean_term, 0.0), axis=1, keepdims=True)

    d_normed = scatter_n.last()
    picked, slope = gx[me.c].astype(F32), gs[me.c].astype(F32)
    mix_ref[...] = picked + branch
    for i in range(2):
        r = slice(CAP * i, CAP * i + CAP)
        feats = slice(WIDE * i, WIDE * i + WIDE)
        gt_ref[pl.ds(CAP * i, CAP), :] = slope[r] + (
            d_normed[r] * gain_ref[:, pl.ds(WIDE * i, WIDE)] - picked[r] * mean_term
            + d_logit * router[:, feats]
        )
    for store in stores:
        store.wait()
    for paths, ref in ((gather_x, gx), (gather_s, gs), (scatter_b, vb), (scatter_n, vn)):
        paths.left(ref)
    net.left(("end", 0), "u1", y.at[:, pl.ds(0, 7)])
    net.left(("g", 0), "u2", h.at[:, pl.ds(0, 7)])
    for name, ref, n in (
        ("cx", cx, 3), ("cz", cz, 7), ("sx", sx, 3), ("sz", sz, 7), ("st", st_slots, 7), ("p", p_slots, 7)
    ):
        net.left((name,), name, ref.at[pl.ds(0, n)])


def block(routes, counts, tokens, cotangent, gain, router, w_gate, w_up, w_down):
    vm = pl.BlockSpec(memory_space=VMEM)
    sm = pl.BlockSpec(memory_space=pltpu.SMEM)
    hbm = pl.BlockSpec(memory_space=pl.ANY)
    ring_b, ring_n = (
        [
            VMEM((2, 2, 4, 2, TALL, wa), BF16),
            VMEM((2, 4, TALL, WIDE - wa), BF16),
            VMEM((4, TALL, wa), BF16),
            VMEM((8, 4, TALL, WIDE - wa), BF16),
            VMEM((2, 2, TALL, wa), BF16),
            VMEM((TALL, WIDE - wa), BF16),
        ]
        for wa in (256, 128)
    )
    return pl.pallas_call(
        block_kernel,
        out_shape=(
            jax.ShapeDtypeStruct((TALL, WIDE), F32),
            jax.ShapeDtypeStruct((TALL, WIDE), F32),
            jax.ShapeDtypeStruct((8, 128), F32),
            jax.ShapeDtypeStruct((8, 128), F32),
            jax.ShapeDtypeStruct((COLS, FFL), BF16),
            jax.ShapeDtypeStruct((COLS, FFL), BF16),
            jax.ShapeDtypeStruct((FFL, COLS), BF16),
        ),
        in_specs=[sm] * 2 + [vm] * 4 + [hbm] * 3,
        out_specs=(vm,) * 4 + (hbm,) * 3,
        scratch_shapes=[
            VMEM((COLS, FFL), BF16),
            VMEM((COLS, FFL), BF16),
            VMEM((FFL, COLS), BF16),
            VMEM((SHARDS, TALL, WIDE), BF16),
            VMEM((SHARDS, TALL, WIDE), BF16),
            VMEM((SLOTS, COLS), BF16),
            VMEM((SLOTS, 128), F32),
            VMEM((ROWS, SLOTS), BF16),
            VMEM((SLOTS, ROWS), BF16),
            VMEM((ROWS, COLS), BF16),
            VMEM((ROWS, COLS), BF16),
            VMEM((ROWS, COLS), BF16),
            VMEM((3, 8, CHUNK, FFL), BF16),
            VMEM((3, 8, CHUNK, FFL), BF16),
            VMEM((3, 4, CHUNK, FFL), BF16),
            VMEM((3, 4, CHUNK, FFL), BF16),
            VMEM((3, 2, CHUNK // 2, FFL), BF16),
            VMEM((3, 2, CHUNK, FFL), BF16),
            VMEM((8, 8, 128), F32),
            VMEM((8, 8, 128), F32),
            VMEM((ROWS, COLS), BF16),
            VMEM((ROWS, COLS), F32),
            VMEM((SHARDS, TALL, WIDE), BF16),
            VMEM((SHARDS, TALL, WIDE), BF16),
            *ring_b,
            *ring_n,
            VMEM((4, 8, 128), F32),
            VMEM((8, 8, 128), F32),
            VMEM((4, 16, 128), F32),
            VMEM((8, 16, 128), F32),
            VMEM((3, COLS, COLS), BF16),
            pltpu.SemaphoreType.DMA((6,)),
            pltpu.SemaphoreType.DMA((SEND_SEMS,)),
            pltpu.SemaphoreType.DMA((RECV_SEMS,)),
        ],
        compiler_params=pltpu.CompilerParams(
            collective_id=0, has_side_effects=True, vmem_limit_bytes=56 << 20
        ),
        name="block",
    )(routes, counts, tokens, cotangent, gain, router, w_gate, w_up, w_down)


def merge_kernel(
    routes_ref, counts_ref, tok_ref, cot_ref, mix_ref, gt_ref, gain_ref, router_ref, a_hbm, b_hbm, c_hbm,
    mixed_ref, grad_ref, gain_out, router_out, a_out, b_out, c_out,
    a, b, c, sems,
):
    n = 2
    ways = []
    for i, (src, held, dst) in enumerate(((a_hbm, a, a_out), (b_hbm, b, b_out), (c_hbm, c, c_out))):
        rows = src.shape[0] // n
        for j in range(n):
            part = pl.ds(rows * j, rows)
            k = i * n + j
            ways.append((
                pltpu.make_async_copy(src.at[part], held.at[part], sems.at[0, k]),
                pltpu.make_async_copy(held.at[part], dst.at[part], sems.at[1, k]),
            ))
    for come, _ in ways:
        come.start()
    gain_out[...] = gain_ref[...]
    router_out[...] = router_ref[...]
    hot = one_hot(slot_ids(routes_ref, counts_ref))
    picked = contract_rows(hot, jnp.ones((32, 128), BF16))[:, 0:1] > 0.5
    blank = jnp.zeros((32 - CAP, COLS), F32)
    for come, go in ways[:2]:
        come.wait()
        go.start()
    for old, new, out in ((tok_ref, mix_ref, mixed_ref), (cot_ref, gt_ref, grad_ref)):
        rows = jnp.concatenate([new[pl.ds(0, CAP), :], new[pl.ds(CAP, CAP), :]], axis=1)
        rows = jnp.concatenate([rows, blank], axis=0).astype(BF16)
        out[...] = jnp.where(picked, contract_rows(hot, rows), old[...].astype(F32)).astype(BF16)
    for come, go in ways[2:]:
        come.wait()
        go.start()
    for _, go in ways:
        go.wait()


def merge(routes, counts, tokens, cotangent, mixed_rows, grad_rows, gain, router, *grads):
    vm = pl.BlockSpec(memory_space=VMEM)
    sm = pl.BlockSpec(memory_space=pltpu.SMEM)
    hbm = pl.BlockSpec(memory_space=pl.ANY)
    same = [
        jax.ShapeDtypeStruct(v.shape, v.dtype) for v in (tokens, cotangent, gain, router) + grads
    ]
    return pl.pallas_call(
        merge_kernel,
        out_shape=same,
        in_specs=[sm] * 2 + [vm] * 6 + [hbm] * 3,
        out_specs=[vm] * 4 + [hbm] * 3,
        scratch_shapes=[VMEM(v.shape, v.dtype) for v in grads] + [pltpu.SemaphoreType.DMA((2, 6))],
        compiler_params=pltpu.CompilerParams(vmem_limit_bytes=60 << 20),
        name="merge",
    )(routes, counts, tokens, cotangent, mixed_rows, grad_rows, gain, router, *grads)


def body(tokens, norm_gain, router, w_gate, w_up, w_down, routes, counts, cotangent):
    new = block(
        routes, counts, tokens, cotangent, norm_gain[None, :], router.reshape(8, 128),
        w_gate, w_up, w_down,
    )
    mixed, grad_tokens, gain, router, *grads = merge(routes, counts, tokens, cotangent, *new)
    return (mixed, grad_tokens, *grads, gain.reshape(COLS), router.reshape(COLS))


def solution(mesh):
    return jax.shard_map(
        body,
        mesh=mesh,
        in_specs=(
            P("context", "tensor"),
            P("tensor"),
            P("tensor"),
            P("tensor", "context"),
            P("tensor", "context"),
            P("context", "tensor"),
            P("context", None),
            P("context"),
            P("context", "tensor"),
        ),
        out_specs=(
            P("context", "tensor"),
            P("context", "tensor"),
            P("tensor", "context"),
            P("tensor", "context"),
            P("context", "tensor"),
            P("tensor"),
            P("tensor"),
        ),
        check_vma=False,
    )
```

```python
import jax
import jax.numpy as jnp
from jax import lax
from jax.experimental import pallas as pl
from jax.experimental.pallas import tpu as pltpu
from jax.sharding import PartitionSpec as P

D = 8192
EPS = 1e-05
NX, NZ, NY = 4, 8, 4
SHARDS = NX * NZ
CAP = 24
SLOTS = SHARDS * CAP
ROWS = 512
CHUNK = 64
FFL = 896
COLS = 1024
TALL, WIDE = 2 * CAP, COLS // 2
SEND_SEMS, RECV_SEMS = 16, 236
MESH = pl.DeviceIdType.MESH
VMEM = pltpu.VMEM
F32 = jnp.float32
BF16 = jnp.bfloat16
FF_TILES = ((0, 256), (256, 256), (512, 256), (768, 128))
COL_TILES = ((0, 256), (256, 256), (512, 256), (768, 256))


def contract_rows(left, right):
    return lax.dot_general(left, right, (((0,), (0,)), ((), ())), preferred_element_type=F32)


def contract_cols(left, right):
    return lax.dot_general(left, right, (((1,), (1,)), ((), ())), preferred_element_type=F32)


def dot(left, right):
    return jnp.dot(left, right, preferred_element_type=F32)


class Net:
    def __init__(self, send_sems, recv_sems, other):
        self.send_sems, self.recv_sems, self.other = send_sems, recv_sems, other
        self.keys, self.groups = {}, {}

    def make(self, key, group, src, dst, device):
        k = self.keys.setdefault(key, len(self.keys))
        g = self.groups.setdefault(group, len(self.groups))
        assert k < RECV_SEMS and g < SEND_SEMS
        return pltpu.make_async_remote_copy(
            src_ref=src,
            dst_ref=dst,
            send_sem=self.send_sems.at[g],
            recv_sem=self.recv_sems.at[k],
            device_id=device,
            device_id_type=MESH,
        )

    def send(self, key, group, src, dst, device):
        self.make(key, group, src, dst, device).start()

    def arrive(self, key, group, ref):
        self.make(key, group, ref, ref, self.other).wait_recv()

    def left(self, key, group, ref):
        self.make(key, group, ref, ref, self.other).wait_send()


def slot_ids(routes_ref, counts_ref):
    row = lax.broadcasted_iota(jnp.int32, (32, 128), 0)
    ids = jnp.full((32, 128), -1, jnp.int32)
    for k in range(CAP):
        ids = jnp.where(row == k, routes_ref[0, k], ids)
    return jnp.where(row < counts_ref[0], ids, -1)


def one_hot(ids):
    lane = lax.broadcasted_iota(jnp.int32, (32, 128), 1)
    return jnp.where(ids == lane, 1.0, 0.0).astype(BF16)


class Place:
    def __init__(self):
        self.c, self.t = lax.axis_index("context"), lax.axis_index("tensor")
        self.z, self.x = lax.div(self.c, NX), lax.rem(self.c, NX)
        self.y, self.core = lax.div(self.t, 2), lax.rem(self.t, 2)
        self.odd = lax.rem(self.x, 2)
        self.pair = lax.div(self.x, 2)

    def at_z(self, dz):
        return lax.rem(self.z + dz + NZ, NZ)

    def at(self, dz, dx):
        return self.at_z(dz) * NX + lax.rem(self.x + dx + NX, NX)

    def dev(self, dz, dx):
        return (self.at(dz, dx), self.t)

    def mate(self, q):
        if q == 1:
            return self.x + 1 - 2 * self.odd
        return lax.rem(self.x + 2, NX) if q == 2 else 3 - self.x

    def mate_at(self, q):
        return self.z * NX + self.mate(q)

    def mate_dev(self, q):
        return (self.mate_at(q), self.t)

    def pair_at(self, dz, other):
        p = 1 - self.pair if other else self.pair
        return pl.ds(self.at_z(dz) * NX + 2 * p, 2)

    def chunk(self, dy, flip=0):
        k = 1 - self.core if flip else self.core
        return lax.rem(self.y + dy + NY, NY) * 2 + k

    def peer(self, dy, flip=0):
        return (self.c, self.chunk(dy, flip))


def flat(v):
    return jnp.concatenate([v[i:i + 1] for i in range(v.shape[0])], axis=1)


PEERS = [(dy, f) for dy in range(NY) for f in (0, 1) if (dy, f) != (0, 0)]


class Paths:
    def __init__(self, tag, net, me, wa):
        self.tag, self.net, self.me = tag, net, me
        self.wa, self.wb = wa, WIDE - wa

    def halves(self, odd):
        cut = 128 if odd else self.wb - 128
        return (0, cut), (cut, self.wb - cut)

    def send(self, key, src, dst, device):
        self.net.send((self.tag,) + key, (self.tag, key[0][0]), src, dst, device)

    def arrive(self, key, ref):
        self.net.arrive((self.tag,) + key, (self.tag, key[0][0]), ref)

    def left(self, ref):
        for part, key, lo, n in (("a", ("a", 2, 0), 0, self.wa), ("b", ("br", 2), self.wa, self.wb)):
            self.net.left((self.tag,) + key, (self.tag, part),
                          ref.at[pl.ds(0, SHARDS - 1), :, pl.ds(lo, n)])

    def longer(self, right, other):
        return right != bool(other)


class Gather(Paths):
    def __init__(self, tag, net, me, wa, g):
        super().__init__(tag, net, me, wa)
        self.g = g

    def part(self, dz, dx, span=None):
        lo, n = span or (0, self.wb)
        return self.g.at[self.me.at(dz, dx), :, pl.ds(self.wa + lo, n)]

    def duo(self, dz, other):
        return self.g.at[self.me.pair_at(dz, other), :, pl.ds(0, self.wa)]

    def pass_on(self, key, ref, device):
        self.send(key, ref, ref, device)

    def a_pass(self, s, other):
        for right, back in ((True, -1), (False, 1)):
            if s < 4 or self.longer(right, other):
                self.pass_on(("a", s, other, right), self.duo(back * (s - 1), other),
                             self.me.dev(-back, 0))

    def a_take(self, s, other):
        for right, back in ((True, -1), (False, 1)):
            if s < 4 or self.longer(right, other):
                self.arrive(("a", s, other, right), self.duo(back * s, other))

    def b_pass(self, s):
        r, l = self.halves(0) if s == 4 else (None, None)
        self.pass_on(("br", s), self.part(1 - s, 0, r), self.me.dev(1, 0))
        self.pass_on(("bl", s), self.part(s - 1, 0, l), self.me.dev(-1, 0))

    def b_take(self, s):
        r, l = self.halves(0) if s == 4 else (None, None)
        self.arrive(("br", s), self.part(-s, 0, r))
        self.arrive(("bl", s), self.part(s, 0, l))

    def b_side(self, o):
        r = self.part(o, 0)
        self.pass_on(("bxr", o), r, self.me.dev(0, 1))
        self.pass_on(("bxl", o), r, self.me.dev(0, -1))

    def b_cross(self, o):
        r, l = self.halves(o % 2)
        self.arrive(("bxr", o), self.part(o, -1))
        self.pass_on(("bd",), self.part(o, -1, r), self.me.dev(0, 1))
        self.arrive(("bxl", o), self.part(o, 1))
        self.pass_on(("bd",), self.part(o, 1, l), self.me.dev(0, -1))

    def start(self):
        own = self.g.at[self.me.c, :, pl.ds(0, self.wa)]
        self.b_pass(1)
        for q in (1, 2, 3):
            self.pass_on(("ax", q), own, self.me.mate_dev(q))
        self.b_side(0)

    def begin_ring(self):
        for q in (1, 2, 3):
            self.arrive(("ax", q), self.g.at[self.me.mate_at(q), :, pl.ds(0, self.wa)])
            if q != 2:
                self.a_pass(1, int(q == 3))

    def step(self, s):
        self.b_take(s)
        if s < 4:
            self.b_pass(s + 1)
            self.b_side(-s)
            self.b_side(s)
        else:
            self.b_side(4)
        for other in (0, 1):
            self.a_take(s, other)
            if s < 4:
                self.a_pass(s + 1, other)
        for o in ((0,) if s == 1 else (1 - s, s - 1)):
            self.b_cross(o)

    def drain(self):
        self.arrive(("bd",), self.g.at[pl.ds(0, NZ), :, pl.ds(self.wa, self.wb)])


class Scatter(Paths):
    ORDER = (4, 3, -3, 2, -2, 1, -1, 0)

    def __init__(self, tag, net, me, wa, v, za, zb, xa, xb, fin, w):
        super().__init__(tag, net, me, wa)
        self.v = v
        self.za, self.zb, self.xa, self.xb, self.fin, self.w = za, zb, xa, xb, fin, w

    def mine(self, dz, dx):
        return self.v[self.me.at(dz, dx), :, pl.ds(self.wa, self.wb)].astype(F32)

    def duo(self, dz, other):
        return self.v.at[self.me.pair_at(dz, other), :, pl.ds(0, self.wa)]

    def b_start(self, i):
        o = self.ORDER[i]
        k = self.me.at(o, 2)
        for d, (lo, n) in enumerate(self.halves(o % 2)):
            self.send(("bx1", i, d), self.v.at[k, :, pl.ds(self.wa + lo, n)],
                      self.xb.at[i, d, :, pl.ds(lo, n)], self.me.dev(0, 1 - 2 * d))

    def join(self, ref, term, came, rest):
        (lo, n), (at, m) = came, rest
        cols = pl.ds(lo, n)
        ref[:, cols] = (ref[:, cols].astype(F32) + term[:, lo:lo + n]).astype(BF16)
        ref[:, pl.ds(at, m)] = term[:, at:at + m].astype(BF16)

    def b_next(self, i):
        o = self.ORDER[i]
        spans = self.halves(o % 2)
        for d in range(2):
            lo, n = spans[d]
            self.arrive(("bx1", i, d), self.xb.at[i, d, :, pl.ds(lo, n)])
            self.join(self.xb.at[i, d], self.mine(o, 1 - 2 * d), spans[d], spans[1 - d])
            self.send(("bx2", i, d), self.xb.at[i, d], self.xb.at[i, 2 + d], self.me.dev(0, 1 - 2 * d))

    def b_sum(self, i):
        for d in range(2):
            self.arrive(("bx2", i, d), self.xb.at[i, 2 + d])
        return (self.mine(self.ORDER[i], 0)
                + self.xb[i, 2].astype(F32) + self.xb[i, 3].astype(F32))

    def a_ring(self, s):
        for other in (1, 0):
            for d, right in ((0, True), (1, False)):
                ahead = (1 - 2 * d) * (5 - s)
                first = 1 if self.longer(right, other) else 2
                if s < first:
                    continue
                term = self.duo(ahead, other)
                src = term
                if s > first:
                    src = self.za.at[other, d, s - 2]
                    self.arrive(("a", s - 1, other, d), src)
                    src[...] = (src[...].astype(F32) + term[...].astype(F32)).astype(BF16)
                self.send(("a", s, other, d), src, self.za.at[other, d, s - 1],
                          self.me.dev(1 - 2 * d, 0))

    def a_sum(self, other):
        for d in range(2):
            self.arrive(("a", 4, other, d), self.za.at[other, d, 3])
        return (self.duo(0, other)[...].astype(F32)
                + self.za[other, 0, 3].astype(F32) + self.za[other, 1, 3].astype(F32))

    def b_ring(self, s, right=None, left=None):
        spans = self.halves(0)
        for d, (name, term) in enumerate((("br", right), ("bl", left))):
            lo, n = spans[d]
            if s == 1:
                src, dst = self.w.at[:, pl.ds(lo, n)], self.zb.at[d, 0, :, pl.ds(lo, n)]
            else:
                src, dst = self.zb.at[d, s - 2], self.zb.at[d, s - 1]
                if s == 2:
                    self.arrive((name, 1), self.zb.at[d, 0, :, pl.ds(lo, n)])
                    self.join(src, term, spans[d], spans[1 - d])
                else:
                    self.arrive((name, s - 1), src)
                    src[...] = (src[...].astype(F32) + term).astype(BF16)
            self.send((name, s), src, dst, self.me.dev(1 - 2 * d, 0))

    def start(self):
        for i in range(4):
            self.b_start(i)
        self.a_ring(1)
        for i in range(4, 8):
            self.b_start(i)

    def turn(self):
        for i in range(3):
            self.b_next(i)
        self.a_ring(2)
        for i in range(3, 8):
            self.b_next(i)

    def second(self):
        self.w[...] = self.b_sum(0).astype(BF16)
        self.b_ring(1)
        self.a_ring(3)
        self.b_ring(2, self.b_sum(1), self.b_sum(2))

    def third(self):
        self.a_ring(4)
        self.b_ring(3, self.b_sum(3), self.b_sum(4))

    def fourth(self):
        me, odd = self.me, self.me.odd
        for other in (1, 0):
            self.fin[other] = self.a_sum(other).astype(BF16)
        for q, other, k in ((3, 1, 1 - odd), (2, 1, odd), (1, 0, 1 - odd)):
            self.send(("ax",), self.fin.at[other, k], self.xa.at[q], me.mate_dev(q))
        self.b_ring(4, self.b_sum(5), self.b_sum(6))

    def last(self):
        self.arrive(("ax",), self.xa.at[pl.ds(1, 3)])
        a = self.fin[0, self.me.odd].astype(F32)
        for q in (1, 3, 2):
            a = a + self.xa[q].astype(F32)
        for d, name in enumerate(("br", "bl")):
            self.arrive((name, 4), self.zb.at[d, 3])
        b = self.b_sum(7) + self.zb[0, 3].astype(F32) + self.zb[1, 3].astype(F32)
        return jnp.concatenate([a, b], axis=1)


class Unit:
    def __init__(self, net, me, y, h, r1, acc, rd, rf):
        self.net, self.me, self.y, self.h = net, me, y, h
        self.r1, self.acc, self.rd, self.rf = r1, acc, rd, rf

    def pair(self, k, dy):
        return self.y[k, self.me.chunk(dy)].astype(F32) + self.r1[k, dy].astype(F32)

    def share(self, k):
        for dy in (2, 1, 3, 0):
            key = ("c", k, dy) if dy else ("end", k)
            self.net.send(key, "u1", self.y.at[k, self.me.chunk(dy, 1)], self.r1.at[k, dy],
                          self.me.peer(0, 1))

    def far(self, k):
        self.net.arrive(("c", k, 2), "u1", self.r1.at[k, 2])
        self.acc[k, 2] = self.pair(k, 2).astype(BF16)
        for i in range(2):
            self.net.send(("d", k, i), "u1", self.acc.at[k, 2, pl.ds(32 * i, 32)],
                          self.rd.at[k, i], self.me.peer(1 - 2 * i))

    def near(self, k):
        for dy, i in ((1, 0), (3, 1)):
            self.net.arrive(("c", k, dy), "u1", self.r1.at[k, dy])
            v = self.pair(k, dy)
            self.net.arrive(("d", k, i), "u1", self.rd.at[k, i])
            lo = 32 * i
            hi = 32 - lo
            self.acc[k, dy, pl.ds(lo, 32)] = (
                v[lo:lo + 32] + self.rd[k, i].astype(F32)
            ).astype(BF16)
            self.acc[k, dy, pl.ds(hi, 32)] = v[hi:hi + 32].astype(BF16)
            self.net.send(("end", k), "u1", self.acc.at[k, dy], self.rf.at[k, i],
                          self.me.peer(1 - 2 * i))

    def settle(self, k):
        self.net.arrive(("end", k), "u1", self.y.at[k, pl.ds(0, 3)])

    def total(self, k, rows):
        return (
            self.y[k, self.me.t, rows].astype(F32)
            + self.r1[k, 0, rows].astype(F32)
            + self.rf[k, 0, rows].astype(F32)
            + self.rf[k, 1, rows].astype(F32)
        )

    def spread(self, k):
        own = self.h.at[k, self.me.t]
        self.net.send(("gr", k), "u2", own, own, self.me.peer(1))
        self.net.send(("gl", k), "u2", own, own, self.me.peer(-1))
        self.net.send(("g", k), "u2", own, own, self.me.peer(0, 1))

    def relay(self, k):
        me = self.me
        for key, dy, lo in (("gr", -1, 0), ("gl", 1, 32)):
            ref = self.h.at[k, me.chunk(dy)]
            self.net.arrive((key, k), "u2", ref)
            half = self.h.at[k, me.chunk(dy), pl.ds(lo, 32)]
            self.net.send(("e", k), "u2", half, half, me.peer(-dy))
            self.net.send(("g", k), "u2", ref, ref, me.peer(0, 1))

    def close(self, k):
        me = self.me
        ref = self.h.at[k, me.chunk(2)]
        self.net.arrive(("e", k), "u2", ref)
        self.net.send(("g", k), "u2", ref, ref, me.peer(0, 1))
        self.net.arrive(("g", k), "u2", self.h.at[k, pl.ds(0, 4)])


def block_kernel(
    routes_ref, counts_ref, tok_ref, cot_ref, gain_ref, router_ref, wg_hbm, wu_hbm, wd_hbm,
    mix_ref, gt_ref, gain_out, router_out, gg_hbm, gu_hbm, gd_hbm,
    wg, wu, wd, gx, gs, pad, spot, sel, sel_t, x_all, x_gain, s_all,
    y, h, r1, acc, rd, rf, st_slots, p_slots, prod, part, vb, vn,
    za_b, zb_b, xa_b, xb_b, fin_b, w_b, za_n, zb_n, xa_n, xb_n, fin_n, w_n,
    cx, cz, sx, sz, go, local_sems, send_sems, recv_sems,
):
    me = Place()
    net = Net(send_sems, recv_sems, me.peer(0, 1))
    barrier = pltpu.get_barrier_semaphore()
    friends = (
        [me.dev(dz, 0) for dz in range(1, NZ)]
        + [me.dev(0, dx) for dx in range(1, NX)]
        + [me.peer(dy, f) for dy, f in PEERS]
    )
    for device in friends:
        pl.semaphore_signal(barrier, inc=1, device_id=device, device_id_type=MESH)
    loads = [
        pltpu.make_async_copy(src, dst, local_sems.at[i])
        for i, (src, dst) in enumerate(((wg_hbm, wg), (wu_hbm, wu), (wd_hbm, wd)))
    ]
    for load in loads:
        load.start()
    hot = one_hot(slot_ids(routes_ref, counts_ref))
    for src, dst in ((tok_ref, gx), (cot_ref, gs)):
        rows = dot(hot, src[...])[:CAP]
        dst[me.c] = jnp.concatenate([rows[:, :WIDE], rows[:, WIDE:]], axis=0).astype(BF16)
    lane8 = lax.broadcasted_iota(jnp.int32, (8, 128), 1)
    cx[0] = jnp.where(lane8 == me.c, counts_ref[0].astype(F32), 0.0)
    pl.semaphore_wait(barrier, len(friends))

    gather_x = Gather("X", net, me, 128, gx)
    gather_s = Gather("S", net, me, 256, gs)
    unit = Unit(net, me, y, h, r1, acc, rd, rf)

    gather_x.start()
    for dx in (1, 2, 3):
        net.send(("cx",), "cx", cx.at[0], cx.at[dx], me.dev(0, dx))
    gather_s.start()
    gather_x.begin_ring()
    net.arrive(("cx",), "cx", cx.at[pl.ds(1, 3)])
    cz[0] = cx[0] + cx[1] + cx[2] + cx[3]
    for dz in range(1, NZ):
        net.send(("cz",), "cz", cz.at[0], cz.at[dz], me.dev(dz, 0))
    gather_s.begin_ring()
    gather_x.step(1)
    gather_s.step(1)
    gather_x.step(2)
    net.arrive(("cz",), "cz", cz.at[pl.ds(1, NZ - 1)])
    held = cz[0]
    for dz in range(1, NZ):
        held = held + cz[dz]

    def place_of(shard, slot, combine):
        ahead = jnp.where(slot >= CAP * shard + CAP, 1.0, 0.0)
        inside = jnp.where(slot >= CAP * shard, 1.0 - ahead, 0.0)
        ahead, inside = ahead.astype(BF16), inside.astype(BF16)
        count, offset, shards = combine(inside, ahead)
        k = (slot[:1] if slot.shape[1] == SLOTS else slot).astype(F32) - CAP * shards
        return jnp.where(k < count, offset + k, -1.0)

    def as_row(inside, ahead):
        c = held.astype(BF16)
        one = jnp.ones((8, 128), BF16)
        return dot(c, inside)[0:1], dot(c, ahead)[0:1], dot(one, ahead)[0:1]

    line = place_of(
        lax.broadcasted_iota(jnp.int32, (128, SLOTS), 0),
        lax.broadcasted_iota(jnp.int32, (128, SLOTS), 1),
        as_row,
    )
    sel[...] = jnp.where(
        line == lax.broadcasted_iota(jnp.int32, (ROWS, SLOTS), 0).astype(F32), 1.0, 0.0
    ).astype(BF16)
    gather_s.step(2)
    gather_x.step(3)
    eye = lax.broadcasted_iota(jnp.int32, (128, 128), 0) == lax.broadcasted_iota(
        jnp.int32, (128, 128), 1
    )

    def as_column(inside, ahead):
        c = jnp.sum(jnp.where(eye, held[0:1], 0.0), axis=1, keepdims=True)
        c = jnp.broadcast_to(c, (128, 128)).astype(BF16)
        one = jnp.ones((128, 128), BF16)
        return dot(inside, c), dot(ahead, c), dot(ahead, one)

    spot[...] = place_of(
        lax.broadcasted_iota(jnp.int32, (SLOTS, 128), 1),
        lax.broadcasted_iota(jnp.int32, (SLOTS, 128), 0),
        as_column,
    )
    sel_t[...] = jnp.where(
        jnp.concatenate([spot[...]] * 4, axis=1)
        == lax.broadcasted_iota(jnp.int32, (SLOTS, ROWS), 1).astype(F32), 1.0, 0.0
    ).astype(BF16)
    gather_s.step(3)
    gather_x.step(4)
    gather_s.step(4)
    gather_x.b_cross(4)
    gather_x.drain()
    gather_s.b_cross(4)

    def flatten(g):
        @pl.loop(0, NZ)
        def _(i):
            v = g[pl.ds(NX * i, NX)].astype(F32)
            rows = pl.ds(pl.multiple_of(i * (NX * CAP), 32), NX * CAP)
            pad[rows, pl.ds(0, WIDE)] = v[:, :CAP].reshape(NX * CAP, WIDE).astype(BF16)
            pad[rows, pl.ds(WIDE, WIDE)] = v[:, CAP:].reshape(NX * CAP, WIDE).astype(BF16)

    flatten(gx)
    for lo, n in COL_TILES:
        cols = pl.ds(lo, n)
        v = dot(sel[...], pad[:, cols])
        x_all[:, cols] = v.astype(BF16)
        x_gain[:, cols] = (v * gain_ref[:, cols]).astype(BF16)
    loads[0].wait()
    for lo, n in FF_TILES:
        v = dot(x_gain[...], wg[:, pl.ds(lo, n)])
        y[0, :, :, pl.ds(lo, n)] = v.astype(BF16).reshape(8, CHUNK, n)
    unit.share(0)
    gather_s.drain()
    loads[1].wait()
    for lo, n in FF_TILES:
        v = dot(x_gain[...], wu[:, pl.ds(lo, n)])
        y[1, :, :, pl.ds(lo, n)] = v.astype(BF16).reshape(8, CHUNK, n)
    unit.share(1)
    unit.far(0)
    flatten(gs)
    for lo, n in COL_TILES:
        cols = pl.ds(lo, n)
        s_all[:, cols] = dot(sel[...], pad[:, cols]).astype(BF16)
    loads[2].wait()
    unit.far(1)
    for lo, n in FF_TILES:
        v = contract_cols(s_all[...], wd[pl.ds(lo, n), :])
        y[2, :, :, pl.ds(lo, n)] = v.astype(BF16).reshape(8, CHUNK, n)
    unit.share(2)
    unit.near(0)

    router = flat(router_ref[...].astype(F32))
    sq = jnp.zeros((ROWS, 128), F32)
    lg = jnp.zeros((ROWS, 128), F32)
    for lo in range(0, COLS, 128):
        v = x_all[:, pl.ds(lo, 128)].astype(F32)
        sq = sq + v * v
        lg = lg + v * router[:, lo:lo + 128]
    sq = jnp.sum(sq, axis=1, keepdims=True)
    lg = jnp.sum(lg, axis=1, keepdims=True)
    for i in range(8):
        v = (sq, lg)[i // 4][128 * (i % 4):128 * (i % 4) + 128]
        st_slots[me.t, pl.ds(i, 1)] = jnp.sum(jnp.where(eye, v, 0.0), axis=0, keepdims=True)
    for dy, f in PEERS:
        ref = st_slots.at[me.t]
        net.send(("st",), "st", ref, ref, me.peer(dy, f))
    unit.near(1)
    unit.far(2)

    net.arrive(("st",), "st", st_slots.at[pl.ds(0, 7)])
    stat = st_slots[0]
    for k in range(1, 8):
        stat = stat + st_slots[k]
    sub = lax.broadcasted_iota(jnp.int32, (8, 128), 0)
    lane = lax.broadcasted_iota(jnp.int32, (CHUNK, 128), 1)
    row = lax.broadcasted_iota(jnp.int32, (CHUNK, 128), 0)
    at_own = lane == row + me.core * CHUNK

    def column(which):
        line = jnp.sum(jnp.where(sub == which, stat, 0.0), axis=0, keepdims=True)
        return jnp.sum(jnp.where(at_own, line, 0.0), axis=1, keepdims=True)

    inv_rms = lax.rsqrt(column(me.y) / D + EPS)
    weight = jax.nn.sigmoid(column(4 + me.y))
    unit.settle(0)
    unit.settle(1)
    for i in range(4):
        rows = pl.ds(16 * i, 16)
        inv = inv_rms[16 * i:16 * i + 16]
        gate, upward = unit.total(0, rows) * inv, unit.total(1, rows) * inv
        h[0, me.t, rows] = (
            gate * jax.nn.sigmoid(gate) * upward * weight[16 * i:16 * i + 16]
        ).astype(BF16)
    unit.spread(0)
    unit.near(2)
    unit.relay(0)
    unit.settle(2)
    firsts, seconds = [], []
    for i in range(4):
        rows = pl.ds(16 * i, 16)
        inv = inv_rms[16 * i:16 * i + 16]
        w = weight[16 * i:16 * i + 16]
        g_raw, u_raw, d_raw = unit.total(0, rows), unit.total(1, rows), unit.total(2, rows)
        gate, upward = g_raw * inv, u_raw * inv
        sigma = jax.nn.sigmoid(gate)
        d_hidden = d_raw * (w * inv)
        d_gate = (d_hidden * upward * sigma * (1.0 + gate * (1.0 - sigma))).astype(BF16)
        d_up = (d_hidden * (gate * sigma)).astype(BF16)
        h[1, me.t, rows] = d_gate
        h[2, me.t, rows] = d_up
        firsts.append(jnp.sum(d_raw * h[0, me.t, rows].astype(F32), axis=1, keepdims=True))
        seconds.append(
            jnp.sum(d_gate.astype(F32) * g_raw + d_up.astype(F32) * u_raw, axis=1, keepdims=True)
        )
    unit.spread(1)
    unit.spread(2)

    def line_of(parts):
        return jnp.sum(jnp.where(at_own, jnp.concatenate(parts, axis=0), 0.0), axis=0, keepdims=True)

    p_slots[me.t] = jnp.where(sub == me.y, line_of(firsts), 0.0) + jnp.where(
        sub == 4 + me.y, line_of(seconds), 0.0
    )
    for dy, f in PEERS:
        ref = p_slots.at[me.t]
        net.send(("p",), "p", ref, ref, me.peer(dy, f))

    scatter_b = Scatter("B", net, me, 256, vb, za_b, zb_b, xa_b, xb_b, fin_b, w_b)
    scatter_n = Scatter("N", net, me, 128, vn, za_n, zb_n, xa_n, xb_n, fin_n, w_n)

    def all_rows(k):
        return h[k].reshape(ROWS, FFL)

    def expand(v):
        for g in range(2):
            s = sel_t[pl.ds(384 * g, 384), :]
            parts = [
                dot(s, prod[:, pl.ds(WIDE * i, WIDE)]).reshape(16, CAP, WIDE) for i in range(2)
            ]
            v[pl.ds(16 * g, 16)] = jnp.concatenate(parts, axis=1).astype(BF16)

    unit.close(0)
    for lo, n in COL_TILES:
        cols = pl.ds(lo, n)
        prod[:, cols] = dot(all_rows(0), wd[:, cols]).astype(BF16)
    expand(vb)
    scatter_b.start()
    unit.relay(1)
    scatter_b.turn()
    unit.relay(2)
    stores = []

    def write(i, src, out):
        store = pltpu.make_async_copy(src, out, local_sems.at[3 + i])
        store.start()
        stores.append(store)

    for lo in range(0, FFL, 128):
        left = h[0, :, :, pl.ds(lo, 128)].reshape(ROWS, 128)
        go[0, pl.ds(lo, 128), :] = contract_rows(left, s_all[...]).astype(BF16)
    write(0, go.at[0, pl.ds(0, FFL)], gd_hbm)
    unit.close(1)
    scatter_b.second()
    for lo, n in COL_TILES:
        cols = pl.ds(lo, n)
        part[:, cols] = contract_cols(all_rows(1), wg[cols, :])
    unit.close(2)
    for i, (lo, n) in enumerate(COL_TILES):
        cols = pl.ds(lo, n)
        v = part[:, cols] + contract_cols(all_rows(2), wu[cols, :])
        prod[:, cols] = v.astype(BF16)
        line = jnp.sum(v * x_all[:, cols].astype(F32), axis=0, keepdims=True)
        sx[0, pl.ds(8 + 2 * i, 1)] = line[:, :128]
        sx[0, pl.ds(9 + 2 * i, 1)] = line[:, 128:]
    net.arrive(("p",), "p", p_slots.at[pl.ds(0, 7)])
    p = p_slots[0]
    for k in range(1, 8):
        p = p + p_slots[k]
    sx[0, pl.ds(0, 8)] = p
    for dx in (1, 2, 3):
        net.send(("sx",), "sx", sx.at[0], sx.at[dx], me.dev(0, dx))
    expand(vn)
    scatter_n.start()
    scatter_b.third()
    net.arrive(("sx",), "sx", sx.at[pl.ds(1, 3)])
    sz[0] = sx[0] + sx[1] + sx[2] + sx[3]
    for dz in range(1, NZ):
        net.send(("sz",), "sz", sz.at[0], sz.at[dz], me.dev(dz, 0))
    scatter_n.turn()
    scatter_b.fourth()
    for lo in range(0, COLS, 256):
        left = x_gain[:, pl.ds(lo, 256)]
        go[1, pl.ds(lo, 256), pl.ds(0, FFL)] = contract_rows(left, all_rows(1)).astype(BF16)
    write(1, go.at[1, :, pl.ds(0, FFL)], gg_hbm)
    scatter_n.second()
    for lo in range(0, COLS, 256):
        left = x_gain[:, pl.ds(lo, 256)]
        go[2, pl.ds(lo, 256), pl.ds(0, FFL)] = contract_rows(left, all_rows(2)).astype(BF16)
    write(2, go.at[2, :, pl.ds(0, FFL)], gu_hbm)
    scatter_n.third()
    branch = scatter_b.last()
    scatter_n.fourth()

    net.arrive(("sz",), "sz", sz.at[pl.ds(1, NZ - 1)])
    tot = sz[0]
    for dz in range(1, NZ):
        tot = tot + sz[dz]
    d_logit = tot[0:4] * (1.0 - jax.nn.sigmoid(stat[4:8]))
    mean_term = tot[4:8] / D / (stat[0:4] / D + EPS)

    d_logit, mean_term = flat(d_logit), flat(mean_term)
    first = d_logit.astype(BF16)
    rest = d_logit - first.astype(F32)
    second = rest.astype(BF16)
    third = (rest - second.astype(F32)).astype(BF16)
    for lo, n in COL_TILES:
        cols = pl.ds(lo, n)
        x = x_all[:, cols]
        line = dot(first, x) + dot(second, x) + dot(third, x)
        for k in range(0, n, 128):
            router_out[pl.ds((lo + k) // 128, 1)] = line[:, k:k + 128]
    gain_out[...] = tot[8:16]
    own = spot[pl.ds(pl.multiple_of(me.c * CAP, 8), CAP), :]
    own = jnp.concatenate([own] * 4, axis=1)
    hit = own == lax.broadcasted_iota(jnp.int32, (CAP, ROWS), 1).astype(F32)
    d_logit = jnp.sum(jnp.where(hit, d_logit, 0.0), axis=1, keepdims=True)
    mean_term = jnp.sum(jnp.where(hit, mean_term, 0.0), axis=1, keepdims=True)

    d_normed = scatter_n.last()
    picked, slope = gx[me.c].astype(F32), gs[me.c].astype(F32)
    mix_ref[...] = picked + branch
    for i in range(2):
        r = slice(CAP * i, CAP * i + CAP)
        feats = slice(WIDE * i, WIDE * i + WIDE)
        gt_ref[pl.ds(CAP * i, CAP), :] = slope[r] + (
            d_normed[r] * gain_ref[:, pl.ds(WIDE * i, WIDE)] - picked[r] * mean_term
            + d_logit * router[:, feats]
        )
    for store in stores:
        store.wait()
    for paths, ref in ((gather_x, gx), (gather_s, gs), (scatter_b, vb), (scatter_n, vn)):
        paths.left(ref)
    net.left(("end", 0), "u1", y.at[:, pl.ds(0, 7)])
    net.left(("g", 0), "u2", h.at[:, pl.ds(0, 7)])
    for name, ref, n in (
        ("cx", cx, 3), ("cz", cz, 7), ("sx", sx, 3), ("sz", sz, 7), ("st", st_slots, 7), ("p", p_slots, 7)
    ):
        net.left((name,), name, ref.at[pl.ds(0, n)])


def block(routes, counts, tokens, cotangent, gain, router, w_gate, w_up, w_down):
    vm = pl.BlockSpec(memory_space=VMEM)
    sm = pl.BlockSpec(memory_space=pltpu.SMEM)
    hbm = pl.BlockSpec(memory_space=pl.ANY)
    ring_b, ring_n = (
        [
            VMEM((2, 2, 4, 2, TALL, wa), BF16),
            VMEM((2, 4, TALL, WIDE - wa), BF16),
            VMEM((4, TALL, wa), BF16),
            VMEM((8, 4, TALL, WIDE - wa), BF16),
            VMEM((2, 2, TALL, wa), BF16),
            VMEM((TALL, WIDE - wa), BF16),
        ]
        for wa in (256, 128)
    )
    return pl.pallas_call(
        block_kernel,
        out_shape=(
            jax.ShapeDtypeStruct((TALL, WIDE), F32),
            jax.ShapeDtypeStruct((TALL, WIDE), F32),
            jax.ShapeDtypeStruct((8, 128), F32),
            jax.ShapeDtypeStruct((8, 128), F32),
            jax.ShapeDtypeStruct((COLS, FFL), BF16),
            jax.ShapeDtypeStruct((COLS, FFL), BF16),
            jax.ShapeDtypeStruct((FFL, COLS), BF16),
        ),
        in_specs=[sm] * 2 + [vm] * 4 + [hbm] * 3,
        out_specs=(vm,) * 4 + (hbm,) * 3,
        scratch_shapes=[
            VMEM((COLS, FFL), BF16),
            VMEM((COLS, FFL), BF16),
            VMEM((FFL, COLS), BF16),
            VMEM((SHARDS, TALL, WIDE), BF16),
            VMEM((SHARDS, TALL, WIDE), BF16),
            VMEM((SLOTS, COLS), BF16),
            VMEM((SLOTS, 128), F32),
            VMEM((ROWS, SLOTS), BF16),
            VMEM((SLOTS, ROWS), BF16),
            VMEM((ROWS, COLS), BF16),
            VMEM((ROWS, COLS), BF16),
            VMEM((ROWS, COLS), BF16),
            VMEM((3, 8, CHUNK, FFL), BF16),
            VMEM((3, 8, CHUNK, FFL), BF16),
            VMEM((3, 4, CHUNK, FFL), BF16),
            VMEM((3, 4, CHUNK, FFL), BF16),
            VMEM((3, 2, CHUNK // 2, FFL), BF16),
            VMEM((3, 2, CHUNK, FFL), BF16),
            VMEM((8, 8, 128), F32),
            VMEM((8, 8, 128), F32),
            VMEM((ROWS, COLS), BF16),
            VMEM((ROWS, COLS), F32),
            VMEM((SHARDS, TALL, WIDE), BF16),
            VMEM((SHARDS, TALL, WIDE), BF16),
            *ring_b,
            *ring_n,
            VMEM((4, 8, 128), F32),
            VMEM((8, 8, 128), F32),
            VMEM((4, 16, 128), F32),
            VMEM((8, 16, 128), F32),
            VMEM((3, COLS, COLS), BF16),
            pltpu.SemaphoreType.DMA((6,)),
            pltpu.SemaphoreType.DMA((SEND_SEMS,)),
            pltpu.SemaphoreType.DMA((RECV_SEMS,)),
        ],
        compiler_params=pltpu.CompilerParams(
            collective_id=0, has_side_effects=True, vmem_limit_bytes=56 << 20
        ),
        name="block",
    )(routes, counts, tokens, cotangent, gain, router, w_gate, w_up, w_down)


def merge_kernel(
    routes_ref, counts_ref, tok_hbm, cot_hbm, mix_hbm, gt_hbm, gain_hbm, router_hbm, a_hbm, b_hbm, c_hbm,
    mixed_out, grad_out, gain_out, router_out, a_out, b_out, c_out,
    tok, cot, mix, gt, gain, router, a, b, c, mixed, grad, in_sems, out_sems,
):
    pieces = [
        (mix_hbm, mix, None), (gt_hbm, gt, None), (tok_hbm, tok, None), (cot_hbm, cot, None),
        (gain_hbm, gain, gain_out), (router_hbm, router, router_out),
    ]
    for src, held, dst in ((a_hbm, a, a_out), (b_hbm, b, b_out), (c_hbm, c, c_out)):
        rows = src.shape[0] // 2
        for j in range(2):
            part = pl.ds(rows * j, rows)
            pieces.append((src.at[part], held.at[part], dst.at[part]))
    come = [
        pltpu.make_async_copy(src, held, in_sems.at[k]) for k, (src, held, _) in enumerate(pieces)
    ]
    for copy in come:
        copy.start()
    gone = []

    def leave(held, dst):
        copy = pltpu.make_async_copy(held, dst, out_sems.at[len(gone)])
        copy.start()
        gone.append(copy)

    hot = one_hot(slot_ids(routes_ref, counts_ref))
    picked = contract_rows(hot, jnp.ones((32, 128), BF16))[:, 0:1] > 0.5
    blank = jnp.zeros((32 - CAP, COLS), F32)
    for copy in come[:4]:
        copy.wait()
    for old, new, held, dst in ((tok, mix, mixed, mixed_out), (cot, gt, grad, grad_out)):
        rows = jnp.concatenate([new[pl.ds(0, CAP), :], new[pl.ds(CAP, CAP), :]], axis=1)
        rows = jnp.concatenate([rows, blank], axis=0).astype(BF16)
        held[...] = jnp.where(picked, contract_rows(hot, rows), old[...].astype(F32)).astype(BF16)
        leave(held, dst)
    for copy, (_, held, dst) in zip(come[4:], pieces[4:]):
        copy.wait()
        leave(held, dst)
    for copy in gone:
        copy.wait()


def merge(routes, counts, tokens, cotangent, *new):
    sm = pl.BlockSpec(memory_space=pltpu.SMEM)
    hbm = pl.BlockSpec(memory_space=pl.ANY)
    out = (tokens, cotangent) + new[2:]
    return pl.pallas_call(
        merge_kernel,
        out_shape=[jax.ShapeDtypeStruct(v.shape, v.dtype) for v in out],
        in_specs=[sm] * 2 + [hbm] * 9,
        out_specs=[hbm] * 7,
        scratch_shapes=[VMEM(v.shape, v.dtype) for v in (tokens, cotangent) + new]
        + [VMEM(v.shape, v.dtype) for v in (tokens, cotangent)]
        + [pltpu.SemaphoreType.DMA((12,)), pltpu.SemaphoreType.DMA((10,))],
        compiler_params=pltpu.CompilerParams(vmem_limit_bytes=60 << 20),
        name="merge",
    )(routes, counts, tokens, cotangent, *new)


def body(tokens, norm_gain, router, w_gate, w_up, w_down, routes, counts, cotangent):
    new = block(
        routes, counts, tokens, cotangent, norm_gain[None, :], router.reshape(8, 128),
        w_gate, w_up, w_down,
    )
    mixed, grad_tokens, gain, router, *grads = merge(routes, counts, tokens, cotangent, *new)
    return (mixed, grad_tokens, *grads, gain.reshape(COLS), router.reshape(COLS))


def solution(mesh):
    return jax.shard_map(
        body,
        mesh=mesh,
        in_specs=(
            P("context", "tensor"),
            P("tensor"),
            P("tensor"),
            P("tensor", "context"),
            P("tensor", "context"),
            P("context", "tensor"),
            P("context", None),
            P("context"),
            P("context", "tensor"),
        ),
        out_specs=(
            P("context", "tensor"),
            P("context", "tensor"),
            P("tensor", "context"),
            P("tensor", "context"),
            P("context", "tensor"),
            P("tensor"),
            P("tensor"),
        ),
        check_vma=False,
    )
```

```python
import jax
import jax.numpy as jnp
from jax import lax
from jax.experimental import pallas as pl
from jax.experimental.pallas import tpu as pltpu
from jax.sharding import PartitionSpec as P

D = 8192
EPS = 1e-05
NX, NZ, NY = 4, 8, 4
SHARDS = NX * NZ
CAP = 24
SLOTS = SHARDS * CAP
ROWS = 512
CHUNK = 64
FFL = 896
COLS = 1024
TALL, WIDE = 2 * CAP, COLS // 2
SEND_SEMS, RECV_SEMS = 16, 236
MESH = pl.DeviceIdType.MESH
VMEM = pltpu.VMEM
F32 = jnp.float32
BF16 = jnp.bfloat16
FF_TILES = ((0, 256), (256, 256), (512, 256), (768, 128))
COL_TILES = ((0, 256), (256, 256), (512, 256), (768, 256))


def contract_rows(left, right):
    return lax.dot_general(left, right, (((0,), (0,)), ((), ())), preferred_element_type=F32)


def contract_cols(left, right):
    return lax.dot_general(left, right, (((1,), (1,)), ((), ())), preferred_element_type=F32)


def dot(left, right):
    return jnp.dot(left, right, preferred_element_type=F32)


class Net:
    def __init__(self, send_sems, recv_sems, other):
        self.send_sems, self.recv_sems, self.other = send_sems, recv_sems, other
        self.keys, self.groups = {}, {}

    def make(self, key, group, src, dst, device):
        k = self.keys.setdefault(key, len(self.keys))
        g = self.groups.setdefault(group, len(self.groups))
        assert k < RECV_SEMS and g < SEND_SEMS
        return pltpu.make_async_remote_copy(
            src_ref=src,
            dst_ref=dst,
            send_sem=self.send_sems.at[g],
            recv_sem=self.recv_sems.at[k],
            device_id=device,
            device_id_type=MESH,
        )

    def send(self, key, group, src, dst, device):
        self.make(key, group, src, dst, device).start()

    def arrive(self, key, group, ref):
        self.make(key, group, ref, ref, self.other).wait_recv()

    def left(self, key, group, ref):
        self.make(key, group, ref, ref, self.other).wait_send()


def slot_ids(routes_ref, counts_ref):
    row = lax.broadcasted_iota(jnp.int32, (32, 128), 0)
    ids = jnp.full((32, 128), -1, jnp.int32)
    for k in range(CAP):
        ids = jnp.where(row == k, routes_ref[0, k], ids)
    return jnp.where(row < counts_ref[0], ids, -1)


def one_hot(ids):
    lane = lax.broadcasted_iota(jnp.int32, (32, 128), 1)
    return jnp.where(ids == lane, 1.0, 0.0).astype(BF16)


class Place:
    def __init__(self):
        self.c, self.t = lax.axis_index("context"), lax.axis_index("tensor")
        self.z, self.x = lax.div(self.c, NX), lax.rem(self.c, NX)
        self.y, self.core = lax.div(self.t, 2), lax.rem(self.t, 2)
        self.odd = lax.rem(self.x, 2)
        self.pair = lax.div(self.x, 2)

    def at_z(self, dz):
        return lax.rem(self.z + dz + NZ, NZ)

    def at(self, dz, dx):
        return self.at_z(dz) * NX + lax.rem(self.x + dx + NX, NX)

    def dev(self, dz, dx):
        return (self.at(dz, dx), self.t)

    def mate(self, q):
        if q == 1:
            return self.x + 1 - 2 * self.odd
        return lax.rem(self.x + 2, NX) if q == 2 else 3 - self.x

    def mate_at(self, q):
        return self.z * NX + self.mate(q)

    def mate_dev(self, q):
        return (self.mate_at(q), self.t)

    def pair_at(self, dz, other):
        p = 1 - self.pair if other else self.pair
        return pl.ds(self.at_z(dz) * NX + 2 * p, 2)

    def chunk(self, dy, flip=0):
        k = 1 - self.core if flip else self.core
        return lax.rem(self.y + dy + NY, NY) * 2 + k

    def peer(self, dy, flip=0):
        return (self.c, self.chunk(dy, flip))


def flat(v):
    return jnp.concatenate([v[i:i + 1] for i in range(v.shape[0])], axis=1)


PEERS = [(dy, f) for dy in range(NY) for f in (0, 1) if (dy, f) != (0, 0)]


class Paths:
    def __init__(self, tag, net, me, wa):
        self.tag, self.net, self.me = tag, net, me
        self.wa, self.wb = wa, WIDE - wa

    def halves(self, odd):
        cut = 128 if odd else self.wb - 128
        return (0, cut), (cut, self.wb - cut)

    def send(self, key, src, dst, device):
        self.net.send((self.tag,) + key, (self.tag, key[0][0]), src, dst, device)

    def arrive(self, key, ref):
        self.net.arrive((self.tag,) + key, (self.tag, key[0][0]), ref)

    def left(self, ref):
        for part, key, lo, n in (("a", ("a", 2, 0), 0, self.wa), ("b", ("br", 2), self.wa, self.wb)):
            self.net.left((self.tag,) + key, (self.tag, part),
                          ref.at[pl.ds(0, SHARDS - 1), :, pl.ds(lo, n)])

    def longer(self, right, other):
        return right != bool(other)


class Gather(Paths):
    def __init__(self, tag, net, me, wa, g):
        super().__init__(tag, net, me, wa)
        self.g = g

    def part(self, dz, dx, span=None):
        lo, n = span or (0, self.wb)
        return self.g.at[self.me.at(dz, dx), :, pl.ds(self.wa + lo, n)]

    def duo(self, dz, other):
        return self.g.at[self.me.pair_at(dz, other), :, pl.ds(0, self.wa)]

    def pass_on(self, key, ref, device):
        self.send(key, ref, ref, device)

    def a_pass(self, s, other):
        for right, back in ((True, -1), (False, 1)):
            if s < 4 or self.longer(right, other):
                self.pass_on(("a", s, other, right), self.duo(back * (s - 1), other),
                             self.me.dev(-back, 0))

    def a_take(self, s, other):
        for right, back in ((True, -1), (False, 1)):
            if s < 4 or self.longer(right, other):
                self.arrive(("a", s, other, right), self.duo(back * s, other))

    def b_pass(self, s):
        r, l = self.halves(0) if s == 4 else (None, None)
        self.pass_on(("br", s), self.part(1 - s, 0, r), self.me.dev(1, 0))
        self.pass_on(("bl", s), self.part(s - 1, 0, l), self.me.dev(-1, 0))

    def b_take(self, s):
        r, l = self.halves(0) if s == 4 else (None, None)
        self.arrive(("br", s), self.part(-s, 0, r))
        self.arrive(("bl", s), self.part(s, 0, l))

    def b_side(self, o):
        r = self.part(o, 0)
        self.pass_on(("bxr", o), r, self.me.dev(0, 1))
        self.pass_on(("bxl", o), r, self.me.dev(0, -1))

    def b_cross(self, o):
        r, l = self.halves(o % 2)
        self.arrive(("bxr", o), self.part(o, -1))
        self.pass_on(("bd",), self.part(o, -1, r), self.me.dev(0, 1))
        self.arrive(("bxl", o), self.part(o, 1))
        self.pass_on(("bd",), self.part(o, 1, l), self.me.dev(0, -1))

    def start(self):
        own = self.g.at[self.me.c, :, pl.ds(0, self.wa)]
        self.b_pass(1)
        for q in (1, 2, 3):
            self.pass_on(("ax", q), own, self.me.mate_dev(q))
        self.b_side(0)

    def begin_ring(self):
        for q in (1, 2, 3):
            self.arrive(("ax", q), self.g.at[self.me.mate_at(q), :, pl.ds(0, self.wa)])
            if q != 2:
                self.a_pass(1, int(q == 3))

    def step(self, s):
        self.b_take(s)
        if s < 4:
            self.b_pass(s + 1)
            self.b_side(-s)
            self.b_side(s)
        else:
            self.b_side(4)
        for other in (0, 1):
            self.a_take(s, other)
            if s < 4:
                self.a_pass(s + 1, other)
        for o in ((0,) if s == 1 else (1 - s, s - 1)):
            self.b_cross(o)

    def drain(self):
        self.arrive(("bd",), self.g.at[pl.ds(0, NZ), :, pl.ds(self.wa, self.wb)])


class Scatter(Paths):
    ORDER = (4, 3, -3, 2, -2, 1, -1, 0)

    def __init__(self, tag, net, me, wa, v, za, zb, xa, xb, fin, w):
        super().__init__(tag, net, me, wa)
        self.v = v
        self.za, self.zb, self.xa, self.xb, self.fin, self.w = za, zb, xa, xb, fin, w

    def mine(self, dz, dx):
        return self.v[self.me.at(dz, dx), :, pl.ds(self.wa, self.wb)].astype(F32)

    def duo(self, dz, other):
        return self.v.at[self.me.pair_at(dz, other), :, pl.ds(0, self.wa)]

    def b_start(self, i):
        o = self.ORDER[i]
        k = self.me.at(o, 2)
        for d, (lo, n) in enumerate(self.halves(o % 2)):
            self.send(("bx1", i, d), self.v.at[k, :, pl.ds(self.wa + lo, n)],
                      self.xb.at[i, d, :, pl.ds(lo, n)], self.me.dev(0, 1 - 2 * d))

    def join(self, ref, term, came, rest):
        (lo, n), (at, m) = came, rest
        cols = pl.ds(lo, n)
        ref[:, cols] = (ref[:, cols].astype(F32) + term[:, lo:lo + n]).astype(BF16)
        ref[:, pl.ds(at, m)] = term[:, at:at + m].astype(BF16)

    def b_next(self, i):
        o = self.ORDER[i]
        spans = self.halves(o % 2)
        for d in range(2):
            lo, n = spans[d]
            self.arrive(("bx1", i, d), self.xb.at[i, d, :, pl.ds(lo, n)])
            self.join(self.xb.at[i, d], self.mine(o, 1 - 2 * d), spans[d], spans[1 - d])
            self.send(("bx2", i, d), self.xb.at[i, d], self.xb.at[i, 2 + d], self.me.dev(0, 1 - 2 * d))

    def b_sum(self, i):
        for d in range(2):
            self.arrive(("bx2", i, d), self.xb.at[i, 2 + d])
        return (self.mine(self.ORDER[i], 0)
                + self.xb[i, 2].astype(F32) + self.xb[i, 3].astype(F32))

    def a_ring(self, s):
        for other in (1, 0):
            for d, right in ((0, True), (1, False)):
                ahead = (1 - 2 * d) * (5 - s)
                first = 1 if self.longer(right, other) else 2
                if s < first:
                    continue
                term = self.duo(ahead, other)
                src = term
                if s > first:
                    src = self.za.at[other, d, s - 2]
                    self.arrive(("a", s - 1, other, d), src)
                    src[...] = (src[...].astype(F32) + term[...].astype(F32)).astype(BF16)
                self.send(("a", s, other, d), src, self.za.at[other, d, s - 1],
                          self.me.dev(1 - 2 * d, 0))

    def a_sum(self, other):
        for d in range(2):
            self.arrive(("a", 4, other, d), self.za.at[other, d, 3])
        return (self.duo(0, other)[...].astype(F32)
                + self.za[other, 0, 3].astype(F32) + self.za[other, 1, 3].astype(F32))

    def b_ring(self, s, right=None, left=None):
        spans = self.halves(0)
        for d, (name, term) in enumerate((("br", right), ("bl", left))):
            lo, n = spans[d]
            if s == 1:
                src, dst = self.w.at[:, pl.ds(lo, n)], self.zb.at[d, 0, :, pl.ds(lo, n)]
            else:
                src, dst = self.zb.at[d, s - 2], self.zb.at[d, s - 1]
                if s == 2:
                    self.arrive((name, 1), self.zb.at[d, 0, :, pl.ds(lo, n)])
                    self.join(src, term, spans[d], spans[1 - d])
                else:
                    self.arrive((name, s - 1), src)
                    src[...] = (src[...].astype(F32) + term).astype(BF16)
            self.send((name, s), src, dst, self.me.dev(1 - 2 * d, 0))

    def start(self):
        for i in range(4):
            self.b_start(i)
        self.a_ring(1)
        for i in range(4, 8):
            self.b_start(i)

    def turn(self):
        for i in range(3):
            self.b_next(i)
        self.a_ring(2)
        for i in range(3, 8):
            self.b_next(i)

    def second(self):
        self.w[...] = self.b_sum(0).astype(BF16)
        self.b_ring(1)
        self.a_ring(3)
        self.b_ring(2, self.b_sum(1), self.b_sum(2))

    def third(self):
        self.a_ring(4)
        self.b_ring(3, self.b_sum(3), self.b_sum(4))

    def fourth(self):
        me, odd = self.me, self.me.odd
        for other in (1, 0):
            self.fin[other] = self.a_sum(other).astype(BF16)
        for q, other, k in ((3, 1, 1 - odd), (2, 1, odd), (1, 0, 1 - odd)):
            self.send(("ax",), self.fin.at[other, k], self.xa.at[q], me.mate_dev(q))
        self.b_ring(4, self.b_sum(5), self.b_sum(6))

    def last(self):
        self.arrive(("ax",), self.xa.at[pl.ds(1, 3)])
        a = self.fin[0, self.me.odd].astype(F32)
        for q in (1, 3, 2):
            a = a + self.xa[q].astype(F32)
        for d, name in enumerate(("br", "bl")):
            self.arrive((name, 4), self.zb.at[d, 3])
        b = self.b_sum(7) + self.zb[0, 3].astype(F32) + self.zb[1, 3].astype(F32)
        return jnp.concatenate([a, b], axis=1)


class Unit:
    def __init__(self, net, me, y, h, r1, acc, rd, rf):
        self.net, self.me, self.y, self.h = net, me, y, h
        self.r1, self.acc, self.rd, self.rf = r1, acc, rd, rf

    def pair(self, k, dy):
        return self.y[k, self.me.chunk(dy)].astype(F32) + self.r1[k, dy].astype(F32)

    def share(self, k):
        for dy in (2, 1, 3, 0):
            key = ("c", k, dy) if dy else ("end", k)
            self.net.send(key, "u1", self.y.at[k, self.me.chunk(dy, 1)], self.r1.at[k, dy],
                          self.me.peer(0, 1))

    def far(self, k):
        self.net.arrive(("c", k, 2), "u1", self.r1.at[k, 2])
        self.acc[k, 2] = self.pair(k, 2).astype(BF16)
        for i in range(2):
            self.net.send(("d", k, i), "u1", self.acc.at[k, 2, pl.ds(32 * i, 32)],
                          self.rd.at[k, i], self.me.peer(1 - 2 * i))

    def near(self, k):
        for dy, i in ((1, 0), (3, 1)):
            self.net.arrive(("c", k, dy), "u1", self.r1.at[k, dy])
            v = self.pair(k, dy)
            self.net.arrive(("d", k, i), "u1", self.rd.at[k, i])
            lo = 32 * i
            hi = 32 - lo
            self.acc[k, dy, pl.ds(lo, 32)] = (
                v[lo:lo + 32] + self.rd[k, i].astype(F32)
            ).astype(BF16)
            self.acc[k, dy, pl.ds(hi, 32)] = v[hi:hi + 32].astype(BF16)
            self.net.send(("end", k), "u1", self.acc.at[k, dy], self.rf.at[k, i],
                          self.me.peer(1 - 2 * i))

    def settle(self, k):
        self.net.arrive(("end", k), "u1", self.y.at[k, pl.ds(0, 3)])

    def total(self, k, rows):
        return (
            self.y[k, self.me.t, rows].astype(F32)
            + self.r1[k, 0, rows].astype(F32)
            + self.rf[k, 0, rows].astype(F32)
            + self.rf[k, 1, rows].astype(F32)
        )

    def spread(self, k):
        own = self.h.at[k, self.me.t]
        self.net.send(("gr", k), "u2", own, own, self.me.peer(1))
        self.net.send(("gl", k), "u2", own, own, self.me.peer(-1))
        self.net.send(("g", k), "u2", own, own, self.me.peer(0, 1))

    def relay(self, k):
        me = self.me
        for key, dy, lo in (("gr", -1, 0), ("gl", 1, 32)):
            ref = self.h.at[k, me.chunk(dy)]
            self.net.arrive((key, k), "u2", ref)
            half = self.h.at[k, me.chunk(dy), pl.ds(lo, 32)]
            self.net.send(("e", k), "u2", half, half, me.peer(-dy))
            self.net.send(("g", k), "u2", ref, ref, me.peer(0, 1))

    def close(self, k):
        me = self.me
        ref = self.h.at[k, me.chunk(2)]
        self.net.arrive(("e", k), "u2", ref)
        self.net.send(("g", k), "u2", ref, ref, me.peer(0, 1))
        self.net.arrive(("g", k), "u2", self.h.at[k, pl.ds(0, 4)])


def block_kernel(
    routes_ref, counts_ref, tok_ref, cot_ref, gain_ref, router_ref, wg_hbm, wu_hbm, wd_hbm,
    mix_ref, gt_ref, gain_out, router_out, gg_hbm, gu_hbm, gd_hbm,
    wg, wu, wd, gx, gs, pad, spot, sel, sel_t, x_all, x_gain, s_all,
    y, h, r1, acc, rd, rf, st_slots, p_slots, prod, part, vb, vn,
    za_b, zb_b, xa_b, xb_b, fin_b, w_b, za_n, zb_n, xa_n, xb_n, fin_n, w_n,
    cx, cz, sx, sz, go, local_sems, send_sems, recv_sems,
):
    me = Place()
    net = Net(send_sems, recv_sems, me.peer(0, 1))
    barrier = pltpu.get_barrier_semaphore()
    friends = (
        [me.dev(dz, 0) for dz in range(1, NZ)]
        + [me.dev(0, dx) for dx in range(1, NX)]
        + [me.peer(dy, f) for dy, f in PEERS]
    )
    for device in friends:
        pl.semaphore_signal(barrier, inc=1, device_id=device, device_id_type=MESH)
    loads = [
        pltpu.make_async_copy(src, dst, local_sems.at[i])
        for i, (src, dst) in enumerate(((wg_hbm, wg), (wu_hbm, wu), (wd_hbm, wd)))
    ]
    for load in loads:
        load.start()
    hot = one_hot(slot_ids(routes_ref, counts_ref))
    for src, dst in ((tok_ref, gx), (cot_ref, gs)):
        rows = dot(hot, src[...])[:CAP]
        dst[me.c] = jnp.concatenate([rows[:, :WIDE], rows[:, WIDE:]], axis=0).astype(BF16)
    lane8 = lax.broadcasted_iota(jnp.int32, (8, 128), 1)
    cx[0] = jnp.where(lane8 == me.c, counts_ref[0].astype(F32), 0.0)
    pl.semaphore_wait(barrier, len(friends))

    gather_x = Gather("X", net, me, 128, gx)
    gather_s = Gather("S", net, me, 256, gs)
    unit = Unit(net, me, y, h, r1, acc, rd, rf)

    gather_x.start()
    for dx in (1, 2, 3):
        net.send(("cx",), "cx", cx.at[0], cx.at[dx], me.dev(0, dx))
    gather_s.start()
    gather_x.begin_ring()
    net.arrive(("cx",), "cx", cx.at[pl.ds(1, 3)])
    cz[0] = cx[0] + cx[1] + cx[2] + cx[3]
    for dz in range(1, NZ):
        net.send(("cz",), "cz", cz.at[0], cz.at[dz], me.dev(dz, 0))
    gather_s.begin_ring()
    gather_x.step(1)
    gather_s.step(1)
    gather_x.step(2)
    net.arrive(("cz",), "cz", cz.at[pl.ds(1, NZ - 1)])
    held = cz[0]
    for dz in range(1, NZ):
        held = held + cz[dz]

    def place_of(shard, slot, combine):
        ahead = jnp.where(slot >= CAP * shard + CAP, 1.0, 0.0)
        inside = jnp.where(slot >= CAP * shard, 1.0 - ahead, 0.0)
        ahead, inside = ahead.astype(BF16), inside.astype(BF16)
        count, offset, shards = combine(inside, ahead)
        k = (slot[:1] if slot.shape[1] == SLOTS else slot).astype(F32) - CAP * shards
        return jnp.where(k < count, offset + k, -1.0)

    def as_row(inside, ahead):
        c = held.astype(BF16)
        one = jnp.ones((8, 128), BF16)
        return dot(c, inside)[0:1], dot(c, ahead)[0:1], dot(one, ahead)[0:1]

    line = place_of(
        lax.broadcasted_iota(jnp.int32, (128, SLOTS), 0),
        lax.broadcasted_iota(jnp.int32, (128, SLOTS), 1),
        as_row,
    )
    sel[...] = jnp.where(
        line == lax.broadcasted_iota(jnp.int32, (ROWS, SLOTS), 0).astype(F32), 1.0, 0.0
    ).astype(BF16)
    gather_s.step(2)
    gather_x.step(3)
    eye = lax.broadcasted_iota(jnp.int32, (128, 128), 0) == lax.broadcasted_iota(
        jnp.int32, (128, 128), 1
    )

    def as_column(inside, ahead):
        c = jnp.sum(jnp.where(eye, held[0:1], 0.0), axis=1, keepdims=True)
        c = jnp.broadcast_to(c, (128, 128)).astype(BF16)
        one = jnp.ones((128, 128), BF16)
        return dot(inside, c), dot(ahead, c), dot(ahead, one)

    spot[...] = place_of(
        lax.broadcasted_iota(jnp.int32, (SLOTS, 128), 1),
        lax.broadcasted_iota(jnp.int32, (SLOTS, 128), 0),
        as_column,
    )
    sel_t[...] = jnp.where(
        jnp.concatenate([spot[...]] * 4, axis=1)
        == lax.broadcasted_iota(jnp.int32, (SLOTS, ROWS), 1).astype(F32), 1.0, 0.0
    ).astype(BF16)
    gather_s.step(3)
    gather_x.step(4)
    gather_s.step(4)
    gather_x.b_cross(4)
    gather_x.drain()
    gather_s.b_cross(4)

    def flatten(g):
        @pl.loop(0, NZ)
        def _(i):
            v = g[pl.ds(NX * i, NX)].astype(F32)
            rows = pl.ds(pl.multiple_of(i * (NX * CAP), 32), NX * CAP)
            pad[rows, pl.ds(0, WIDE)] = v[:, :CAP].reshape(NX * CAP, WIDE).astype(BF16)
            pad[rows, pl.ds(WIDE, WIDE)] = v[:, CAP:].reshape(NX * CAP, WIDE).astype(BF16)

    flatten(gx)
    for lo, n in COL_TILES:
        cols = pl.ds(lo, n)
        v = dot(sel[...], pad[:, cols])
        x_all[:, cols] = v.astype(BF16)
        x_gain[:, cols] = (v * gain_ref[:, cols]).astype(BF16)
    loads[0].wait()
    for lo, n in FF_TILES:
        v = dot(x_gain[...], wg[:, pl.ds(lo, n)])
        y[0, :, :, pl.ds(lo, n)] = v.astype(BF16).reshape(8, CHUNK, n)
    unit.share(0)
    gather_s.drain()
    loads[1].wait()
    for lo, n in FF_TILES:
        v = dot(x_gain[...], wu[:, pl.ds(lo, n)])
        y[1, :, :, pl.ds(lo, n)] = v.astype(BF16).reshape(8, CHUNK, n)
    unit.share(1)
    unit.far(0)
    flatten(gs)
    for lo, n in COL_TILES:
        cols = pl.ds(lo, n)
        s_all[:, cols] = dot(sel[...], pad[:, cols]).astype(BF16)
    loads[2].wait()
    unit.far(1)
    for lo, n in FF_TILES:
        v = contract_cols(s_all[...], wd[pl.ds(lo, n), :])
        y[2, :, :, pl.ds(lo, n)] = v.astype(BF16).reshape(8, CHUNK, n)
    unit.share(2)
    unit.near(0)

    router = flat(router_ref[...].astype(F32))
    sq = jnp.zeros((ROWS, 128), F32)
    lg = jnp.zeros((ROWS, 128), F32)
    for lo in range(0, COLS, 128):
        v = x_all[:, pl.ds(lo, 128)].astype(F32)
        sq = sq + v * v
        lg = lg + v * router[:, lo:lo + 128]
    sq = jnp.sum(sq, axis=1, keepdims=True)
    lg = jnp.sum(lg, axis=1, keepdims=True)
    for i in range(8):
        v = (sq, lg)[i // 4][128 * (i % 4):128 * (i % 4) + 128]
        st_slots[me.t, pl.ds(i, 1)] = jnp.sum(jnp.where(eye, v, 0.0), axis=0, keepdims=True)
    for dy, f in PEERS:
        ref = st_slots.at[me.t]
        net.send(("st",), "st", ref, ref, me.peer(dy, f))
    unit.near(1)
    unit.far(2)

    net.arrive(("st",), "st", st_slots.at[pl.ds(0, 7)])
    stat = st_slots[0]
    for k in range(1, 8):
        stat = stat + st_slots[k]
    sub = lax.broadcasted_iota(jnp.int32, (8, 128), 0)
    lane = lax.broadcasted_iota(jnp.int32, (CHUNK, 128), 1)
    row = lax.broadcasted_iota(jnp.int32, (CHUNK, 128), 0)
    at_own = lane == row + me.core * CHUNK

    def column(which):
        line = jnp.sum(jnp.where(sub == which, stat, 0.0), axis=0, keepdims=True)
        return jnp.sum(jnp.where(at_own, line, 0.0), axis=1, keepdims=True)

    inv_rms = lax.rsqrt(column(me.y) / D + EPS)
    weight = jax.nn.sigmoid(column(4 + me.y))
    unit.settle(0)
    unit.settle(1)
    for i in range(4):
        rows = pl.ds(16 * i, 16)
        inv = inv_rms[16 * i:16 * i + 16]
        gate, upward = unit.total(0, rows) * inv, unit.total(1, rows) * inv
        h[0, me.t, rows] = (
            gate * jax.nn.sigmoid(gate) * upward * weight[16 * i:16 * i + 16]
        ).astype(BF16)
    unit.spread(0)
    unit.near(2)
    unit.relay(0)
    unit.settle(2)
    firsts, seconds = [], []
    for i in range(4):
        rows = pl.ds(16 * i, 16)
        inv = inv_rms[16 * i:16 * i + 16]
        w = weight[16 * i:16 * i + 16]
        g_raw, u_raw, d_raw = unit.total(0, rows), unit.total(1, rows), unit.total(2, rows)
        gate, upward = g_raw * inv, u_raw * inv
        sigma = jax.nn.sigmoid(gate)
        d_hidden = d_raw * (w * inv)
        d_gate = (d_hidden * upward * sigma * (1.0 + gate * (1.0 - sigma))).astype(BF16)
        d_up = (d_hidden * (gate * sigma)).astype(BF16)
        h[1, me.t, rows] = d_gate
        h[2, me.t, rows] = d_up
        firsts.append(jnp.sum(d_raw * h[0, me.t, rows].astype(F32), axis=1, keepdims=True))
        seconds.append(
            jnp.sum(d_gate.astype(F32) * g_raw + d_up.astype(F32) * u_raw, axis=1, keepdims=True)
        )
    unit.spread(1)
    unit.spread(2)

    def line_of(parts):
        return jnp.sum(jnp.where(at_own, jnp.concatenate(parts, axis=0), 0.0), axis=0, keepdims=True)

    p_slots[me.t] = jnp.where(sub == me.y, line_of(firsts), 0.0) + jnp.where(
        sub == 4 + me.y, line_of(seconds), 0.0
    )
    for dy, f in PEERS:
        ref = p_slots.at[me.t]
        net.send(("p",), "p", ref, ref, me.peer(dy, f))

    scatter_b = Scatter("B", net, me, 256, vb, za_b, zb_b, xa_b, xb_b, fin_b, w_b)
    scatter_n = Scatter("N", net, me, 128, vn, za_n, zb_n, xa_n, xb_n, fin_n, w_n)

    def all_rows(k):
        return h[k].reshape(ROWS, FFL)

    def expand(v):
        for g in range(2):
            s = sel_t[pl.ds(384 * g, 384), :]
            parts = [
                dot(s, prod[:, pl.ds(WIDE * i, WIDE)]).reshape(16, CAP, WIDE) for i in range(2)
            ]
            v[pl.ds(16 * g, 16)] = jnp.concatenate(parts, axis=1).astype(BF16)

    unit.close(0)
    for lo, n in COL_TILES:
        cols = pl.ds(lo, n)
        prod[:, cols] = dot(all_rows(0), wd[:, cols]).astype(BF16)
    expand(vb)
    scatter_b.start()
    unit.relay(1)
    unit.relay(2)
    scatter_b.turn()
    stores = []

    def write(i, src, out):
        store = pltpu.make_async_copy(src, out, local_sems.at[3 + i])
        store.start()
        stores.append(store)

    unit.close(1)
    scatter_b.second()
    for lo, n in COL_TILES:
        cols = pl.ds(lo, n)
        part[:, cols] = contract_cols(all_rows(1), wg[cols, :])
    unit.close(2)
    for i, (lo, n) in enumerate(COL_TILES):
        cols = pl.ds(lo, n)
        v = part[:, cols] + contract_cols(all_rows(2), wu[cols, :])
        prod[:, cols] = v.astype(BF16)
        line = jnp.sum(v * x_all[:, cols].astype(F32), axis=0, keepdims=True)
        sx[0, pl.ds(8 + 2 * i, 1)] = line[:, :128]
        sx[0, pl.ds(9 + 2 * i, 1)] = line[:, 128:]
    net.arrive(("p",), "p", p_slots.at[pl.ds(0, 7)])
    p = p_slots[0]
    for k in range(1, 8):
        p = p + p_slots[k]
    sx[0, pl.ds(0, 8)] = p
    for dx in (1, 2, 3):
        net.send(("sx",), "sx", sx.at[0], sx.at[dx], me.dev(0, dx))
    expand(vn)
    scatter_n.start()
    scatter_b.third()
    for lo in range(0, FFL, 128):
        left = h[0, :, :, pl.ds(lo, 128)].reshape(ROWS, 128)
        go[0, pl.ds(lo, 128), :] = contract_rows(left, s_all[...]).astype(BF16)
    write(0, go.at[0, pl.ds(0, FFL)], gd_hbm)
    net.arrive(("sx",), "sx", sx.at[pl.ds(1, 3)])
    sz[0] = sx[0] + sx[1] + sx[2] + sx[3]
    for dz in range(1, NZ):
        net.send(("sz",), "sz", sz.at[0], sz.at[dz], me.dev(dz, 0))
    scatter_n.turn()
    scatter_b.fourth()
    for lo in range(0, COLS, 256):
        left = x_gain[:, pl.ds(lo, 256)]
        go[1, pl.ds(lo, 256), pl.ds(0, FFL)] = contract_rows(left, all_rows(1)).astype(BF16)
    write(1, go.at[1, :, pl.ds(0, FFL)], gg_hbm)
    scatter_n.second()
    for lo in range(0, COLS, 256):
        left = x_gain[:, pl.ds(lo, 256)]
        go[2, pl.ds(lo, 256), pl.ds(0, FFL)] = contract_rows(left, all_rows(2)).astype(BF16)
    write(2, go.at[2, :, pl.ds(0, FFL)], gu_hbm)
    scatter_n.third()
    branch = scatter_b.last()
    scatter_n.fourth()

    net.arrive(("sz",), "sz", sz.at[pl.ds(1, NZ - 1)])
    tot = sz[0]
    for dz in range(1, NZ):
        tot = tot + sz[dz]
    d_logit = tot[0:4] * (1.0 - jax.nn.sigmoid(stat[4:8]))
    mean_term = tot[4:8] / D / (stat[0:4] / D + EPS)

    d_logit, mean_term = flat(d_logit), flat(mean_term)
    first = d_logit.astype(BF16)
    rest = d_logit - first.astype(F32)
    second = rest.astype(BF16)
    third = (rest - second.astype(F32)).astype(BF16)
    for lo, n in COL_TILES:
        cols = pl.ds(lo, n)
        x = x_all[:, cols]
        line = dot(first, x) + dot(second, x) + dot(third, x)
        for k in range(0, n, 128):
            router_out[pl.ds((lo + k) // 128, 1)] = line[:, k:k + 128]
    gain_out[...] = tot[8:16]
    own = spot[pl.ds(pl.multiple_of(me.c * CAP, 8), CAP), :]
    own = jnp.concatenate([own] * 4, axis=1)
    hit = own == lax.broadcasted_iota(jnp.int32, (CAP, ROWS), 1).astype(F32)
    d_logit = jnp.sum(jnp.where(hit, d_logit, 0.0), axis=1, keepdims=True)
    mean_term = jnp.sum(jnp.where(hit, mean_term, 0.0), axis=1, keepdims=True)

    d_normed = scatter_n.last()
    picked, slope = gx[me.c].astype(F32), gs[me.c].astype(F32)
    mix_ref[...] = picked + branch
    for i in range(2):
        r = slice(CAP * i, CAP * i + CAP)
        feats = slice(WIDE * i, WIDE * i + WIDE)
        gt_ref[pl.ds(CAP * i, CAP), :] = slope[r] + (
            d_normed[r] * gain_ref[:, pl.ds(WIDE * i, WIDE)] - picked[r] * mean_term
            + d_logit * router[:, feats]
        )
    for store in stores:
        store.wait()
    for paths, ref in ((gather_x, gx), (gather_s, gs), (scatter_b, vb), (scatter_n, vn)):
        paths.left(ref)
    net.left(("end", 0), "u1", y.at[:, pl.ds(0, 7)])
    net.left(("g", 0), "u2", h.at[:, pl.ds(0, 7)])
    for name, ref, n in (
        ("cx", cx, 3), ("cz", cz, 7), ("sx", sx, 3), ("sz", sz, 7), ("st", st_slots, 7), ("p", p_slots, 7)
    ):
        net.left((name,), name, ref.at[pl.ds(0, n)])


def block(routes, counts, tokens, cotangent, gain, router, w_gate, w_up, w_down):
    vm = pl.BlockSpec(memory_space=VMEM)
    sm = pl.BlockSpec(memory_space=pltpu.SMEM)
    hbm = pl.BlockSpec(memory_space=pl.ANY)
    ring_b, ring_n = (
        [
            VMEM((2, 2, 4, 2, TALL, wa), BF16),
            VMEM((2, 4, TALL, WIDE - wa), BF16),
            VMEM((4, TALL, wa), BF16),
            VMEM((8, 4, TALL, WIDE - wa), BF16),
            VMEM((2, 2, TALL, wa), BF16),
            VMEM((TALL, WIDE - wa), BF16),
        ]
        for wa in (256, 128)
    )
    return pl.pallas_call(
        block_kernel,
        out_shape=(
            jax.ShapeDtypeStruct((TALL, WIDE), F32),
            jax.ShapeDtypeStruct((TALL, WIDE), F32),
            jax.ShapeDtypeStruct((8, 128), F32),
            jax.ShapeDtypeStruct((8, 128), F32),
            jax.ShapeDtypeStruct((COLS, FFL), BF16),
            jax.ShapeDtypeStruct((COLS, FFL), BF16),
            jax.ShapeDtypeStruct((FFL, COLS), BF16),
        ),
        in_specs=[sm] * 2 + [vm] * 4 + [hbm] * 3,
        out_specs=(vm,) * 4 + (hbm,) * 3,
        scratch_shapes=[
            VMEM((COLS, FFL), BF16),
            VMEM((COLS, FFL), BF16),
            VMEM((FFL, COLS), BF16),
            VMEM((SHARDS, TALL, WIDE), BF16),
            VMEM((SHARDS, TALL, WIDE), BF16),
            VMEM((SLOTS, COLS), BF16),
            VMEM((SLOTS, 128), F32),
            VMEM((ROWS, SLOTS), BF16),
            VMEM((SLOTS, ROWS), BF16),
            VMEM((ROWS, COLS), BF16),
            VMEM((ROWS, COLS), BF16),
            VMEM((ROWS, COLS), BF16),
            VMEM((3, 8, CHUNK, FFL), BF16),
            VMEM((3, 8, CHUNK, FFL), BF16),
            VMEM((3, 4, CHUNK, FFL), BF16),
            VMEM((3, 4, CHUNK, FFL), BF16),
            VMEM((3, 2, CHUNK // 2, FFL), BF16),
            VMEM((3, 2, CHUNK, FFL), BF16),
            VMEM((8, 8, 128), F32),
            VMEM((8, 8, 128), F32),
            VMEM((ROWS, COLS), BF16),
            VMEM((ROWS, COLS), F32),
            VMEM((SHARDS, TALL, WIDE), BF16),
            VMEM((SHARDS, TALL, WIDE), BF16),
            *ring_b,
            *ring_n,
            VMEM((4, 8, 128), F32),
            VMEM((8, 8, 128), F32),
            VMEM((4, 16, 128), F32),
            VMEM((8, 16, 128), F32),
            VMEM((3, COLS, COLS), BF16),
            pltpu.SemaphoreType.DMA((6,)),
            pltpu.SemaphoreType.DMA((SEND_SEMS,)),
            pltpu.SemaphoreType.DMA((RECV_SEMS,)),
        ],
        compiler_params=pltpu.CompilerParams(
            collective_id=0, has_side_effects=True, vmem_limit_bytes=56 << 20
        ),
        name="block",
    )(routes, counts, tokens, cotangent, gain, router, w_gate, w_up, w_down)


def merge_kernel(
    routes_ref, counts_ref, tok_hbm, cot_hbm, mix_hbm, gt_hbm, gain_hbm, router_hbm, a_hbm, b_hbm, c_hbm,
    mixed_out, grad_out, gain_out, router_out, a_out, b_out, c_out,
    tok, cot, mix, gt, gain, router, a, b, c, mixed, grad, in_sems, out_sems,
):
    pieces = [
        (mix_hbm, mix, None), (gt_hbm, gt, None), (tok_hbm, tok, None), (cot_hbm, cot, None),
        (gain_hbm, gain, gain_out), (router_hbm, router, router_out),
    ]
    for src, held, dst in ((a_hbm, a, a_out), (b_hbm, b, b_out), (c_hbm, c, c_out)):
        rows = src.shape[0] // 2
        for j in range(2):
            part = pl.ds(rows * j, rows)
            pieces.append((src.at[part], held.at[part], dst.at[part]))
    come = [
        pltpu.make_async_copy(src, held, in_sems.at[k]) for k, (src, held, _) in enumerate(pieces)
    ]
    for copy in come:
        copy.start()
    gone = []

    def leave(held, dst):
        copy = pltpu.make_async_copy(held, dst, out_sems.at[len(gone)])
        copy.start()
        gone.append(copy)

    hot = one_hot(slot_ids(routes_ref, counts_ref))
    picked = contract_rows(hot, jnp.ones((32, 128), BF16))[:, 0:1] > 0.5
    blank = jnp.zeros((32 - CAP, COLS), F32)
    for copy in come[:4]:
        copy.wait()
    for old, new, held, dst in ((tok, mix, mixed, mixed_out), (cot, gt, grad, grad_out)):
        rows = jnp.concatenate([new[pl.ds(0, CAP), :], new[pl.ds(CAP, CAP), :]], axis=1)
        rows = jnp.concatenate([rows, blank], axis=0).astype(BF16)
        held[...] = jnp.where(picked, contract_rows(hot, rows), old[...].astype(F32)).astype(BF16)
        leave(held, dst)
    for copy, (_, held, dst) in zip(come[4:], pieces[4:]):
        copy.wait()
        leave(held, dst)
    for copy in gone:
        copy.wait()


def merge(routes, counts, tokens, cotangent, *new):
    sm = pl.BlockSpec(memory_space=pltpu.SMEM)
    hbm = pl.BlockSpec(memory_space=pl.ANY)
    out = (tokens, cotangent) + new[2:]
    return pl.pallas_call(
        merge_kernel,
        out_shape=[jax.ShapeDtypeStruct(v.shape, v.dtype) for v in out],
        in_specs=[sm] * 2 + [hbm] * 9,
        out_specs=[hbm] * 7,
        scratch_shapes=[VMEM(v.shape, v.dtype) for v in (tokens, cotangent) + new]
        + [VMEM(v.shape, v.dtype) for v in (tokens, cotangent)]
        + [pltpu.SemaphoreType.DMA((12,)), pltpu.SemaphoreType.DMA((10,))],
        compiler_params=pltpu.CompilerParams(vmem_limit_bytes=60 << 20),
        name="merge",
    )(routes, counts, tokens, cotangent, *new)


def body(tokens, norm_gain, router, w_gate, w_up, w_down, routes, counts, cotangent):
    new = block(
        routes, counts, tokens, cotangent, norm_gain[None, :], router.reshape(8, 128),
        w_gate, w_up, w_down,
    )
    mixed, grad_tokens, gain, router, *grads = merge(routes, counts, tokens, cotangent, *new)
    return (mixed, grad_tokens, *grads, gain.reshape(COLS), router.reshape(COLS))


def solution(mesh):
    return jax.shard_map(
        body,
        mesh=mesh,
        in_specs=(
            P("context", "tensor"),
            P("tensor"),
            P("tensor"),
            P("tensor", "context"),
            P("tensor", "context"),
            P("context", "tensor"),
            P("context", None),
            P("context"),
            P("context", "tensor"),
        ),
        out_specs=(
            P("context", "tensor"),
            P("context", "tensor"),
            P("tensor", "context"),
            P("tensor", "context"),
            P("context", "tensor"),
            P("tensor"),
            P("tensor"),
        ),
        check_vma=False,
    )
```
